32 devices in a mesh: tile: 8 (over z, x), height: 4 (over y, core).
Axes of the slice: x: 2, y: 2, z: 4, core: 2. Of those that a mesh axis runs over, the one named last changes fastest.
Arguments:
- material: int32 [32, 256, 128], P('height', 'tile'), may hold values from 0 to 2
- clamped: int32 [32, 256, 128], P('height', 'tile'), may hold values from 0 to 1, as said below
- stiffness_table: float32 [3], replicated, may hold values from 0.5 to 4
- eigenstrain: float32 [3, 3], replicated, may hold values from -6 to 6
Outputs:
- displacement: float32 [3, 32, 256, 128], P(None, 'height', 'tile')
The draws below stay inside these ranges and needn't reach their ends.
Inputs may be any that keep to these rules, and one draw needn't show every extreme that they name: `clamped`: only voxels of the lowest 2 layers can be 1; in those layers 0 and 1 are equally likely.
All inputs are finite; a program needn't handle non-finite values.
Results may differ from the reference program's by a relative error of at most 0.00016.
Values sent between devices are 32-bit elements; how exact they have to be, the bound alone decides.
No kernel may reach another device: no remote copies, remote signals or barrier semaphores. Data moves between devices by JAX's collectives and lax.ppermute only.
A program may use at most 128 MiB of HBM per device.

```python
import math
import jax
import jax.numpy as jnp
from jax import lax

CY = 128
NLABEL = 3
LEVELS = 3
PRE = 2
POST = 1
COARSE_SWEEPS = 6
CLAMP_LAYERS = 2
NZ = 32
BX = 256


def draw_clamped(key, part):
    joined = jax.random.randint(key, (NZ, BX, CY), 0, 2, dtype=jnp.int32)
    layer_idx = lax.broadcasted_iota(jnp.int32, (NZ, BX, CY), 0)
    return jnp.where(layer_idx < CLAMP_LAYERS, joined, jnp.zeros_like(joined))


def plant(entries, stream_key, smallest, largest):
    extent = entries.shape
    index_at = [jax.random.randint(jax.random.fold_in(stream_key, axis), (), 0, extent[axis]) for axis in range(len(extent))]
    entries = entries.at[tuple(index_at)].set(smallest)
    longest = extent.index(max(extent))
    index_at[longest] = (index_at[longest] + 1) % extent[longest]
    return entries.at[tuple(index_at)].set(largest)


def gaussian(rng, shape, spread, bound, held_as=jnp.bfloat16):
    return jnp.clip(spread * jax.random.normal(rng, shape, jnp.float32), -bound, bound).astype(held_as)


def setup_inputs(seed: int = 0) -> dict:
    seeds = jax.random.split(jax.random.key(seed), 5)
    material = plant(jax.random.randint(seeds[0], (NZ, BX, CY), 0, 3), jax.random.fold_in(seeds[0], 1), 0, 2).astype(jnp.int32)
    clamped = draw_clamped(jax.random.fold_in(seeds[4], 71), 0)
    stiffness_table = jnp.clip(jnp.exp(jax.random.uniform(seeds[2], (NLABEL,), jnp.float32, math.log(0.5), math.log(4.0))), 0.5, 4.0)
    eigenstrain = gaussian(seeds[3], (NLABEL, 3), 2.0, 6.0, jnp.float32)
    return {"material": material, "clamped": clamped, "stiffness_table": stiffness_table, "eigenstrain": eigenstrain}


GAMMA = 1.0
PENALTY = 50.0
OMEGA = 0.6


def lookup(labels, table):
    result = jnp.zeros(labels.shape, table.dtype)
    for label_id in range(NLABEL):
        result = result + (labels == label_id).astype(table.dtype) * table[label_id]
    return result


def block_sum(field):
    dims_now = field.shape
    shaped = field.reshape(dims_now[0], dims_now[1] // 2, 2, dims_now[2] // 2, 2, dims_now[3] // 2, 2)
    return shaped.sum(axis=(2, 4, 6))


def prolong(field):
    return jnp.repeat(jnp.repeat(jnp.repeat(field, 2, axis=1), 2, axis=2), 2, axis=3)


def direction_factor(direction, dtype):
    return jnp.where(jnp.arange(3) == direction, 1.0 + GAMMA, 1.0).astype(dtype).reshape(3, 1, 1, 1)


def lower_of(field, axis_dim):
    widths = [(0, 0)] * 4
    widths[axis_dim] = (1, 0)
    return lax.slice_in_dim(jnp.pad(field, widths), 0, field.shape[axis_dim], axis=axis_dim)


def upper_of(field, axis_dim):
    widths = [(0, 0)] * 4
    widths[axis_dim] = (0, 1)
    return lax.slice_in_dim(jnp.pad(field, widths), 1, field.shape[axis_dim] + 1, axis=axis_dim)


def grid_pairs(field):
    return [(lower_of(field, direction + 1), upper_of(field, direction + 1)) for direction in range(3)]


def coefficients(stiffness, spring, pairs):
    k_lower, k_upper = [], []
    diagonal = jnp.broadcast_to(spring, (3,) + spring.shape[1:])
    for direction in range(3):
        lower_nb, upper_nb = pairs[direction]
        low_face = 0.5 * (stiffness + lower_nb)
        high_face = 0.5 * (stiffness + upper_nb)
        diagonal = diagonal + direction_factor(direction, stiffness.dtype) * (low_face + high_face)
        k_lower.append(low_face)
        k_upper.append(high_face)
    return k_lower, k_upper, diagonal


def apply_operator(motion, spring, k_lower, k_upper, pairs):
    result = spring * motion
    for direction in range(3):
        lower_nb, upper_nb = pairs[direction]
        term = k_lower[direction] * (motion - lower_nb) + k_upper[direction] * (motion - upper_nb)
        result = result + direction_factor(direction, motion.dtype) * term
    return result


def smooth_from_zero(source, spring, terms, sweeps, pairs_fn):
    k_lower, k_upper, diagonal = terms
    motion = OMEGA * source / diagonal
    for turn_idx in range(sweeps - 1):
        motion = motion + OMEGA * (source - apply_operator(motion, spring, k_lower, k_upper, pairs_fn(motion))) / diagonal
    return motion


def reference(material, clamped, stiffness_table, eigenstrain):
    labels = material[None]
    stiffness = lookup(labels, stiffness_table)
    spring = PENALTY * clamped[None].astype(jnp.float32)
    pieces = []
    for component in range(3):
        stress = stiffness * lookup(labels, eigenstrain[:, component])
        pieces.append(0.5 * (lower_of(stress, component + 1) - upper_of(stress, component + 1)))
    source = jnp.concatenate(pieces, 0)
    saved = []
    for grid_level in range(LEVELS):
        terms = coefficients(stiffness, spring, grid_pairs(stiffness))
        motion = smooth_from_zero(source, spring, terms, PRE, grid_pairs)
        remain = source - apply_operator(motion, spring, terms[0], terms[1], grid_pairs(motion))
        saved.append((motion, source, spring, terms))
        source = block_sum(remain)
        stiffness = 0.5 * block_sum(stiffness)
        spring = block_sum(spring)
    terms = coefficients(stiffness, spring, grid_pairs(stiffness))
    motion = smooth_from_zero(source, spring, terms, COARSE_SWEEPS, grid_pairs)
    for grid_level in reversed(range(LEVELS)):
        level_motion, level_source, level_spring, terms = saved[grid_level]
        k_lower, k_upper, diagonal = terms
        motion = level_motion + prolong(motion)
        for turn_idx in range(POST):
            motion = motion + OMEGA * (level_source - apply_operator(motion, level_spring, k_lower, k_upper, grid_pairs(motion))) / diagonal
    return motion
```

```python
import functools

import jax
import jax.numpy as jnp
from jax import lax
from jax.experimental import pallas as pl
from jax.experimental.pallas import tpu as pltpu
from jax.sharding import PartitionSpec as P

PENALTY = 50.0
OMEGA = 0.6
COARSE_SWEEPS = 6
LANES = 128
HALO = 9
REACH = 16
F32 = jnp.float32


def chunks(start, stop, size):
    return [(row, min(size, stop - row)) for row in range(start, stop, size)]


def lane_of(rows):
    return lax.broadcasted_iota(jnp.int32, (rows, LANES), 1)


def roll(x, shift):
    return pltpu.roll(x, shift % LANES, 1)


def rows_at(ref, layer, row, count):
    return ref[layer, pl.ds(row, count), :]


def cross_faces(s_ref, layer, row, count):
    here = rows_at(s_ref, layer, row, count)
    return here, [
        here + rows_at(s_ref, layer - 1, row, count),
        here + rows_at(s_ref, layer + 1, row, count),
        here + rows_at(s_ref, layer, row - 1, count),
        here + rows_at(s_ref, layer, row + 1, count),
    ]


def lane_faces(here, step):
    lane = lane_of(here.shape[0])
    first, last = lane < step, lane >= LANES - step
    low = here + jnp.where(first, 0.0, roll(here, step))
    high = here + jnp.where(last, 0.0, roll(here, -step))
    return low, high, jnp.where(first, 0.0, low), jnp.where(last, 0.0, high)


def neighbours(v_ref, faces, layer, row, count, step):
    here = rows_at(v_ref, layer, row, count)
    along = [
        faces[0] * rows_at(v_ref, layer - 1, row, count)
        + faces[1] * rows_at(v_ref, layer + 1, row, count),
        faces[2] * rows_at(v_ref, layer, row - 1, count)
        + faces[3] * rows_at(v_ref, layer, row + 1, count),
        faces[4] * roll(here, step) + faces[5] * roll(here, -step),
    ]
    return here, along


def total(along, component):
    return (along[0] + along[1] + along[2]) + along[component]


def safe_rate(here, doubled):
    return jnp.where(here > 0.0, OMEGA / doubled, 0.0)


def pair_lanes(x, step):
    upper = (lane_of(x.shape[0]) & step) != 0
    return x + jnp.where(upper, roll(x, step), roll(x, -step))


def pair_rows(ref, row, count):
    return ref[pl.ds(row, count, stride=2), :] + ref[pl.ds(row + 1, count, stride=2), :]


def spread_rows(ref, x):
    count = x.shape[0]
    ref[pl.ds(0, count, stride=2), :] = x
    ref[pl.ds(1, count, stride=2), :] = x


def level_setup(s_ref, p_ref, r_ref, d_ref, g_ref, y_ref, b_of, layer, row, count, step):
    here, cross = cross_faces(s_ref, layer, row, count)
    low, high, low_in, high_in = lane_faces(here, step)
    y_ref[0, layer, pl.ds(row, count), :] = low_in
    y_ref[1, layer, pl.ds(row, count), :] = high_in
    sums = [cross[0] + cross[1], cross[2] + cross[3], low + high]
    base = rows_at(p_ref, layer, row, count) + (sums[0] + sums[1] + sums[2])
    for c in range(3):
        doubled = base + sums[c]
        rate = safe_rate(here, doubled)
        d_ref[c, layer, pl.ds(row, count), :] = doubled
        r_ref[c, layer, pl.ds(row, count), :] = rate
        g_ref[c, layer, pl.ds(row, count), :] = (2.0 * rate) * b_of(c)


def all_faces(s_ref, y_ref, layer, row, count):
    _, cross = cross_faces(s_ref, layer, row, count)
    return cross + [
        y_ref[0, layer, pl.ds(row, count), :],
        y_ref[1, layer, pl.ds(row, count), :],
    ]


def first_sweep(s_ref, y_ref, r_ref, g_ref, v_ref, layer, row, count, step):
    faces = all_faces(s_ref, y_ref, layer, row, count)
    for c in range(3):
        here, along = neighbours(g_ref.at[c], faces, layer, row, count, step)
        rate = r_ref[c, layer, pl.ds(row, count), :]
        v_ref[c, layer, pl.ds(row, count), :] = (2.0 - OMEGA) * here + rate * total(along, c)


def remainder(s_ref, y_ref, b_ref, d_ref, v_ref, layer, row, count, step):
    faces = all_faces(s_ref, y_ref, layer, row, count)
    result = []
    for c in range(3):
        here, along = neighbours(v_ref.at[c], faces, layer, row, count, step)
        doubled = d_ref[c, layer, pl.ds(row, count), :]
        source = b_ref[c, layer, pl.ds(row, count), :]
        result.append(source + 0.5 * (total(along, c) - doubled * here))
    return result


def down_kernel(
    heights, tiles, bz, bx,
    x_ref, table_ref, strain_ref,
    send_ref, s0_out, y0_out, v0_out, g0_out, r0_out, s1_out, y1_out, v1_out, g1_out, r1_out,
    s, p, st, b, r, d, g, y, v, tmp, s1, p1, b1, r1, d1, g1, y1, v1, sem,
):
    h, t = lax.axis_index("height"), lax.axis_index("tile")
    nz, n1 = bz + 2 * HALO, bz // 2 + 8
    bx1, bx2 = bx // 2, bx // 4
    low, high = 8, bx + 24
    own_rows, halo_rows = (bz + 2) * bx, (bz + 2) * HALO
    before = jnp.where(t > 0, 1.0, 0.0)
    behind = jnp.where(t < tiles - 1, 1.0, 0.0)

    def read_layer(layer, carry):
        z = bz * h - HALO + layer
        inside = jnp.where((z >= 0) & (z < heights * bz), 1.0, 0.0)
        bottom = jnp.where((z >= 0) & (z < 2), 2.0 * PENALTY, 0.0)
        z_in = jnp.clip(z, 0, heights * bz - 1)
        brick, slot = z_in // bz, z_in % bz
        clamp_slot = bz + jnp.clip(z, 0, 1)
        parts = [
            (slot * bx, clamp_slot * bx, bx, 16, 1.0),
            (own_rows + slot * HALO, own_rows + clamp_slot * HALO, HALO, 16 - HALO, before),
            (own_rows + halo_rows + slot * HALO, own_rows + halo_rows + clamp_slot * HALO, HALO, 16 + bx, behind),
        ]
        for at, clamp_at, count, to, valid in parts:
            label = x_ref[brick, pl.ds(at, count), :]
            is0, is1 = label == 0, label == 1
            weight = inside * valid
            stiff = [table_ref[k] * weight for k in range(3)]
            dst = pl.ds(to, count)
            s[layer, dst, :] = jnp.where(is0, stiff[0], jnp.where(is1, stiff[1], stiff[2]))
            for c in range(3):
                e = [stiff[k] * strain_ref[k, c] for k in range(3)]
                st[c, layer, dst, :] = jnp.where(is0, e[0], jnp.where(is1, e[1], e[2]))
            joined = x_ref[0, pl.ds(clamp_at, count), :].astype(F32)
            p[layer, dst, :] = joined * (bottom * valid)
        return carry

    lax.fori_loop(0, nz, read_layer, 0)

    def setup0(layer, carry):
        for row, count in chunks(low, high, 16):
            lane = lane_of(count)
            here = st[2, layer, pl.ds(row, count), :]
            source = [
                0.5 * (rows_at(st.at[0], layer - 1, row, count) - rows_at(st.at[0], layer + 1, row, count)),
                0.5 * (rows_at(st.at[1], layer, row - 1, count) - rows_at(st.at[1], layer, row + 1, count)),
                0.5 * (jnp.where(lane < 1, 0.0, roll(here, 1)) - jnp.where(lane >= LANES - 1, 0.0, roll(here, -1))),
            ]
            for c in range(3):
                b[c, layer, pl.ds(row, count), :] = source[c]
            level_setup(s, p, r, d, g, y, lambda c: source[c], layer, row, count, 1)
        return carry

    lax.fori_loop(1, nz - 1, setup0, 0)

    def sweep0(layer, carry):
        for row, count in chunks(low, high, 16):
            first_sweep(s, y, r, g, v, layer, row, count, 1)
        return carry

    lax.fori_loop(2, nz - 2, sweep0, 0)

    own = (pl.ds(HALO, bz), pl.ds(16, bx))
    near = (pl.ds(HALO - 1, bz + 2), pl.ds(low, bx + 16))
    copies = [
        (s.at[near[0], near[1]], s0_out),
        (y.at[:, own[0], own[1]], y0_out),
        (v.at[:, near[0], near[1]], v0_out),
        (g.at[:, own[0], own[1]], g0_out),
        (r.at[:, own[0], own[1]], r0_out),
    ]
    started = []
    for k, (src, dst) in enumerate(copies):
        started.append(pltpu.make_async_copy(src, dst, sem.at[k]))
        started[-1].start()

    rows1 = bx1 + 8

    def restrict0(j, carry):
        layer = 3 + 2 * j
        for row, count in chunks(low, high, 16):
            one = remainder(s, y, b, d, v, layer, row, count, 1)
            two = remainder(s, y, b, d, v, layer + 1, row, count, 1)
            for c in range(3):
                tmp[c, pl.ds(row, count), :] = one[c] + two[c]
        for c in range(3):
            b1[c, j + 1, pl.ds(8, rows1), :] = pair_lanes(pair_rows(tmp.at[c], low, rows1), 1)
        return carry

    lax.fori_loop(0, n1 - 2, restrict0, 0)

    def coarse0(k, carry):
        for field, scale, into in ((s, 0.5, s1), (p, 1.0, p1)):
            both = [pair_rows(field.at[1 + 2 * k + i], low, rows1) for i in range(2)]
            into[k, pl.ds(8, rows1), :] = scale * pair_lanes(both[0] + both[1], 1)
        return carry

    lax.fori_loop(0, n1, coarse0, 0)

    def setup1(layer, carry):
        level_setup(
            s1, p1, r1, d1, g1, y1,
            lambda c: b1[c, layer, pl.ds(8, rows1), :], layer, 8, rows1, 2,
        )
        return carry

    lax.fori_loop(1, n1 - 1, setup1, 0)

    def sweep1(layer, carry):
        first_sweep(s1, y1, r1, g1, v1, layer, 8, rows1, 2)
        return carry

    lax.fori_loop(2, n1 - 2, sweep1, 0)

    copies = [
        (s1.at[pl.ds(2, n1 - 4), pl.ds(8, rows1)], s1_out),
        (y1.at[:, pl.ds(3, n1 - 6), pl.ds(8, rows1)], y1_out),
        (v1.at[:, pl.ds(2, n1 - 4), pl.ds(8, rows1)], v1_out),
        (g1.at[:, pl.ds(3, n1 - 6), pl.ds(8, rows1)], g1_out),
        (r1.at[:, pl.ds(3, n1 - 6), pl.ds(8, rows1)], r1_out),
    ]
    for k, (src, dst) in enumerate(copies):
        started.append(pltpu.make_async_copy(src, dst, sem.at[5 + k]))
        started[-1].start()

    lane = lane_of(bx2) & 3
    packed = []
    for m in range(bz // 4):
        layer = 4 + 2 * m
        one = remainder(s1, y1, b1, d1, v1, layer, 8, rows1, 2)
        two = remainder(s1, y1, b1, d1, v1, layer + 1, 8, rows1, 2)
        fields = []
        for c in range(3):
            tmp[c, pl.ds(0, rows1), :] = one[c] + two[c]
            fields.append(pair_lanes(pair_rows(tmp.at[c], 4, bx2), 2))
        both = [pair_rows(s1.at[layer + i], 12, bx2) for i in range(2)]
        stiff = 0.5 * pair_lanes(both[0] + both[1], 2)
        packed.append(
            jnp.where(lane == 0, fields[0], jnp.where(lane == 1, fields[1], jnp.where(lane == 2, fields[2], stiff)))
        )
    both = [pair_rows(p1.at[4 + i], 12, bx2) for i in range(2)]
    packed.append(pair_lanes(both[0] + both[1], 2))

    def fill(i, carry):
        for m, value in enumerate(packed):
            send_ref[i, m, :, :] = value
        return carry

    lax.fori_loop(0, heights * tiles, fill, 0)
    for copy in started:
        copy.wait()


def up_kernel(
    heights, tiles, bz, bx,
    recv_ref, s0_in, y0_in, v0_in, g0_in, r0_in, s1_in, y1_in, v1_in, g1_in, r1_in,
    out_ref,
    s0, y0, v0, g0, r0, s1, y1, v1, g1, r1, f1, s2, p2, b2, q2, r2, d2, g2, v2, f2, s3, p3, b3, q3, r3, g3, va, vb, tmp, sem,
):
    h, t = lax.axis_index("height"), lax.axis_index("tile")
    bx1, bx2, bz2 = bx // 2, bx // 4, bz // 4
    n1, n2, n3 = bz // 2 + 4, heights * bz // 4, heights * bz // 8
    rows1 = bx1 + 8
    near = pl.ds(8, bx + 16)
    own = pl.ds(16, bx)
    mid = pl.ds(8, rows1)
    copies = [
        (s1_in, s1.at[:, mid]), (y1_in, y1.at[:, pl.ds(1, n1 - 2), mid]), (v1_in, v1.at[:, :, mid]),
        (g1_in, g1.at[:, pl.ds(1, n1 - 2), mid]), (r1_in, r1.at[:, pl.ds(1, n1 - 2), mid]),
        (s0_in, s0.at[:, near]), (y0_in, y0.at[:, pl.ds(1, bz), own]), (v0_in, v0.at[:, :, near]),
        (g0_in, g0.at[:, pl.ds(1, bz), own]), (r0_in, r0.at[:, pl.ds(1, bz), own]),
    ]
    started = []
    for k, (src, dst) in enumerate(copies):
        started.append(pltpu.make_async_copy(src, dst, sem.at[k]))
        started[-1].start()

    for ref in (s2, p2, g2, v2, f2, s3, p3, g3, va, vb):
        ref[...] = jnp.zeros(ref.shape, F32)
    tmp[...] = jnp.zeros(tmp.shape, F32)

    side = REACH // bx2
    lane = lane_of(bx2) & 3
    for dt in range(-side, side + 1):
        other = t + dt
        valid = (other >= 0) & (other < tiles)
        other = jnp.clip(other, 0, tiles - 1)
        scale = jnp.where(valid, 1.0, 0.0)
        dst = pl.ds(8 + (dt + side) * bx2, bx2)
        for hh in range(heights):
            for m in range(bz2):
                x = recv_ref[other * heights + hh, m] * scale
                layer = 1 + hh * bz2 + m
                b2[layer, dst, :] = jnp.where(lane == 3, 0.0, x)
                s2[layer, dst, :] = jnp.where(
                    lane == 3, x, jnp.where(lane == 2, roll(x, -1), jnp.where(lane == 1, roll(x, -2), roll(x, -3)))
                )
        p2[1, dst, :] = recv_ref[other * heights, bz2] * scale

    def weights(count):
        kind = lane_of(count) & 3
        return [jnp.where(kind == c, 2.0, 1.0) for c in range(3)]

    def setup(s_ref, p_ref, b_ref, q_ref, r_ref, d_ref, g_ref, layer, row, count, step):
        here, cross = cross_faces(s_ref, layer, row, count)
        low, high, low_in, high_in = lane_faces(here, step)
        w = weights(count)
        dst = pl.ds(row, count)
        for k in range(4):
            q_ref[k, layer, dst, :] = w[k // 2] * cross[k]
        q_ref[4, layer, dst, :] = w[2] * low_in
        q_ref[5, layer, dst, :] = w[2] * high_in
        doubled = rows_at(p_ref, layer, row, count) + (
            w[0] * (cross[0] + cross[1]) + w[1] * (cross[2] + cross[3]) + w[2] * (low + high)
        )
        rate = safe_rate(here, doubled)
        r_ref[layer, dst, :] = rate
        if d_ref is not None:
            d_ref[layer, dst, :] = doubled
        g_ref[layer, dst, :] = (2.0 * rate) * rows_at(b_ref, layer, row, count)

    def packed_sum(v_ref, q_ref, layer, row, count, step):
        faces = [q_ref[k, layer, pl.ds(row, count), :] for k in range(6)]
        here, along = neighbours(v_ref, faces, layer, row, count, step)
        return here, along[0] + along[1] + along[2]

    rows2 = bx2 + 2 * REACH

    def setup2(layer, carry):
        setup(s2, p2, b2, q2, r2, d2, g2, layer, 8, rows2, 4)
        return carry

    lax.fori_loop(1, n2 + 1, setup2, 0)

    def sweep2(layer, carry):
        here, total_ = packed_sum(g2, q2, layer, 8, rows2, 4)
        v2[layer, pl.ds(8, rows2), :] = (2.0 - OMEGA) * here + rows_at(r2, layer, 8, rows2) * total_
        return carry

    lax.fori_loop(1, n2 + 1, sweep2, 0)

    rows3 = -(-(rows2 // 2) // 8) * 8

    def restrict2(j, carry):
        rest = 0.0
        for i in range(2):
            layer = 1 + 2 * j + i
            here, total_ = packed_sum(v2, q2, layer, 8, rows2, 4)
            rest = rest + rows_at(b2, layer, 8, rows2) + 0.5 * (total_ - rows_at(d2, layer, 8, rows2) * here)
        tmp[0, pl.ds(8, rows2), :] = rest
        dst = pl.ds(8, rows3)
        b3[j + 1, dst, :] = pair_lanes(pair_rows(tmp.at[0], 8, rows3), 4)
        for field, scale, into in ((s2, 0.5, s3), (p2, 1.0, p3)):
            both = [pair_rows(field.at[1 + 2 * j + i], 8, rows3) for i in range(2)]
            into[j + 1, dst, :] = scale * pair_lanes(both[0] + both[1], 4)
        return carry

    lax.fori_loop(0, n3, restrict2, 0)

    for layer in range(1, n3 + 1):
        setup(s3, p3, b3, q3, r3, None, g3, layer, 8, rows3, 8)
    source, target = g3, va
    for _ in range(COARSE_SWEEPS - 1):
        for layer in range(1, n3 + 1):
            here, total_ = packed_sum(source, q3, layer, 8, rows3, 8)
            target[layer, pl.ds(8, rows3), :] = (
                (1.0 - OMEGA) * here + rows_at(g3, layer, 8, rows3) + rows_at(r3, layer, 8, rows3) * total_
            )
        source, target = target, (vb if target is va else va)
    coarse = source

    wide2 = bx2 + 16

    def lift2(layer, carry):
        spread_rows(tmp.at[0], coarse[(layer + 1) // 2, pl.ds(12, wide2 // 2), :])
        v2[layer, pl.ds(16, wide2), :] += tmp[0, pl.ds(0, wide2), :]
        return carry

    lax.fori_loop(1, n2 + 1, lift2, 0)

    def post2(layer, carry):
        here, total_ = packed_sum(v2, q2, layer, 16, wide2, 4)
        f2[layer, pl.ds(16, wide2), :] = (
            (1.0 - OMEGA) * here + rows_at(g2, layer, 16, wide2) + rows_at(r2, layer, 16, wide2) * total_
        )
        return carry

    lax.fori_loop(1, n2 + 1, post2, 0)

    for copy in started[:5]:
        copy.wait()
    kind = lane_of(bx2 + 4) & 3

    def lift1(m, carry):
        x = f2[bz2 * h + m, pl.ds(22, bx2 + 4), :]
        moved = {shift: roll(x, shift) if shift else x for shift in range(-2, 4)}
        for c in range(3):
            part = jnp.where(
                kind == 0, moved[-c], jnp.where(kind == 1, moved[1 - c], jnp.where(kind == 2, moved[2 - c], moved[3 - c]))
            )
            spread_rows(tmp.at[c], part)
            lifted = tmp[c, pl.ds(0, rows1), :]
            for i in range(2):
                v1[c, 2 * m + i, mid, :] += lifted
        return carry

    lax.fori_loop(0, n1 // 2, lift1, 0)

    def post(s_ref, y_ref, g_ref, r_ref, v_ref, into, layer, to, row, count, step):
        faces = all_faces(s_ref, y_ref, layer, row, count)
        for c in range(3):
            here, along = neighbours(v_ref.at[c], faces, layer, row, count, step)
            dst = pl.ds(row, count)
            into(c, (1.0 - OMEGA) * here + g_ref[c, layer, dst, :] + r_ref[c, layer, dst, :] * total(along, c))

    def post1(layer, carry):
        def into(c, value):
            f1[c, layer, mid, :] = value

        post(s1, y1, g1, r1, v1, into, layer, layer, 8, rows1, 2)
        return carry

    lax.fori_loop(1, n1 - 1, post1, 0)

    for copy in started[5:]:
        copy.wait()

    for c in range(3):
        for k in range(1, n1 - 1):
            spread_rows(tmp.at[c], f1[c, k, mid, :])
            lifted = tmp[c, pl.ds(0, bx + 16), :]
            for i in (2 * k - 3, 2 * k - 2):
                if 0 <= i < bz + 2:
                    v0[c, i, near, :] += lifted

    def post0(layer, carry):
        for row, count in chunks(16, 16 + bx, 16):

            def into(c, value):
                out_ref[c, layer - 1, pl.ds(row - 16, count), :] = value

            post(s0, y0, g0, r0, v0, into, layer, layer, row, count, 1)
        return carry

    lax.fori_loop(1, bz + 1, post0, 0)


def passed_along(x, axis, by):
    size = lax.axis_size(axis)
    return lax.ppermute(x, axis, [(i, i + by) for i in range(size) if 0 <= i + by < size])


def vmem(*shape):
    return pltpu.VMEM(shape, F32)


def local(heights, tiles, material, clamped, stiffness_table, eigenstrain):
    bz, bx, _ = material.shape
    labels = jnp.concatenate([material, clamped[:2]], 0)
    after = passed_along(labels[:, bx - HALO :].reshape(-1, LANES), "tile", 1)
    ahead = passed_along(labels[:, :HALO].reshape(-1, LANES), "tile", -1)
    rows = (bz + 2) * (bx + 2 * HALO)
    pad = jnp.zeros((-rows % 8, LANES), labels.dtype)
    brick = jnp.concatenate([labels.reshape(-1, LANES), after, ahead, pad], 0)
    bricks = lax.all_gather(brick, "height")

    bx1, bx2 = bx // 2, bx // 4
    nz, n1 = bz + 2 * HALO, bz // 2 + 8
    r0, r1 = bx + 32, bx1 + 24
    rows1 = bx1 + 8
    held = pl.BlockSpec(memory_space=pltpu.VMEM)
    scalar = pl.BlockSpec(memory_space=pltpu.SMEM)
    anywhere = pl.BlockSpec(memory_space=pl.ANY)
    kept = [
        (bz + 2, bx + 16), (2, bz, bx), (3, bz + 2, bx + 16), (3, bz, bx), (3, bz, bx),
        (n1 - 4, rows1), (2, n1 - 6, rows1), (3, n1 - 4, rows1), (3, n1 - 6, rows1), (3, n1 - 6, rows1),
    ]
    kept = [jax.ShapeDtypeStruct((*shape, LANES), F32) for shape in kept]
    field0, field1 = (nz, r0, LANES), (n1, r1, LANES)
    send, *saved = pl.pallas_call(
        functools.partial(down_kernel, heights, tiles, bz, bx),
        out_shape=[jax.ShapeDtypeStruct((heights * tiles, bz // 4 + 1, bx2, LANES), F32), *kept],
        in_specs=[held, scalar, scalar],
        out_specs=[held] + [anywhere] * len(kept),
        scratch_shapes=[
            vmem(*field0), vmem(*field0), vmem(3, *field0), vmem(3, *field0), vmem(3, *field0), vmem(3, *field0),
            vmem(3, *field0), vmem(2, *field0), vmem(3, *field0), vmem(3, r0, LANES),
            vmem(*field1), vmem(*field1), vmem(3, *field1), vmem(3, *field1), vmem(3, *field1), vmem(3, *field1),
            vmem(2, *field1), vmem(3, *field1), pltpu.SemaphoreType.DMA((10,)),
        ],
        compiler_params=pltpu.CompilerParams(vmem_limit_bytes=40 * 2**20),
    )(bricks, stiffness_table, eigenstrain)

    received = lax.all_to_all(send, ("tile", "height"), 0, 0)

    rows2 = bx2 + 2 * REACH
    rows3 = -(-(rows2 // 2) // 8) * 8
    up0, up1 = (bz + 2, r0, LANES), (n1 - 4, r1, LANES)
    up2 = (heights * bz // 4 + 2, rows2 + 16, LANES)
    up3 = (heights * bz // 8 + 2, rows3 + 16, LANES)
    return pl.pallas_call(
        functools.partial(up_kernel, heights, tiles, bz, bx),
        out_shape=jax.ShapeDtypeStruct((3, bz, bx, LANES), F32),
        in_specs=[held] + [anywhere] * len(kept),
        out_specs=held,
        scratch_shapes=[
            vmem(*up0), vmem(2, *up0), vmem(3, *up0), vmem(3, *up0), vmem(3, *up0),
            vmem(*up1), vmem(2, *up1), vmem(3, *up1), vmem(3, *up1), vmem(3, *up1), vmem(3, *up1),
            vmem(*up2), vmem(*up2), vmem(*up2), vmem(6, *up2), vmem(*up2), vmem(*up2), vmem(*up2), vmem(*up2), vmem(*up2),
            vmem(*up3), vmem(*up3), vmem(*up3), vmem(6, *up3), vmem(*up3), vmem(*up3), vmem(*up3), vmem(*up3),
            vmem(3, r0, LANES), pltpu.SemaphoreType.DMA((10,)),
        ],
        compiler_params=pltpu.CompilerParams(vmem_limit_bytes=40 * 2**20),
    )(received, *saved)


def solution(mesh):
    sides = mesh.shape["height"], mesh.shape["tile"]
    in_specs = (P("height", "tile", None), P("height", "tile", None), P(), P())
    out_specs = P(None, "height", "tile", None)
    return jax.shard_map(
        functools.partial(local, *sides), mesh=mesh, in_specs=in_specs, out_specs=out_specs, check_vma=False
    )
```

```python
import functools

import jax
import jax.numpy as jnp
from jax import lax
from jax.experimental import pallas as pl
from jax.experimental.pallas import tpu as pltpu
from jax.sharding import PartitionSpec as P

PENALTY = 50.0
OMEGA = 0.6
COARSE_SWEEPS = 6
LANES = 128
HALO = 9
REACH = 16
SPARE = 4
F32 = jnp.float32


def each(start, stop, body, step):
    groups = (stop - start) // step

    def group(i, carry):
        for k in range(step):
            body(start + i * step + k, 0)
        return carry

    if groups > 1:
        lax.fori_loop(0, groups, group, 0)
    elif groups == 1:
        group(0, 0)
    for layer in range(start + groups * step, stop):
        body(layer, 0)


def chunks(start, stop, size):
    return [(row, min(size, stop - row)) for row in range(start, stop, size)]


def lane_of(rows):
    return lax.broadcasted_iota(jnp.int32, (rows, LANES), 1)


def roll(x, shift):
    return pltpu.roll(x, shift % LANES, 1)


def rows_at(ref, layer, row, count):
    return ref[layer, pl.ds(row, count), :]


def cross_faces(s_ref, layer, row, count):
    here = rows_at(s_ref, layer, row, count)
    return here, [
        here + rows_at(s_ref, layer - 1, row, count),
        here + rows_at(s_ref, layer + 1, row, count),
        here + rows_at(s_ref, layer, row - 1, count),
        here + rows_at(s_ref, layer, row + 1, count),
    ]


def lane_faces(here, step):
    lane = lane_of(here.shape[0])
    first, last = lane < step, lane >= LANES - step
    low = here + jnp.where(first, 0.0, roll(here, step))
    high = here + jnp.where(last, 0.0, roll(here, -step))
    return low, high, jnp.where(first, 0.0, low), jnp.where(last, 0.0, high)


def neighbours(v_ref, faces, layer, row, count, step):
    here = rows_at(v_ref, layer, row, count)
    along = [
        faces[0] * rows_at(v_ref, layer - 1, row, count)
        + faces[1] * rows_at(v_ref, layer + 1, row, count),
        faces[2] * rows_at(v_ref, layer, row - 1, count)
        + faces[3] * rows_at(v_ref, layer, row + 1, count),
        faces[4] * roll(here, step) + faces[5] * roll(here, -step),
    ]
    return here, along


def total(along, component):
    return (along[0] + along[1] + along[2]) + along[component]


def safe_rate(here, doubled):
    return jnp.where(here > 0.0, OMEGA / doubled, 0.0)


def pair_lanes(x, step):
    upper = (lane_of(x.shape[0]) & step) != 0
    return x + jnp.where(upper, roll(x, step), roll(x, -step))


def pair_rows(ref, row, count):
    return ref[pl.ds(row, count, stride=2), :] + ref[pl.ds(row + 1, count, stride=2), :]


def spread_rows(ref, x):
    count = x.shape[0]
    ref[pl.ds(0, count, stride=2), :] = x
    ref[pl.ds(1, count, stride=2), :] = x


def level_setup(s_ref, p_ref, r_ref, d_ref, g_ref, y_ref, b_of, layer, row, count, step):
    here, cross = cross_faces(s_ref, layer, row, count)
    low, high, low_in, high_in = lane_faces(here, step)
    y_ref[0, layer, pl.ds(row, count), :] = low_in
    y_ref[1, layer, pl.ds(row, count), :] = high_in
    sums = [cross[0] + cross[1], cross[2] + cross[3], low + high]
    base = rows_at(p_ref, layer, row, count) + (sums[0] + sums[1] + sums[2])
    for c in range(3):
        doubled = base + sums[c]
        rate = safe_rate(here, doubled)
        d_ref[c, layer, pl.ds(row, count), :] = doubled
        r_ref[c, layer, pl.ds(row, count), :] = rate
        g_ref[c, layer, pl.ds(row, count), :] = (2.0 * rate) * b_of(c)


def all_faces(s_ref, y_ref, layer, row, count):
    _, cross = cross_faces(s_ref, layer, row, count)
    return cross + [
        y_ref[0, layer, pl.ds(row, count), :],
        y_ref[1, layer, pl.ds(row, count), :],
    ]


def first_sweep(s_ref, y_ref, r_ref, g_ref, v_ref, layer, row, count, step):
    faces = all_faces(s_ref, y_ref, layer, row, count)
    for c in range(3):
        here, along = neighbours(g_ref.at[c], faces, layer, row, count, step)
        rate = r_ref[c, layer, pl.ds(row, count), :]
        v_ref[c, layer, pl.ds(row, count), :] = (2.0 - OMEGA) * here + rate * total(along, c)


def remainder(s_ref, y_ref, b_ref, d_ref, v_ref, layer, row, count, step):
    faces = all_faces(s_ref, y_ref, layer, row, count)
    result = []
    for c in range(3):
        here, along = neighbours(v_ref.at[c], faces, layer, row, count, step)
        doubled = d_ref[c, layer, pl.ds(row, count), :]
        source = b_ref[c, layer, pl.ds(row, count), :]
        result.append(source + 0.5 * (total(along, c) - doubled * here))
    return result


def pack_kernel(
    bz, bx, material_ref, clamped_ref, table_ref, strain_ref, own_ref, after_ref, ahead_ref, label, joined, table, strain, sem
):
    copies = [
        pltpu.make_async_copy(material_ref, label, sem.at[0]),
        pltpu.make_async_copy(clamped_ref.at[pl.ds(0, 2)], joined, sem.at[1]),
        pltpu.make_async_copy(table_ref, table, sem.at[2]),
        pltpu.make_async_copy(strain_ref, strain, sem.at[3]),
    ]
    for copy in copies:
        copy.start()
    for copy in copies:
        copy.wait()
    for slot in range(bz + 2):
        src = label.at[slot] if slot < bz else joined.at[slot - bz]
        own_ref[pl.ds(slot * bx, bx), :] = src[...].astype(F32)
        after_ref[pl.ds(slot * HALO, HALO), :] = src[pl.ds(bx - HALO, HALO), :].astype(F32)
        ahead_ref[pl.ds(slot * HALO, HALO), :] = src[pl.ds(0, HALO), :].astype(F32)
    lane = lane_of(SPARE)
    row = jnp.zeros((SPARE, LANES), F32)
    for k in range(3):
        row = jnp.where(lane == k, table[k], row)
        for c in range(3):
            row = jnp.where(lane == 3 + 3 * c + k, table[k] * strain[k, c], row)
    own_ref[pl.ds((bz + 2) * bx, SPARE), :] = row


def down_kernel(
    heights, tiles, bz, bx,
    x_ref,
    send_ref, s0_out, y0_out, v0_out, g0_out, r0_out, s1_out, y1_out, v1_out, g1_out, r1_out,
    s, p, st, b, r, d, g, y, v, tmp, s1, p1, b1, r1, d1, g1, y1, v1, sem,
):
    h, t = lax.axis_index("height"), lax.axis_index("tile")
    nz, n1 = bz + 2 * HALO, bz // 2 + 8
    bx1, bx2 = bx // 2, bx // 4
    low, high = 8, bx + 24
    own_rows, halo_rows = (bz + 2) * bx + SPARE, (bz + 2) * HALO
    spare = x_ref[0, pl.ds(own_rows - SPARE, 1), :]
    table = [jnp.broadcast_to(spare[:, k : k + 1], (1, LANES)) for k in range(12)]
    strain = [table[3 + 3 * c : 6 + 3 * c] for c in range(3)]
    before = jnp.where(t > 0, 1.0, 0.0)
    behind = jnp.where(t < tiles - 1, 1.0, 0.0)

    def read_layer(layer, carry):
        z = bz * h - HALO + layer
        inside = jnp.where((z >= 0) & (z < heights * bz), 1.0, 0.0)
        bottom = jnp.where((z >= 0) & (z < 2), 2.0 * PENALTY, 0.0)
        z_in = jnp.clip(z, 0, heights * bz - 1)
        brick, slot = z_in // bz, z_in % bz
        clamp_slot = bz + jnp.clip(z, 0, 1)
        parts = [
            (slot * bx, clamp_slot * bx, bx, 16, 1.0),
            (own_rows + slot * HALO, own_rows + clamp_slot * HALO, HALO, 16 - HALO, before),
            (own_rows + halo_rows + slot * HALO, own_rows + halo_rows + clamp_slot * HALO, HALO, 16 + bx, behind),
        ]
        for at, clamp_at, count, to, valid in parts:
            label = x_ref[brick, pl.ds(at, count), :]
            is0, is1 = label == 0.0, label == 1.0
            weight = inside * valid
            stiff = [table[k] * weight for k in range(3)]
            dst = pl.ds(to, count)
            s[layer, dst, :] = jnp.where(is0, stiff[0], jnp.where(is1, stiff[1], stiff[2]))
            for c in range(3):
                e = [strain[c][k] * weight for k in range(3)]
                st[c, layer, dst, :] = jnp.where(is0, e[0], jnp.where(is1, e[1], e[2]))
            joined = x_ref[0, pl.ds(clamp_at, count), :]
            p[layer, dst, :] = joined * (bottom * valid)
        return carry

    each(0, nz, read_layer, 8)

    def setup0(layer, carry):
        for row, count in chunks(low, high, 16):
            lane = lane_of(count)
            here = st[2, layer, pl.ds(row, count), :]
            source = [
                0.5 * (rows_at(st.at[0], layer - 1, row, count) - rows_at(st.at[0], layer + 1, row, count)),
                0.5 * (rows_at(st.at[1], layer, row - 1, count) - rows_at(st.at[1], layer, row + 1, count)),
                0.5 * (jnp.where(lane < 1, 0.0, roll(here, 1)) - jnp.where(lane >= LANES - 1, 0.0, roll(here, -1))),
            ]
            for c in range(3):
                b[c, layer, pl.ds(row, count), :] = source[c]
            level_setup(s, p, r, d, g, y, lambda c: source[c], layer, row, count, 1)
        return carry

    each(1, nz - 1, setup0, 8)

    def sweep0(layer, carry):
        for row, count in chunks(low, high, 16):
            first_sweep(s, y, r, g, v, layer, row, count, 1)
        return carry

    each(2, nz - 2, sweep0, 8)

    own = (pl.ds(HALO, bz), pl.ds(16, bx))
    near = (pl.ds(HALO - 1, bz + 2), pl.ds(low, bx + 16))
    copies = [
        (s.at[near[0], near[1]], s0_out),
        (y.at[:, own[0], own[1]], y0_out),
        (v.at[:, near[0], near[1]], v0_out),
        (g.at[:, own[0], own[1]], g0_out),
        (r.at[:, own[0], own[1]], r0_out),
    ]
    started = []
    for k, (src, dst) in enumerate(copies):
        started.append(pltpu.make_async_copy(src, dst, sem.at[k]))
        started[-1].start()

    rows1 = bx1 + 8

    def restrict0(j, carry):
        layer = 3 + 2 * j
        for row, count in chunks(low, high, 16):
            one = remainder(s, y, b, d, v, layer, row, count, 1)
            two = remainder(s, y, b, d, v, layer + 1, row, count, 1)
            for c in range(3):
                tmp[c, pl.ds(row, count), :] = one[c] + two[c]
        for c in range(3):
            b1[c, j + 1, pl.ds(8, rows1), :] = pair_lanes(pair_rows(tmp.at[c], low, rows1), 1)
        return carry

    each(0, n1 - 2, restrict0, 8)

    def coarse0(k, carry):
        for field, scale, into in ((s, 0.5, s1), (p, 1.0, p1)):
            both = [pair_rows(field.at[1 + 2 * k + i], low, rows1) for i in range(2)]
            into[k, pl.ds(8, rows1), :] = scale * pair_lanes(both[0] + both[1], 1)
        return carry

    each(0, n1, coarse0, 8)

    def setup1(layer, carry):
        level_setup(
            s1, p1, r1, d1, g1, y1,
            lambda c: b1[c, layer, pl.ds(8, rows1), :], layer, 8, rows1, 2,
        )
        return carry

    each(1, n1 - 1, setup1, 8)

    def sweep1(layer, carry):
        first_sweep(s1, y1, r1, g1, v1, layer, 8, rows1, 2)
        return carry

    each(2, n1 - 2, sweep1, 8)

    copies = [
        (s1.at[pl.ds(2, n1 - 4), pl.ds(8, rows1)], s1_out),
        (y1.at[:, pl.ds(3, n1 - 6), pl.ds(8, rows1)], y1_out),
        (v1.at[:, pl.ds(2, n1 - 4), pl.ds(8, rows1)], v1_out),
        (g1.at[:, pl.ds(3, n1 - 6), pl.ds(8, rows1)], g1_out),
        (r1.at[:, pl.ds(3, n1 - 6), pl.ds(8, rows1)], r1_out),
    ]
    for k, (src, dst) in enumerate(copies):
        started.append(pltpu.make_async_copy(src, dst, sem.at[5 + k]))
        started[-1].start()

    lane = lane_of(bx2) & 3
    packed = []
    for m in range(bz // 4):
        layer = 4 + 2 * m
        one = remainder(s1, y1, b1, d1, v1, layer, 8, rows1, 2)
        two = remainder(s1, y1, b1, d1, v1, layer + 1, 8, rows1, 2)
        fields = []
        for c in range(3):
            tmp[c, pl.ds(0, rows1), :] = one[c] + two[c]
            fields.append(pair_lanes(pair_rows(tmp.at[c], 4, bx2), 2))
        both = [pair_rows(s1.at[layer + i], 12, bx2) for i in range(2)]
        stiff = 0.5 * pair_lanes(both[0] + both[1], 2)
        packed.append(
            jnp.where(lane == 0, fields[0], jnp.where(lane == 1, fields[1], jnp.where(lane == 2, fields[2], stiff)))
        )
    both = [pair_rows(p1.at[4 + i], 12, bx2) for i in range(2)]
    tmp[0, pl.ds(0, bx2), :] = pair_lanes(both[0] + both[1], 2)
    quarter = bx2 // 4
    part = [tmp[0, pl.ds(j, quarter, stride=4), :] for j in range(4)]
    lane = lane_of(quarter) & 3
    packed.append(jnp.where(lane == 0, part[0], jnp.where(lane == 1, part[1], jnp.where(lane == 2, part[2], part[3]))))

    def fill(i, carry):
        for m, value in enumerate(packed):
            for k in range(value.shape[0] // 2):
                send_ref[i, m * bx2 // 2 + k, :, :] = value[2 * k : 2 * k + 2]
        return carry

    each(0, heights * tiles, fill, 8)
    for copy in started:
        copy.wait()


def up_kernel(
    heights, tiles, bz, bx,
    recv_ref, s0_in, y0_in, v0_in, g0_in, r0_in, s1_in, y1_in, v1_in, g1_in, r1_in,
    out_ref,
    s0, y0, v0, g0, r0, s1, y1, v1, g1, r1, f1, s2, p2, b2, q2, r2, d2, g2, v2, f2, s3, p3, b3, q3, r3, g3, va, vb, tmp, sem,
):
    h, t = lax.axis_index("height"), lax.axis_index("tile")
    bx1, bx2, bz2 = bx // 2, bx // 4, bz // 4
    n1, n2, n3 = bz // 2 + 4, heights * bz // 4, heights * bz // 8
    rows1 = bx1 + 8
    near = pl.ds(8, bx + 16)
    own = pl.ds(16, bx)
    mid = pl.ds(8, rows1)
    copies = [
        (s1_in, s1.at[:, mid]), (y1_in, y1.at[:, pl.ds(1, n1 - 2), mid]), (v1_in, v1.at[:, :, mid]),
        (g1_in, g1.at[:, pl.ds(1, n1 - 2), mid]), (r1_in, r1.at[:, pl.ds(1, n1 - 2), mid]),
        (s0_in, s0.at[:, near]), (y0_in, y0.at[:, pl.ds(1, bz), own]), (v0_in, v0.at[:, :, near]),
        (g0_in, g0.at[:, pl.ds(1, bz), own]), (r0_in, r0.at[:, pl.ds(1, bz), own]),
    ]
    started = []
    for k, (src, dst) in enumerate(copies):
        started.append(pltpu.make_async_copy(src, dst, sem.at[k]))
        started[-1].start()

    for ref in (s2, p2, g2, v2, f2, s3, p3, g3, va, vb):
        ref[...] = jnp.zeros(ref.shape, F32)
    tmp[...] = jnp.zeros(tmp.shape, F32)

    side = REACH // bx2
    lane = lane_of(bx2) & 3
    for dt in range(-side, side + 1):
        other = t + dt
        valid = (other >= 0) & (other < tiles)
        other = jnp.clip(other, 0, tiles - 1)
        scale = jnp.where(valid, 1.0, 0.0)
        dst = pl.ds(8 + (dt + side) * bx2, bx2)
        for hh in range(heights):
            for m in range(bz2):
                x = recv_ref[other * heights + hh, pl.ds(m * bx2 // 2, bx2 // 2)].reshape(bx2, LANES) * scale
                layer = 1 + hh * bz2 + m
                b2[layer, dst, :] = jnp.where(lane == 3, 0.0, x)
                s2[layer, dst, :] = jnp.where(
                    lane == 3, x, jnp.where(lane == 2, roll(x, -1), jnp.where(lane == 1, roll(x, -2), roll(x, -3)))
                )
        quarter = bx2 // 4
        x = recv_ref[other * heights, pl.ds(bz2 * bx2 // 2, quarter // 2)].reshape(quarter, LANES) * scale
        moved = {shift: roll(x, shift) if shift else x for shift in range(-3, 4)}
        small = lane_of(quarter) & 3
        for j in range(4):
            p2[1, pl.ds(8 + (dt + side) * bx2 + j, quarter, stride=4), :] = jnp.where(
                small == 0, moved[-j], jnp.where(small == 1, moved[1 - j], jnp.where(small == 2, moved[2 - j], moved[3 - j]))
            )

    def weights(count):
        kind = lane_of(count) & 3
        return [jnp.where(kind == c, 2.0, 1.0) for c in range(3)]

    def setup(s_ref, p_ref, b_ref, q_ref, r_ref, d_ref, g_ref, layer, row, count, step):
        here, cross = cross_faces(s_ref, layer, row, count)
        low, high, low_in, high_in = lane_faces(here, step)
        w = weights(count)
        dst = pl.ds(row, count)
        for k in range(4):
            q_ref[k, layer, dst, :] = w[k // 2] * cross[k]
        q_ref[4, layer, dst, :] = w[2] * low_in
        q_ref[5, layer, dst, :] = w[2] * high_in
        doubled = rows_at(p_ref, layer, row, count) + (
            w[0] * (cross[0] + cross[1]) + w[1] * (cross[2] + cross[3]) + w[2] * (low + high)
        )
        rate = safe_rate(here, doubled)
        r_ref[layer, dst, :] = rate
        if d_ref is not None:
            d_ref[layer, dst, :] = doubled
        g_ref[layer, dst, :] = (2.0 * rate) * rows_at(b_ref, layer, row, count)

    def packed_sum(v_ref, q_ref, layer, row, count, step):
        faces = [q_ref[k, layer, pl.ds(row, count), :] for k in range(6)]
        here, along = neighbours(v_ref, faces, layer, row, count, step)
        return here, along[0] + along[1] + along[2]

    rows2 = bx2 + 2 * REACH

    def setup2(layer, carry):
        setup(s2, p2, b2, q2, r2, d2, g2, layer, 8, rows2, 4)
        return carry

    each(1, n2 + 1, setup2, 8)

    def sweep2(layer, carry):
        here, total_ = packed_sum(g2, q2, layer, 8, rows2, 4)
        v2[layer, pl.ds(8, rows2), :] = (2.0 - OMEGA) * here + rows_at(r2, layer, 8, rows2) * total_
        return carry

    each(1, n2 + 1, sweep2, 8)

    rows3 = -(-(rows2 // 2) // 8) * 8

    def restrict2(j, carry):
        rest = 0.0
        for i in range(2):
            layer = 1 + 2 * j + i
            here, total_ = packed_sum(v2, q2, layer, 8, rows2, 4)
            rest = rest + rows_at(b2, layer, 8, rows2) + 0.5 * (total_ - rows_at(d2, layer, 8, rows2) * here)
        tmp[0, pl.ds(8, rows2), :] = rest
        dst = pl.ds(8, rows3)
        b3[j + 1, dst, :] = pair_lanes(pair_rows(tmp.at[0], 8, rows3), 4)
        for field, scale, into in ((s2, 0.5, s3), (p2, 1.0, p3)):
            both = [pair_rows(field.at[1 + 2 * j + i], 8, rows3) for i in range(2)]
            into[j + 1, dst, :] = scale * pair_lanes(both[0] + both[1], 4)
        return carry

    each(0, n3, restrict2, 8)

    for layer in range(1, n3 + 1):
        setup(s3, p3, b3, q3, r3, None, g3, layer, 8, rows3, 8)
    source, target = g3, va
    for _ in range(COARSE_SWEEPS - 1):
        for layer in range(1, n3 + 1):
            here, total_ = packed_sum(source, q3, layer, 8, rows3, 8)
            target[layer, pl.ds(8, rows3), :] = (
                (1.0 - OMEGA) * here + rows_at(g3, layer, 8, rows3) + rows_at(r3, layer, 8, rows3) * total_
            )
        source, target = target, (vb if target is va else va)
    coarse = source

    wide2 = bx2 + 16

    def lift2(layer, carry):
        spread_rows(tmp.at[0], coarse[(layer + 1) // 2, pl.ds(12, wide2 // 2), :])
        v2[layer, pl.ds(16, wide2), :] += tmp[0, pl.ds(0, wide2), :]
        return carry

    each(1, n2 + 1, lift2, 8)

    def post2(layer, carry):
        here, total_ = packed_sum(v2, q2, layer, 16, wide2, 4)
        f2[layer, pl.ds(16, wide2), :] = (
            (1.0 - OMEGA) * here + rows_at(g2, layer, 16, wide2) + rows_at(r2, layer, 16, wide2) * total_
        )
        return carry

    each(1, n2 + 1, post2, 8)

    for copy in started[:5]:
        copy.wait()
    kind = lane_of(bx2 + 4) & 3

    def lift1(m, carry):
        x = f2[bz2 * h + m, pl.ds(22, bx2 + 4), :]
        moved = {shift: roll(x, shift) if shift else x for shift in range(-2, 4)}
        for c in range(3):
            part = jnp.where(
                kind == 0, moved[-c], jnp.where(kind == 1, moved[1 - c], jnp.where(kind == 2, moved[2 - c], moved[3 - c]))
            )
            spread_rows(tmp.at[c], part)
            lifted = tmp[c, pl.ds(0, rows1), :]
            for i in range(2):
                v1[c, 2 * m + i, mid, :] += lifted
        return carry

    each(0, n1 // 2, lift1, 8)

    def post(s_ref, y_ref, g_ref, r_ref, v_ref, into, layer, to, row, count, step):
        faces = all_faces(s_ref, y_ref, layer, row, count)
        for c in range(3):
            here, along = neighbours(v_ref.at[c], faces, layer, row, count, step)
            dst = pl.ds(row, count)
            into(c, (1.0 - OMEGA) * here + g_ref[c, layer, dst, :] + r_ref[c, layer, dst, :] * total(along, c))

    def post1(layer, carry):
        def into(c, value):
            f1[c, layer, mid, :] = value

        post(s1, y1, g1, r1, v1, into, layer, layer, 8, rows1, 2)
        return carry

    each(1, n1 - 1, post1, 8)

    for copy in started[5:]:
        copy.wait()

    for c in range(3):
        for k in range(1, n1 - 1):
            spread_rows(tmp.at[c], f1[c, k, mid, :])
            lifted = tmp[c, pl.ds(0, bx + 16), :]
            for i in (2 * k - 3, 2 * k - 2):
                if 0 <= i < bz + 2:
                    v0[c, i, near, :] += lifted

    def post0(layer, carry):
        for row, count in chunks(16, 16 + bx, 16):

            def into(c, value):
                out_ref[c, layer - 1, pl.ds(row - 16, count), :] = value

            post(s0, y0, g0, r0, v0, into, layer, layer, row, count, 1)
        return carry

    each(1, bz + 1, post0, 8)


def passed_along(x, axis, by):
    size = lax.axis_size(axis)
    return lax.ppermute(x, axis, [(i, i + by) for i in range(size) if 0 <= i + by < size])


def vmem(*shape):
    return pltpu.VMEM(shape, F32)


def local(heights, tiles, material, clamped, stiffness_table, eigenstrain):
    bz, bx, _ = material.shape

    held = pl.BlockSpec(memory_space=pltpu.VMEM)
    anywhere = pl.BlockSpec(memory_space=pl.ANY)
    outside = pl.BlockSpec(memory_space=pltpu.HBM)
    slots = bz + 2
    own, after, ahead = pl.pallas_call(
        functools.partial(pack_kernel, bz, bx),
        out_shape=[
            pltpu.VMEM((rows, LANES), F32)
            for rows in (slots * bx + SPARE, slots * HALO, slots * HALO)
        ],
        in_specs=[outside] * 4,
        out_specs=[held] * 3,
        scratch_shapes=[
            pltpu.VMEM((bz, bx, LANES), jnp.int32), pltpu.VMEM((2, bx, LANES), jnp.int32),
            pltpu.SMEM((3,), F32), pltpu.SMEM((3, 3), F32), pltpu.SemaphoreType.DMA((4,)),
        ],
    )(material, clamped, stiffness_table, eigenstrain)
    after, ahead = passed_along(after, "tile", 1), passed_along(ahead, "tile", -1)
    bricks = lax.all_gather(jnp.concatenate([own, after, ahead], 0), "height")

    bx1, bx2 = bx // 2, bx // 4
    nz, n1 = bz + 2 * HALO, bz // 2 + 8
    r0, r1 = bx + 32, bx1 + 24
    rows1 = bx1 + 8
    kept = [
        (bz + 2, bx + 16), (2, bz, bx), (3, bz + 2, bx + 16), (3, bz, bx), (3, bz, bx),
        (n1 - 4, rows1), (2, n1 - 6, rows1), (3, n1 - 4, rows1), (3, n1 - 6, rows1), (3, n1 - 6, rows1),
    ]
    kept = [jax.ShapeDtypeStruct((*shape, LANES), F32) for shape in kept]
    field0, field1 = (nz, r0, LANES), (n1, r1, LANES)
    send, *saved = pl.pallas_call(
        functools.partial(down_kernel, heights, tiles, bz, bx),
        out_shape=[jax.ShapeDtypeStruct((heights * tiles, (bz // 4 * bx2 + bx2 // 4) // 2, 2, LANES), F32), *kept],
        in_specs=[held],
        out_specs=[held] + [anywhere] * len(kept),
        scratch_shapes=[
            vmem(*field0), vmem(*field0), vmem(3, *field0), vmem(3, *field0), vmem(3, *field0), vmem(3, *field0),
            vmem(3, *field0), vmem(2, *field0), vmem(3, *field0), vmem(3, r0, LANES),
            vmem(*field1), vmem(*field1), vmem(3, *field1), vmem(3, *field1), vmem(3, *field1), vmem(3, *field1),
            vmem(2, *field1), vmem(3, *field1), pltpu.SemaphoreType.DMA((10,)),
        ],
        compiler_params=pltpu.CompilerParams(vmem_limit_bytes=40 * 2**20),
    )(bricks)

    received = lax.all_to_all(send, ("tile", "height"), 0, 0)

    rows2 = bx2 + 2 * REACH
    rows3 = -(-(rows2 // 2) // 8) * 8
    up0, up1 = (bz + 2, r0, LANES), (n1 - 4, r1, LANES)
    up2 = (heights * bz // 4 + 2, rows2 + 16, LANES)
    up3 = (heights * bz // 8 + 2, rows3 + 16, LANES)
    return pl.pallas_call(
        functools.partial(up_kernel, heights, tiles, bz, bx),
        out_shape=jax.ShapeDtypeStruct((3, bz, bx, LANES), F32),
        in_specs=[held] + [anywhere] * len(kept),
        out_specs=held,
        scratch_shapes=[
            vmem(*up0), vmem(2, *up0), vmem(3, *up0), vmem(3, *up0), vmem(3, *up0),
            vmem(*up1), vmem(2, *up1), vmem(3, *up1), vmem(3, *up1), vmem(3, *up1), vmem(3, *up1),
            vmem(*up2), vmem(*up2), vmem(*up2), vmem(6, *up2), vmem(*up2), vmem(*up2), vmem(*up2), vmem(*up2), vmem(*up2),
            vmem(*up3), vmem(*up3), vmem(*up3), vmem(6, *up3), vmem(*up3), vmem(*up3), vmem(*up3), vmem(*up3),
            vmem(3, r0, LANES), pltpu.SemaphoreType.DMA((10,)),
        ],
        compiler_params=pltpu.CompilerParams(vmem_limit_bytes=40 * 2**20),
    )(received, *saved)


def solution(mesh):
    sides = mesh.shape["height"], mesh.shape["tile"]
    in_specs = (P("height", "tile", None), P("height", "tile", None), P(), P())
    out_specs = P(None, "height", "tile", None)
    return jax.shard_map(
        functools.partial(local, *sides), mesh=mesh, in_specs=in_specs, out_specs=out_specs, check_vma=False
    )
```

```python
import functools

import jax
import jax.numpy as jnp
from jax import lax
from jax.experimental import pallas as pl
from jax.experimental.pallas import tpu as pltpu
from jax.sharding import PartitionSpec as P

PENALTY = 50.0
OMEGA = 0.6
COARSE_SWEEPS = 6
LANES = 128
HALO = 9
REACH = 16
SPARE = 4
F32 = jnp.float32


def each(start, stop, body, step):
    groups = (stop - start) // step

    def group(i, carry):
        for k in range(step):
            body(start + i * step + k, 0)
        return carry

    if groups > 1:
        lax.fori_loop(0, groups, group, 0)
    elif groups == 1:
        group(0, 0)
    for layer in range(start + groups * step, stop):
        body(layer, 0)


def chunks(start, stop, size):
    return [(row, min(size, stop - row)) for row in range(start, stop, size)]


def lane_of(rows):
    return lax.broadcasted_iota(jnp.int32, (rows, LANES), 1)


def roll(x, shift):
    return pltpu.roll(x, shift % LANES, 1)


def rows_at(ref, layer, row, count):
    return ref[layer, pl.ds(row, count), :]


def cross_faces(s_ref, layer, row, count):
    here = rows_at(s_ref, layer, row, count)
    return here, [
        here + rows_at(s_ref, layer - 1, row, count),
        here + rows_at(s_ref, layer + 1, row, count),
        here + rows_at(s_ref, layer, row - 1, count),
        here + rows_at(s_ref, layer, row + 1, count),
    ]


def lane_faces(here, step):
    lane = lane_of(here.shape[0])
    first, last = lane < step, lane >= LANES - step
    low = here + jnp.where(first, 0.0, roll(here, step))
    high = here + jnp.where(last, 0.0, roll(here, -step))
    return low, high, jnp.where(first, 0.0, low), jnp.where(last, 0.0, high)


def neighbours(v_ref, faces, layer, row, count, step):
    here = rows_at(v_ref, layer, row, count)
    along = [
        faces[0] * rows_at(v_ref, layer - 1, row, count)
        + faces[1] * rows_at(v_ref, layer + 1, row, count),
        faces[2] * rows_at(v_ref, layer, row - 1, count)
        + faces[3] * rows_at(v_ref, layer, row + 1, count),
        faces[4] * roll(here, step) + faces[5] * roll(here, -step),
    ]
    return here, along


def total(along, component):
    return (along[0] + along[1] + along[2]) + along[component]


def safe_rate(here, doubled):
    return jnp.where(here > 0.0, OMEGA / doubled, 0.0)


def pair_lanes(x, step):
    upper = (lane_of(x.shape[0]) & step) != 0
    return x + jnp.where(upper, roll(x, step), roll(x, -step))


def pair_rows(ref, row, count):
    return ref[pl.ds(row, count, stride=2), :] + ref[pl.ds(row + 1, count, stride=2), :]


def spread_rows(ref, x):
    count = x.shape[0]
    ref[pl.ds(0, count, stride=2), :] = x
    ref[pl.ds(1, count, stride=2), :] = x


def level_setup(s_ref, p_ref, r_ref, d_ref, g_ref, y_ref, b_of, layer, row, count, step):
    here, cross = cross_faces(s_ref, layer, row, count)
    low, high, low_in, high_in = lane_faces(here, step)
    y_ref[0, layer, pl.ds(row, count), :] = low_in
    y_ref[1, layer, pl.ds(row, count), :] = high_in
    sums = [cross[0] + cross[1], cross[2] + cross[3], low + high]
    base = rows_at(p_ref, layer, row, count) + (sums[0] + sums[1] + sums[2])
    for c in range(3):
        doubled = base + sums[c]
        rate = safe_rate(here, doubled)
        d_ref[c, layer, pl.ds(row, count), :] = doubled
        r_ref[c, layer, pl.ds(row, count), :] = rate
        g_ref[c, layer, pl.ds(row, count), :] = (2.0 * rate) * b_of(c)


def all_faces(s_ref, y_ref, layer, row, count):
    _, cross = cross_faces(s_ref, layer, row, count)
    return cross + [
        y_ref[0, layer, pl.ds(row, count), :],
        y_ref[1, layer, pl.ds(row, count), :],
    ]


def first_sweep(s_ref, y_ref, r_ref, g_ref, v_ref, layer, row, count, step):
    faces = all_faces(s_ref, y_ref, layer, row, count)
    for c in range(3):
        here, along = neighbours(g_ref.at[c], faces, layer, row, count, step)
        rate = r_ref[c, layer, pl.ds(row, count), :]
        v_ref[c, layer, pl.ds(row, count), :] = (2.0 - OMEGA) * here + rate * total(along, c)


def remainder(s_ref, y_ref, b_ref, d_ref, v_ref, layer, row, count, step):
    faces = all_faces(s_ref, y_ref, layer, row, count)
    result = []
    for c in range(3):
        here, along = neighbours(v_ref.at[c], faces, layer, row, count, step)
        doubled = d_ref[c, layer, pl.ds(row, count), :]
        source = b_ref[c, layer, pl.ds(row, count), :]
        result.append(source + 0.5 * (total(along, c) - doubled * here))
    return result


def pack_kernel(
    bz, bx, material_ref, clamped_ref, table_ref, strain_ref, own_ref, near_ref, far_ref, label, joined, table, strain, sem
):
    copies = [
        pltpu.make_async_copy(material_ref, label, sem.at[0]),
        pltpu.make_async_copy(clamped_ref.at[pl.ds(0, 2)], joined, sem.at[1]),
        pltpu.make_async_copy(table_ref, table, sem.at[2]),
        pltpu.make_async_copy(strain_ref, strain, sem.at[3]),
    ]
    for copy in copies:
        copy.start()
    for copy in copies:
        copy.wait()
    odd = (lax.axis_index("tile") & 1) == 1
    for slot in range(bz + 2):
        src = label.at[slot] if slot < bz else joined.at[slot - bz]
        own_ref[pl.ds(slot * bx, bx), :] = src[...].astype(F32)
        first = src[pl.ds(0, HALO), :].astype(F32)
        last = src[pl.ds(bx - HALO, HALO), :].astype(F32)
        near_ref[pl.ds(slot * HALO, HALO), :] = jnp.where(odd, first, last)
        far_ref[pl.ds(slot * HALO, HALO), :] = jnp.where(odd, last, first)
    lane = lane_of(SPARE)
    row = jnp.zeros((SPARE, LANES), F32)
    for k in range(3):
        row = jnp.where(lane == k, table[k], row)
        for c in range(3):
            row = jnp.where(lane == 3 + 3 * c + k, table[k] * strain[k, c], row)
    own_ref[pl.ds((bz + 2) * bx, SPARE), :] = row


def down_kernel(
    heights, tiles, bz, bx,
    x_ref,
    send_ref, s0_out, y0_out, v0_out, g0_out, r0_out, s1_out, y1_out, v1_out, g1_out, r1_out,
    s, p, st, b, r, d, g, y, v, tmp, s1, p1, b1, r1, d1, g1, y1, v1, sem,
):
    h, t = lax.axis_index("height"), lax.axis_index("tile")
    nz, n1 = bz + 2 * HALO, bz // 2 + 8
    bx1, bx2 = bx // 2, bx // 4
    low, high = 8, bx + 24
    own_rows, halo_rows = (bz + 2) * bx + SPARE, (bz + 2) * HALO
    low_rows = own_rows + jnp.where((t & 1) == 1, 0, halo_rows)
    high_rows = own_rows + jnp.where((t & 1) == 1, halo_rows, 0)
    spare = x_ref[0, pl.ds(own_rows - SPARE, 1), :]
    table = [jnp.broadcast_to(spare[:, k : k + 1], (1, LANES)) for k in range(12)]
    strain = [table[3 + 3 * c : 6 + 3 * c] for c in range(3)]
    before = jnp.where(t > 0, 1.0, 0.0)
    behind = jnp.where(t < tiles - 1, 1.0, 0.0)

    def read_layer(layer, carry):
        z = bz * h - HALO + layer
        inside = jnp.where((z >= 0) & (z < heights * bz), 1.0, 0.0)
        bottom = jnp.where((z >= 0) & (z < 2), 2.0 * PENALTY, 0.0)
        z_in = jnp.clip(z, 0, heights * bz - 1)
        brick, slot = z_in // bz, z_in % bz
        clamp_slot = bz + jnp.clip(z, 0, 1)
        parts = [
            (slot * bx, clamp_slot * bx, bx, 16, 1.0),
            (low_rows + slot * HALO, low_rows + clamp_slot * HALO, HALO, 16 - HALO, before),
            (high_rows + slot * HALO, high_rows + clamp_slot * HALO, HALO, 16 + bx, behind),
        ]
        for at, clamp_at, count, to, valid in parts:
            label = x_ref[brick, pl.ds(at, count), :]
            is0, is1 = label == 0.0, label == 1.0
            weight = inside * valid
            stiff = [table[k] * weight for k in range(3)]
            dst = pl.ds(to, count)
            s[layer, dst, :] = jnp.where(is0, stiff[0], jnp.where(is1, stiff[1], stiff[2]))
            for c in range(3):
                e = [strain[c][k] * weight for k in range(3)]
                st[c, layer, dst, :] = jnp.where(is0, e[0], jnp.where(is1, e[1], e[2]))
            joined = x_ref[0, pl.ds(clamp_at, count), :]
            p[layer, dst, :] = joined * (bottom * valid)
        return carry

    each(0, nz, read_layer, 8)

    def setup0(layer, carry):
        for row, count in chunks(low, high, 16):
            lane = lane_of(count)
            here = st[2, layer, pl.ds(row, count), :]
            source = [
                0.5 * (rows_at(st.at[0], layer - 1, row, count) - rows_at(st.at[0], layer + 1, row, count)),
                0.5 * (rows_at(st.at[1], layer, row - 1, count) - rows_at(st.at[1], layer, row + 1, count)),
                0.5 * (jnp.where(lane < 1, 0.0, roll(here, 1)) - jnp.where(lane >= LANES - 1, 0.0, roll(here, -1))),
            ]
            for c in range(3):
                b[c, layer, pl.ds(row, count), :] = source[c]
            level_setup(s, p, r, d, g, y, lambda c: source[c], layer, row, count, 1)
        return carry

    each(1, nz - 1, setup0, 8)

    def sweep0(layer, carry):
        for row, count in chunks(low, high, 16):
            first_sweep(s, y, r, g, v, layer, row, count, 1)
        return carry

    each(2, nz - 2, sweep0, 8)

    own = (pl.ds(HALO, bz), pl.ds(16, bx))
    near = (pl.ds(HALO - 1, bz + 2), pl.ds(low, bx + 16))
    copies = [
        (s.at[near[0], near[1]], s0_out),
        (y.at[:, own[0], own[1]], y0_out),
        (v.at[:, near[0], near[1]], v0_out),
        (g.at[:, own[0], own[1]], g0_out),
        (r.at[:, own[0], own[1]], r0_out),
    ]
    started = []
    for k, (src, dst) in enumerate(copies):
        started.append(pltpu.make_async_copy(src, dst, sem.at[k]))
        started[-1].start()

    rows1 = bx1 + 8

    def restrict0(j, carry):
        layer = 3 + 2 * j
        for row, count in chunks(low, high, 16):
            one = remainder(s, y, b, d, v, layer, row, count, 1)
            two = remainder(s, y, b, d, v, layer + 1, row, count, 1)
            for c in range(3):
                tmp[j, c, pl.ds(row, count), :] = one[c] + two[c]
        for c in range(3):
            b1[c, j + 1, pl.ds(8, rows1), :] = pair_lanes(pair_rows(tmp.at[j, c], low, rows1), 1)
        return carry

    each(0, n1 - 2, restrict0, 8)

    def coarse0(k, carry):
        for field, scale, into in ((s, 0.5, s1), (p, 1.0, p1)):
            both = [pair_rows(field.at[1 + 2 * k + i], low, rows1) for i in range(2)]
            into[k, pl.ds(8, rows1), :] = scale * pair_lanes(both[0] + both[1], 1)
        return carry

    each(0, n1, coarse0, 8)

    def setup1(layer, carry):
        level_setup(
            s1, p1, r1, d1, g1, y1,
            lambda c: b1[c, layer, pl.ds(8, rows1), :], layer, 8, rows1, 2,
        )
        return carry

    each(1, n1 - 1, setup1, 8)

    def sweep1(layer, carry):
        first_sweep(s1, y1, r1, g1, v1, layer, 8, rows1, 2)
        return carry

    each(2, n1 - 2, sweep1, 8)

    copies = [
        (s1.at[pl.ds(2, n1 - 4), pl.ds(8, rows1)], s1_out),
        (y1.at[:, pl.ds(3, n1 - 6), pl.ds(8, rows1)], y1_out),
        (v1.at[:, pl.ds(2, n1 - 4), pl.ds(8, rows1)], v1_out),
        (g1.at[:, pl.ds(3, n1 - 6), pl.ds(8, rows1)], g1_out),
        (r1.at[:, pl.ds(3, n1 - 6), pl.ds(8, rows1)], r1_out),
    ]
    for k, (src, dst) in enumerate(copies):
        started.append(pltpu.make_async_copy(src, dst, sem.at[5 + k]))
        started[-1].start()

    lane = lane_of(bx2) & 3
    packed = []
    for m in range(bz // 4):
        layer = 4 + 2 * m
        one = remainder(s1, y1, b1, d1, v1, layer, 8, rows1, 2)
        two = remainder(s1, y1, b1, d1, v1, layer + 1, 8, rows1, 2)
        fields = []
        for c in range(3):
            tmp[m, c, pl.ds(0, rows1), :] = one[c] + two[c]
            fields.append(pair_lanes(pair_rows(tmp.at[m, c], 4, bx2), 2))
        both = [pair_rows(s1.at[layer + i], 12, bx2) for i in range(2)]
        stiff = 0.5 * pair_lanes(both[0] + both[1], 2)
        packed.append(
            jnp.where(lane == 0, fields[0], jnp.where(lane == 1, fields[1], jnp.where(lane == 2, fields[2], stiff)))
        )
    both = [pair_rows(p1.at[4 + i], 12, bx2) for i in range(2)]
    tmp[2, 0, pl.ds(0, bx2), :] = pair_lanes(both[0] + both[1], 2)
    quarter = bx2 // 4
    part = [tmp[2, 0, pl.ds(j, quarter, stride=4), :] for j in range(4)]
    lane = lane_of(quarter) & 3
    packed.append(jnp.where(lane == 0, part[0], jnp.where(lane == 1, part[1], jnp.where(lane == 2, part[2], part[3]))))

    def fill(i, carry):
        for m, value in enumerate(packed):
            for k in range(value.shape[0] // 2):
                send_ref[i, m * bx2 // 2 + k, :, :] = value[2 * k : 2 * k + 2]
        return carry

    each(0, heights * tiles, fill, 8)
    for copy in started:
        copy.wait()


def up_kernel(
    heights, tiles, bz, bx,
    recv_ref, s0_in, y0_in, v0_in, g0_in, r0_in, s1_in, y1_in, v1_in, g1_in, r1_in,
    out_ref,
    s0, y0, v0, g0, r0, s1, y1, v1, g1, r1, f1, s2, p2, b2, q2, r2, d2, g2, v2, f2, s3, p3, b3, q3, r3, g3, va, vb, rest2, tmp, sem,
):
    h, t = lax.axis_index("height"), lax.axis_index("tile")
    bx1, bx2, bz2 = bx // 2, bx // 4, bz // 4
    n1, n2, n3 = bz // 2 + 4, heights * bz // 4, heights * bz // 8
    rows1 = bx1 + 8
    near = pl.ds(8, bx + 16)
    own = pl.ds(16, bx)
    mid = pl.ds(8, rows1)
    copies = [
        (s1_in, s1.at[:, mid]), (y1_in, y1.at[:, pl.ds(1, n1 - 2), mid]), (v1_in, v1.at[:, :, mid]),
        (g1_in, g1.at[:, pl.ds(1, n1 - 2), mid]), (r1_in, r1.at[:, pl.ds(1, n1 - 2), mid]),
        (s0_in, s0.at[:, near]), (y0_in, y0.at[:, pl.ds(1, bz), own]), (v0_in, v0.at[:, :, near]),
        (g0_in, g0.at[:, pl.ds(1, bz), own]), (r0_in, r0.at[:, pl.ds(1, bz), own]),
    ]
    started = []
    for k, (src, dst) in enumerate(copies):
        started.append(pltpu.make_async_copy(src, dst, sem.at[k]))
        started[-1].start()

    for ref in (s2, p2, g2, v2, f2, s3, p3, g3, va, vb):
        ref[...] = jnp.zeros(ref.shape, F32)
    rest2[...] = jnp.zeros(rest2.shape, F32)

    side = REACH // bx2
    lane = lane_of(bx2) & 3
    for dt in range(-side, side + 1):
        other = t + dt
        valid = (other >= 0) & (other < tiles)
        other = jnp.clip(other, 0, tiles - 1)
        scale = jnp.where(valid, 1.0, 0.0)
        dst = pl.ds(8 + (dt + side) * bx2, bx2)
        for hh in range(heights):
            for m in range(bz2):
                x = recv_ref[other * heights + hh, pl.ds(m * bx2 // 2, bx2 // 2)].reshape(bx2, LANES) * scale
                layer = 1 + hh * bz2 + m
                b2[layer, dst, :] = jnp.where(lane == 3, 0.0, x)
                s2[layer, dst, :] = jnp.where(
                    lane == 3, x, jnp.where(lane == 2, roll(x, -1), jnp.where(lane == 1, roll(x, -2), roll(x, -3)))
                )
        quarter = bx2 // 4
        x = recv_ref[other * heights, pl.ds(bz2 * bx2 // 2, quarter // 2)].reshape(quarter, LANES) * scale
        moved = {shift: roll(x, shift) if shift else x for shift in range(-3, 4)}
        small = lane_of(quarter) & 3
        for j in range(4):
            p2[1, pl.ds(8 + (dt + side) * bx2 + j, quarter, stride=4), :] = jnp.where(
                small == 0, moved[-j], jnp.where(small == 1, moved[1 - j], jnp.where(small == 2, moved[2 - j], moved[3 - j]))
            )

    def weights(count):
        kind = lane_of(count) & 3
        return [jnp.where(kind == c, 2.0, 1.0) for c in range(3)]

    def setup(s_ref, p_ref, b_ref, q_ref, r_ref, d_ref, g_ref, layer, row, count, step):
        here, cross = cross_faces(s_ref, layer, row, count)
        low, high, low_in, high_in = lane_faces(here, step)
        w = weights(count)
        dst = pl.ds(row, count)
        for k in range(4):
            q_ref[k, layer, dst, :] = w[k // 2] * cross[k]
        q_ref[4, layer, dst, :] = w[2] * low_in
        q_ref[5, layer, dst, :] = w[2] * high_in
        doubled = rows_at(p_ref, layer, row, count) + (
            w[0] * (cross[0] + cross[1]) + w[1] * (cross[2] + cross[3]) + w[2] * (low + high)
        )
        rate = safe_rate(here, doubled)
        r_ref[layer, dst, :] = rate
        if d_ref is not None:
            d_ref[layer, dst, :] = doubled
        g_ref[layer, dst, :] = (2.0 * rate) * rows_at(b_ref, layer, row, count)

    def packed_sum(v_ref, q_ref, layer, row, count, step):
        faces = [q_ref[k, layer, pl.ds(row, count), :] for k in range(6)]
        here, along = neighbours(v_ref, faces, layer, row, count, step)
        return here, along[0] + along[1] + along[2]

    rows2 = bx2 + 2 * REACH

    def setup2(layer, carry):
        setup(s2, p2, b2, q2, r2, d2, g2, layer, 8, rows2, 4)
        return carry

    each(1, n2 + 1, setup2, 8)

    def sweep2(layer, carry):
        here, total_ = packed_sum(g2, q2, layer, 8, rows2, 4)
        v2[layer, pl.ds(8, rows2), :] = (2.0 - OMEGA) * here + rows_at(r2, layer, 8, rows2) * total_
        return carry

    each(1, n2 + 1, sweep2, 8)

    rows3 = -(-(rows2 // 2) // 8) * 8

    def restrict2(j, carry):
        rest = 0.0
        for i in range(2):
            layer = 1 + 2 * j + i
            here, total_ = packed_sum(v2, q2, layer, 8, rows2, 4)
            rest = rest + rows_at(b2, layer, 8, rows2) + 0.5 * (total_ - rows_at(d2, layer, 8, rows2) * here)
        rest2[j, pl.ds(8, rows2), :] = rest
        dst = pl.ds(8, rows3)
        b3[j + 1, dst, :] = pair_lanes(pair_rows(rest2.at[j], 8, rows3), 4)
        for field, scale, into in ((s2, 0.5, s3), (p2, 1.0, p3)):
            both = [pair_rows(field.at[1 + 2 * j + i], 8, rows3) for i in range(2)]
            into[j + 1, dst, :] = scale * pair_lanes(both[0] + both[1], 4)
        return carry

    each(0, n3, restrict2, 8)

    for layer in range(1, n3 + 1):
        setup(s3, p3, b3, q3, r3, None, g3, layer, 8, rows3, 8)
    source, target = g3, va
    for _ in range(COARSE_SWEEPS - 1):
        for layer in range(1, n3 + 1):
            here, total_ = packed_sum(source, q3, layer, 8, rows3, 8)
            target[layer, pl.ds(8, rows3), :] = (
                (1.0 - OMEGA) * here + rows_at(g3, layer, 8, rows3) + rows_at(r3, layer, 8, rows3) * total_
            )
        source, target = target, (vb if target is va else va)
    coarse = source

    wide2 = bx2 + 16

    def lift2(layer, carry):
        spread_rows(tmp.at[layer - 1], coarse[(layer + 1) // 2, pl.ds(12, wide2 // 2), :])
        v2[layer, pl.ds(16, wide2), :] += tmp[layer - 1, pl.ds(0, wide2), :]
        return carry

    each(1, n2 + 1, lift2, 8)

    def post2(layer, carry):
        here, total_ = packed_sum(v2, q2, layer, 16, wide2, 4)
        f2[layer, pl.ds(16, wide2), :] = (
            (1.0 - OMEGA) * here + rows_at(g2, layer, 16, wide2) + rows_at(r2, layer, 16, wide2) * total_
        )
        return carry

    each(1, n2 + 1, post2, 8)

    for copy in started[:5]:
        copy.wait()
    kind = lane_of(bx2 + 4) & 3

    def lift1(m, carry):
        x = f2[bz2 * h + m, pl.ds(22, bx2 + 4), :]
        moved = {shift: roll(x, shift) if shift else x for shift in range(-2, 4)}
        for c in range(3):
            part = jnp.where(
                kind == 0, moved[-c], jnp.where(kind == 1, moved[1 - c], jnp.where(kind == 2, moved[2 - c], moved[3 - c]))
            )
            spread_rows(tmp.at[3 * m + c], part)
            lifted = tmp[3 * m + c, pl.ds(0, rows1), :]
            for i in range(2):
                v1[c, 2 * m + i, mid, :] += lifted
        return carry

    each(0, n1 // 2, lift1, 8)

    def post(s_ref, y_ref, g_ref, r_ref, v_ref, into, layer, to, row, count, step):
        faces = all_faces(s_ref, y_ref, layer, row, count)
        for c in range(3):
            here, along = neighbours(v_ref.at[c], faces, layer, row, count, step)
            dst = pl.ds(row, count)
            into(c, (1.0 - OMEGA) * here + g_ref[c, layer, dst, :] + r_ref[c, layer, dst, :] * total(along, c))

    def post1(layer, carry):
        def into(c, value):
            f1[c, layer, mid, :] = value

        post(s1, y1, g1, r1, v1, into, layer, layer, 8, rows1, 2)
        return carry

    each(1, n1 - 1, post1, 8)

    for copy in started[5:]:
        copy.wait()

    for c in range(3):
        for k in range(1, n1 - 1):
            slot = 3 * (k - 1) + c
            spread_rows(tmp.at[slot], f1[c, k, mid, :])
            lifted = tmp[slot, pl.ds(0, bx + 16), :]
            for i in (2 * k - 3, 2 * k - 2):
                if 0 <= i < bz + 2:
                    v0[c, i, near, :] += lifted

    def post0(layer, carry):
        for row, count in chunks(16, 16 + bx, 16):

            def into(c, value):
                out_ref[c, layer - 1, pl.ds(row - 16, count), :] = value

            post(s0, y0, g0, r0, v0, into, layer, layer, row, count, 1)
        return carry

    each(1, bz + 1, post0, 8)


def swapped(x, axis, start):
    pairs = [(i, i + 1) for i in range(start, lax.axis_size(axis) - 1, 2)]
    return lax.ppermute(x, axis, pairs + [(j, i) for i, j in pairs])


def vmem(*shape):
    return pltpu.VMEM(shape, F32)


def local(heights, tiles, material, clamped, stiffness_table, eigenstrain):
    bz, bx, _ = material.shape

    held = pl.BlockSpec(memory_space=pltpu.VMEM)
    anywhere = pl.BlockSpec(memory_space=pl.ANY)
    outside = pl.BlockSpec(memory_space=pltpu.HBM)
    slots = bz + 2
    own, near, far = pl.pallas_call(
        functools.partial(pack_kernel, bz, bx),
        out_shape=[
            pltpu.VMEM((rows, LANES), F32)
            for rows in (slots * bx + SPARE, slots * HALO, slots * HALO)
        ],
        in_specs=[outside] * 4,
        out_specs=[held] * 3,
        scratch_shapes=[
            pltpu.VMEM((bz, bx, LANES), jnp.int32), pltpu.VMEM((2, bx, LANES), jnp.int32),
            pltpu.SMEM((3,), F32), pltpu.SMEM((3, 3), F32), pltpu.SemaphoreType.DMA((4,)),
        ],
    )(material, clamped, stiffness_table, eigenstrain)
    far = swapped(far, "tile", 1)
    near = swapped(near, "tile", 0)
    bricks = lax.all_gather(jnp.concatenate([own, near, far], 0), "height")

    bx1, bx2 = bx // 2, bx // 4
    nz, n1 = bz + 2 * HALO, bz // 2 + 8
    r0, r1 = bx + 32, bx1 + 24
    rows1 = bx1 + 8
    kept = [
        (bz + 2, bx + 16), (2, bz, bx), (3, bz + 2, bx + 16), (3, bz, bx), (3, bz, bx),
        (n1 - 4, rows1), (2, n1 - 6, rows1), (3, n1 - 4, rows1), (3, n1 - 6, rows1), (3, n1 - 6, rows1),
    ]
    kept = [jax.ShapeDtypeStruct((*shape, LANES), F32) for shape in kept]
    field0, field1 = (nz, r0, LANES), (n1, r1, LANES)
    send, *saved = pl.pallas_call(
        functools.partial(down_kernel, heights, tiles, bz, bx),
        out_shape=[jax.ShapeDtypeStruct((heights * tiles, (bz // 4 * bx2 + bx2 // 4) // 2, 2, LANES), F32), *kept],
        in_specs=[held],
        out_specs=[held] + [anywhere] * len(kept),
        scratch_shapes=[
            vmem(*field0), vmem(*field0), vmem(3, *field0), vmem(3, *field0), vmem(3, *field0), vmem(3, *field0),
            vmem(3, *field0), vmem(2, *field0), vmem(3, *field0), vmem(n1 - 2, 3, r0, LANES),
            vmem(*field1), vmem(*field1), vmem(3, *field1), vmem(3, *field1), vmem(3, *field1), vmem(3, *field1),
            vmem(2, *field1), vmem(3, *field1), pltpu.SemaphoreType.DMA((10,)),
        ],
        compiler_params=pltpu.CompilerParams(vmem_limit_bytes=40 * 2**20),
    )(bricks)

    received = lax.all_to_all(send, ("tile", "height"), 0, 0)

    rows2 = bx2 + 2 * REACH
    rows3 = -(-(rows2 // 2) // 8) * 8
    up0, up1 = (bz + 2, r0, LANES), (n1 - 4, r1, LANES)
    up2 = (heights * bz // 4 + 2, rows2 + 16, LANES)
    up3 = (heights * bz // 8 + 2, rows3 + 16, LANES)
    return pl.pallas_call(
        functools.partial(up_kernel, heights, tiles, bz, bx),
        out_shape=jax.ShapeDtypeStruct((3, bz, bx, LANES), F32),
        in_specs=[held] + [anywhere] * len(kept),
        out_specs=held,
        scratch_shapes=[
            vmem(*up0), vmem(2, *up0), vmem(3, *up0), vmem(3, *up0), vmem(3, *up0),
            vmem(*up1), vmem(2, *up1), vmem(3, *up1), vmem(3, *up1), vmem(3, *up1), vmem(3, *up1),
            vmem(*up2), vmem(*up2), vmem(*up2), vmem(6, *up2), vmem(*up2), vmem(*up2), vmem(*up2), vmem(*up2), vmem(*up2),
            vmem(*up3), vmem(*up3), vmem(*up3), vmem(6, *up3), vmem(*up3), vmem(*up3), vmem(*up3), vmem(*up3),
            vmem(heights * bz // 8, rows2 + 24, LANES), vmem(max(heights * bz // 4, 3 * (n1 - 6)), r0, LANES), pltpu.SemaphoreType.DMA((10,)),
        ],
        compiler_params=pltpu.CompilerParams(vmem_limit_bytes=40 * 2**20),
    )(received, *saved)


def solution(mesh):
    sides = mesh.shape["height"], mesh.shape["tile"]
    in_specs = (P("height", "tile", None), P("height", "tile", None), P(), P())
    out_specs = P(None, "height", "tile", None)
    return jax.shard_map(
        functools.partial(local, *sides), mesh=mesh, in_specs=in_specs, out_specs=out_specs, check_vma=False
    )
```

```python
import functools

import jax
import jax.numpy as jnp
from jax import lax
from jax.experimental import pallas as pl
from jax.experimental.pallas import tpu as pltpu
from jax.sharding import PartitionSpec as P

PENALTY = 50.0
OMEGA = 0.6
COARSE_SWEEPS = 6
LANES = 128
HALO = 9
REACH = 16
SPARE = 4
F32 = jnp.float32


def each(start, stop, body, step):
    groups = (stop - start) // step

    def group(i, carry):
        for k in range(step):
            body(start + i * step + k, 0)
        return carry

    if groups > 1:
        lax.fori_loop(0, groups, group, 0)
    elif groups == 1:
        group(0, 0)
    for layer in range(start + groups * step, stop):
        body(layer, 0)


def chunks(start, stop, size):
    return [(row, min(size, stop - row)) for row in range(start, stop, size)]


def lane_of(rows):
    return lax.broadcasted_iota(jnp.int32, (rows, LANES), 1)


def roll(x, shift):
    return pltpu.roll(x, shift % LANES, 1)


def rows_at(ref, layer, row, count):
    return ref[layer, pl.ds(row, count), :]


def cross_faces(s_ref, layer, row, count):
    here = rows_at(s_ref, layer, row, count)
    return here, [
        here + rows_at(s_ref, layer - 1, row, count),
        here + rows_at(s_ref, layer + 1, row, count),
        here + rows_at(s_ref, layer, row - 1, count),
        here + rows_at(s_ref, layer, row + 1, count),
    ]


def lane_faces(here, step):
    lane = lane_of(here.shape[0])
    first, last = lane < step, lane >= LANES - step
    low = here + jnp.where(first, 0.0, roll(here, step))
    high = here + jnp.where(last, 0.0, roll(here, -step))
    return low, high, jnp.where(first, 0.0, low), jnp.where(last, 0.0, high)


def neighbours(v_ref, faces, layer, row, count, step):
    here = rows_at(v_ref, layer, row, count)
    along = [
        faces[0] * rows_at(v_ref, layer - 1, row, count)
        + faces[1] * rows_at(v_ref, layer + 1, row, count),
        faces[2] * rows_at(v_ref, layer, row - 1, count)
        + faces[3] * rows_at(v_ref, layer, row + 1, count),
        faces[4] * roll(here, step) + faces[5] * roll(here, -step),
    ]
    return here, along


def total(along, component):
    return (along[0] + along[1] + along[2]) + along[component]


def safe_rate(here, doubled):
    return jnp.where(here > 0.0, OMEGA / doubled, 0.0)


def pair_lanes(x, step):
    upper = (lane_of(x.shape[0]) & step) != 0
    return x + jnp.where(upper, roll(x, step), roll(x, -step))


def pair_rows(ref, row, count):
    return ref[pl.ds(row, count, stride=2), :] + ref[pl.ds(row + 1, count, stride=2), :]


def spread_rows(ref, x):
    count = x.shape[0]
    ref[pl.ds(0, count, stride=2), :] = x
    ref[pl.ds(1, count, stride=2), :] = x


def level_setup(s_ref, p_ref, r_ref, d_ref, g_ref, y_ref, b_of, layer, row, count, step):
    here, cross = cross_faces(s_ref, layer, row, count)
    low, high, low_in, high_in = lane_faces(here, step)
    y_ref[0, layer, pl.ds(row, count), :] = low_in
    y_ref[1, layer, pl.ds(row, count), :] = high_in
    sums = [cross[0] + cross[1], cross[2] + cross[3], low + high]
    base = rows_at(p_ref, layer, row, count) + (sums[0] + sums[1] + sums[2])
    for c in range(3):
        doubled = base + sums[c]
        rate = safe_rate(here, doubled)
        d_ref[c, layer, pl.ds(row, count), :] = doubled
        r_ref[c, layer, pl.ds(row, count), :] = rate
        g_ref[c, layer, pl.ds(row, count), :] = (2.0 * rate) * b_of(c)


def all_faces(s_ref, y_ref, layer, row, count):
    _, cross = cross_faces(s_ref, layer, row, count)
    return cross + [
        y_ref[0, layer, pl.ds(row, count), :],
        y_ref[1, layer, pl.ds(row, count), :],
    ]


def first_sweep(s_ref, y_ref, r_ref, g_ref, v_ref, layer, row, count, step):
    faces = all_faces(s_ref, y_ref, layer, row, count)
    for c in range(3):
        here, along = neighbours(g_ref.at[c], faces, layer, row, count, step)
        rate = r_ref[c, layer, pl.ds(row, count), :]
        v_ref[c, layer, pl.ds(row, count), :] = (2.0 - OMEGA) * here + rate * total(along, c)


def remainder(s_ref, y_ref, b_ref, d_ref, v_ref, layer, row, count, step):
    faces = all_faces(s_ref, y_ref, layer, row, count)
    result = []
    for c in range(3):
        here, along = neighbours(v_ref.at[c], faces, layer, row, count, step)
        doubled = d_ref[c, layer, pl.ds(row, count), :]
        source = b_ref[c, layer, pl.ds(row, count), :]
        result.append(source + 0.5 * (total(along, c) - doubled * here))
    return result


def strips(bz):
    counts = [min(layer, HALO, bz + 2 * HALO - 1 - layer) for layer in range(bz + 2 * HALO)]
    starts = [sum(counts[:layer]) for layer in range(len(counts))]
    return counts, starts, sum(counts)


def pack_kernel(bz, bx, material_ref, clamped_ref, table_ref, strain_ref, own_ref, label, joined, table, strain, sem):
    copies = [
        pltpu.make_async_copy(material_ref, label, sem.at[0]),
        pltpu.make_async_copy(clamped_ref.at[pl.ds(0, 2)], joined, sem.at[1]),
        pltpu.make_async_copy(table_ref, table, sem.at[2]),
        pltpu.make_async_copy(strain_ref, strain, sem.at[3]),
    ]
    for copy in copies:
        copy.start()
    for copy in copies:
        copy.wait()
    for slot in range(bz + 2):
        src = label.at[slot] if slot < bz else joined.at[slot - bz]
        own_ref[pl.ds(slot * bx, bx), :] = src[...].astype(F32)
    lane = lane_of(SPARE)
    row = jnp.zeros((SPARE, LANES), F32)
    for k in range(3):
        row = jnp.where(lane == k, table[k], row)
        for c in range(3):
            row = jnp.where(lane == 3 + 3 * c + k, table[k] * strain[k, c], row)
    own_ref[pl.ds((bz + 2) * bx, SPARE), :] = row


def place(heights, bz, layer):
    z = bz * lax.axis_index("height") - HALO + layer
    z_in = jnp.clip(z, 0, heights * bz - 1)
    return z, z_in // bz, z_in % bz


def strip_kernel(heights, bz, bx, x_ref, near_ref, far_ref):
    odd = (lax.axis_index("tile") & 1) == 1
    counts, starts, end = strips(bz)
    wanted = [(place(heights, bz, layer)[1:], count, start) for layer, (count, start) in enumerate(zip(counts, starts))]
    wanted += [((0, bz + k), HALO, end + HALO * k) for k in range(2)]
    for (brick, slot), count, start in wanted:
        if count:
            first = x_ref[brick, pl.ds(slot * bx, count), :]
            last = x_ref[brick, pl.ds(slot * bx + bx - count, count), :]
            near_ref[pl.ds(start, count), :] = jnp.where(odd, first, last)
            far_ref[pl.ds(start, count), :] = jnp.where(odd, last, first)


def tables_of(x_ref, row):
    spare = x_ref[0, pl.ds(row, 1), :]
    table = [jnp.broadcast_to(spare[:, k : k + 1], (1, LANES)) for k in range(12)]
    return table[:3], [table[3 + 3 * c : 6 + 3 * c] for c in range(3)]


def store_layer(s, st, label, layer, to, weight, tables):
    is0, is1 = label == 0.0, label == 1.0
    dst = pl.ds(to, label.shape[0])
    for ref, values in zip((s, *(st.at[c] for c in range(3))), (tables[0], *tables[1])):
        a, b, c = (value * weight for value in values)
        ref[layer, dst, :] = jnp.where(is0, a, jnp.where(is1, b, c))


def store_strip(s, st, p, strip_ref, heights, bz, layer, far_side, valid, bx, tables):
    counts, starts, end = strips(bz)
    z, _, _ = place(heights, bz, layer)
    weight = jnp.where((z >= 0) & (z < heights * bz), valid, 0.0)
    count = counts[layer]
    if count:
        to = jnp.where(far_side, 16 + bx, 16 - count)
        store_layer(s, st, strip_ref[pl.ds(starts[layer], count), :], layer, to, weight, tables)
    joined = strip_ref[pl.ds(end + HALO * jnp.clip(z, 0, 1), HALO), :]
    to = jnp.where(far_side, 16 + bx, 16 - HALO)
    p[layer, pl.ds(to, HALO), :] = joined * jnp.where((z >= 0) & (z < 2), 2.0 * PENALTY * valid, 0.0)


def fine_setup(s, p, st, b, r, d, g, y, layer, row, count):
    lane = lane_of(count)
    here = st[2, layer, pl.ds(row, count), :]
    source = [
        0.5 * (rows_at(st.at[0], layer - 1, row, count) - rows_at(st.at[0], layer + 1, row, count)),
        0.5 * (rows_at(st.at[1], layer, row - 1, count) - rows_at(st.at[1], layer, row + 1, count)),
        0.5 * (jnp.where(lane < 1, 0.0, roll(here, 1)) - jnp.where(lane >= LANES - 1, 0.0, roll(here, -1))),
    ]
    for c in range(3):
        b[c, layer, pl.ds(row, count), :] = source[c]
    level_setup(s, p, r, d, g, y, lambda c: source[c], layer, row, count, 1)


def fine_down(bz, s, p, st, b, r, d, g, y, v, rest, rows, step):
    nz = bz + 2 * HALO

    def setup0(layer, carry):
        for row in rows[0]:
            fine_setup(s, p, st, b, r, d, g, y, layer, row, 16)
        return carry

    def sweep0(layer, carry):
        for row in rows[1]:
            first_sweep(s, y, r, g, v, layer, row, 16, 1)
        return carry

    def restrict0(j, carry):
        layer = 3 + 2 * j
        for row in rows[2]:
            one = remainder(s, y, b, d, v, layer, row, 16, 1)
            two = remainder(s, y, b, d, v, layer + 1, row, 16, 1)
            for c in range(3):
                rest[j, c, pl.ds(row, 16), :] = one[c] + two[c]
        return carry

    each(1, nz - 1, setup0, step)
    each(2, nz - 2, sweep0, step)
    each(0, bz // 2 + 6, restrict0, step)


def inner_kernel(heights, tiles, bz, bx, x_ref, near_ref, s, p, st, b, r, d, g, y, v, rest):
    t = lax.axis_index("tile")
    odd = (t & 1) == 1
    tables = tables_of(x_ref, (bz + 2) * bx)
    valid = jnp.where(odd | (t < tiles - 1), 1.0, 0.0)

    def read_layer(layer, carry):
        z, brick, slot = place(heights, bz, layer)
        inside = jnp.where((z >= 0) & (z < heights * bz), 1.0, 0.0)
        store_layer(s, st, x_ref[brick, pl.ds(slot * bx, bx), :], layer, 16, inside, tables)
        bottom = jnp.where((z >= 0) & (z < 2), 2.0 * PENALTY, 0.0)
        p[layer, pl.ds(16, bx), :] = x_ref[0, pl.ds((bz + jnp.clip(z, 0, 1)) * bx, bx), :] * bottom
        store_strip(s, st, p, near_ref, heights, bz, layer, jnp.logical_not(odd), valid, bx, tables)
        return carry

    each(0, bz + 2 * HALO, read_layer, bz + 2 * HALO + 1)
    rows = [[jnp.where(odd, 8 - k, 24 + k) + at for at in range(0, bx, 16)] for k in range(3)]
    fine_down(bz, s, p, st, b, r, d, g, y, v, rest, rows, 8)


def down_kernel(
    heights, tiles, bz, bx,
    x_ref, far_ref, *refs,
):
    (
        send_ref, s0_out, y0_out, v0_out, g0_out, r0_out, s1_out, y1_out, v1_out, g1_out, r1_out,
        s, p, st, b, r, d, g, y, v, rest, tmp, s1, p1, b1, r1, d1, g1, y1, v1, sem,
    ) = refs[10:]
    t = lax.axis_index("tile")
    odd = (t & 1) == 1
    n1 = bz // 2 + 8
    bx1, bx2 = bx // 2, bx // 4
    low = 8
    tables = tables_of(x_ref, (bz + 2) * bx)
    valid = jnp.where(jnp.where(odd, t < tiles - 1, t > 0), 1.0, 0.0)

    def read_layer(layer, carry):
        store_strip(s, st, p, far_ref, heights, bz, layer, odd, valid, bx, tables)
        return carry

    each(0, bz + 2 * HALO, read_layer, bz + 2 * HALO + 1)
    rows = [[jnp.where(odd, bx + 8 - k, 8 + k)] for k in range(3)]
    fine_down(bz, s, p, st, b, r, d, g, y, v, rest, rows, 24)

    own = (pl.ds(HALO, bz), pl.ds(16, bx))
    near = (pl.ds(HALO - 1, bz + 2), pl.ds(low, bx + 16))
    copies = [
        (s.at[near[0], near[1]], s0_out),
        (y.at[:, own[0], own[1]], y0_out),
        (v.at[:, near[0], near[1]], v0_out),
        (g.at[:, own[0], own[1]], g0_out),
        (r.at[:, own[0], own[1]], r0_out),
    ]
    started = []
    for k, (src, dst) in enumerate(copies):
        started.append(pltpu.make_async_copy(src, dst, sem.at[k]))
        started[-1].start()

    rows1 = bx1 + 8

    def restrict0(j, carry):
        for c in range(3):
            b1[c, j + 1, pl.ds(8, rows1), :] = pair_lanes(pair_rows(rest.at[j, c], low, rows1), 1)
        return carry

    each(0, n1 - 2, restrict0, 8)

    def coarse0(k, carry):
        for field, scale, into in ((s, 0.5, s1), (p, 1.0, p1)):
            both = [pair_rows(field.at[1 + 2 * k + i], low, rows1) for i in range(2)]
            into[k, pl.ds(8, rows1), :] = scale * pair_lanes(both[0] + both[1], 1)
        return carry

    each(0, n1, coarse0, 8)

    def setup1(layer, carry):
        level_setup(
            s1, p1, r1, d1, g1, y1,
            lambda c: b1[c, layer, pl.ds(8, rows1), :], layer, 8, rows1, 2,
        )
        return carry

    each(1, n1 - 1, setup1, 8)

    def sweep1(layer, carry):
        first_sweep(s1, y1, r1, g1, v1, layer, 8, rows1, 2)
        return carry

    each(2, n1 - 2, sweep1, 8)

    copies = [
        (s1.at[pl.ds(2, n1 - 4), pl.ds(8, rows1)], s1_out),
        (y1.at[:, pl.ds(3, n1 - 6), pl.ds(8, rows1)], y1_out),
        (v1.at[:, pl.ds(2, n1 - 4), pl.ds(8, rows1)], v1_out),
        (g1.at[:, pl.ds(3, n1 - 6), pl.ds(8, rows1)], g1_out),
        (r1.at[:, pl.ds(3, n1 - 6), pl.ds(8, rows1)], r1_out),
    ]
    for k, (src, dst) in enumerate(copies):
        started.append(pltpu.make_async_copy(src, dst, sem.at[5 + k]))
        started[-1].start()

    lane = lane_of(bx2) & 3
    packed = []
    for m in range(bz // 4):
        layer = 4 + 2 * m
        one = remainder(s1, y1, b1, d1, v1, layer, 8, rows1, 2)
        two = remainder(s1, y1, b1, d1, v1, layer + 1, 8, rows1, 2)
        fields = []
        for c in range(3):
            tmp[m, c, pl.ds(0, rows1), :] = one[c] + two[c]
            fields.append(pair_lanes(pair_rows(tmp.at[m, c], 4, bx2), 2))
        both = [pair_rows(s1.at[layer + i], 12, bx2) for i in range(2)]
        stiff = 0.5 * pair_lanes(both[0] + both[1], 2)
        packed.append(
            jnp.where(lane == 0, fields[0], jnp.where(lane == 1, fields[1], jnp.where(lane == 2, fields[2], stiff)))
        )
    both = [pair_rows(p1.at[4 + i], 12, bx2) for i in range(2)]
    tmp[2, 0, pl.ds(0, bx2), :] = pair_lanes(both[0] + both[1], 2)
    quarter = bx2 // 4
    part = [tmp[2, 0, pl.ds(j, quarter, stride=4), :] for j in range(4)]
    lane = lane_of(quarter) & 3
    packed.append(jnp.where(lane == 0, part[0], jnp.where(lane == 1, part[1], jnp.where(lane == 2, part[2], part[3]))))

    def fill(i, carry):
        for m, value in enumerate(packed):
            for k in range(value.shape[0] // 2):
                send_ref[i, m * bx2 // 2 + k, :, :] = value[2 * k : 2 * k + 2]
        return carry

    each(0, heights * tiles, fill, 8)
    for copy in started:
        copy.wait()


def up_kernel(
    heights, tiles, bz, bx,
    recv_ref, s0_in, y0_in, v0_in, g0_in, r0_in, s1_in, y1_in, v1_in, g1_in, r1_in,
    out_ref,
    s0, y0, v0, g0, r0, s1, y1, v1, g1, r1, f1, s2, p2, b2, q2, r2, d2, g2, v2, f2, s3, p3, b3, q3, r3, g3, va, vb, rest2, tmp, sem,
):
    h, t = lax.axis_index("height"), lax.axis_index("tile")
    bx1, bx2, bz2 = bx // 2, bx // 4, bz // 4
    n1, n2, n3 = bz // 2 + 4, heights * bz // 4, heights * bz // 8
    rows1 = bx1 + 8
    near = pl.ds(8, bx + 16)
    own = pl.ds(16, bx)
    mid = pl.ds(8, rows1)
    copies = [
        (s1_in, s1.at[:, mid]), (y1_in, y1.at[:, pl.ds(1, n1 - 2), mid]), (v1_in, v1.at[:, :, mid]),
        (g1_in, g1.at[:, pl.ds(1, n1 - 2), mid]), (r1_in, r1.at[:, pl.ds(1, n1 - 2), mid]),
        (s0_in, s0.at[:, near]), (y0_in, y0.at[:, pl.ds(1, bz), own]), (v0_in, v0.at[:, :, near]),
        (g0_in, g0.at[:, pl.ds(1, bz), own]), (r0_in, r0.at[:, pl.ds(1, bz), own]),
    ]
    started = []
    for k, (src, dst) in enumerate(copies):
        started.append(pltpu.make_async_copy(src, dst, sem.at[k]))
        started[-1].start()

    for ref in (s2, p2, g2, v2, f2, s3, p3, g3, va, vb):
        ref[...] = jnp.zeros(ref.shape, F32)
    rest2[...] = jnp.zeros(rest2.shape, F32)

    side = REACH // bx2
    lane = lane_of(bx2) & 3
    for dt in range(-side, side + 1):
        other = t + dt
        valid = (other >= 0) & (other < tiles)
        other = jnp.clip(other, 0, tiles - 1)
        scale = jnp.where(valid, 1.0, 0.0)
        dst = pl.ds(8 + (dt + side) * bx2, bx2)
        for hh in range(heights):
            for m in range(bz2):
                x = recv_ref[other * heights + hh, pl.ds(m * bx2 // 2, bx2 // 2)].reshape(bx2, LANES) * scale
                layer = 1 + hh * bz2 + m
                b2[layer, dst, :] = jnp.where(lane == 3, 0.0, x)
                s2[layer, dst, :] = jnp.where(
                    lane == 3, x, jnp.where(lane == 2, roll(x, -1), jnp.where(lane == 1, roll(x, -2), roll(x, -3)))
                )
        quarter = bx2 // 4
        x = recv_ref[other * heights, pl.ds(bz2 * bx2 // 2, quarter // 2)].reshape(quarter, LANES) * scale
        moved = {shift: roll(x, shift) if shift else x for shift in range(-3, 4)}
        small = lane_of(quarter) & 3
        for j in range(4):
            p2[1, pl.ds(8 + (dt + side) * bx2 + j, quarter, stride=4), :] = jnp.where(
                small == 0, moved[-j], jnp.where(small == 1, moved[1 - j], jnp.where(small == 2, moved[2 - j], moved[3 - j]))
            )

    def weights(count):
        kind = lane_of(count) & 3
        return [jnp.where(kind == c, 2.0, 1.0) for c in range(3)]

    def setup(s_ref, p_ref, b_ref, q_ref, r_ref, d_ref, g_ref, layer, row, count, step):
        here, cross = cross_faces(s_ref, layer, row, count)
        low, high, low_in, high_in = lane_faces(here, step)
        w = weights(count)
        dst = pl.ds(row, count)
        for k in range(4):
            q_ref[k, layer, dst, :] = w[k // 2] * cross[k]
        q_ref[4, layer, dst, :] = w[2] * low_in
        q_ref[5, layer, dst, :] = w[2] * high_in
        doubled = rows_at(p_ref, layer, row, count) + (
            w[0] * (cross[0] + cross[1]) + w[1] * (cross[2] + cross[3]) + w[2] * (low + high)
        )
        rate = safe_rate(here, doubled)
        r_ref[layer, dst, :] = rate
        if d_ref is not None:
            d_ref[layer, dst, :] = doubled
        g_ref[layer, dst, :] = (2.0 * rate) * rows_at(b_ref, layer, row, count)

    def packed_sum(v_ref, q_ref, layer, row, count, step):
        faces = [q_ref[k, layer, pl.ds(row, count), :] for k in range(6)]
        here, along = neighbours(v_ref, faces, layer, row, count, step)
        return here, along[0] + along[1] + along[2]

    rows2 = bx2 + 2 * REACH

    def setup2(layer, carry):
        setup(s2, p2, b2, q2, r2, d2, g2, layer, 8, rows2, 4)
        return carry

    each(1, n2 + 1, setup2, 8)

    def sweep2(layer, carry):
        here, total_ = packed_sum(g2, q2, layer, 8, rows2, 4)
        v2[layer, pl.ds(8, rows2), :] = (2.0 - OMEGA) * here + rows_at(r2, layer, 8, rows2) * total_
        return carry

    each(1, n2 + 1, sweep2, 8)

    rows3 = -(-(rows2 // 2) // 8) * 8

    def restrict2(j, carry):
        rest = 0.0
        for i in range(2):
            layer = 1 + 2 * j + i
            here, total_ = packed_sum(v2, q2, layer, 8, rows2, 4)
            rest = rest + rows_at(b2, layer, 8, rows2) + 0.5 * (total_ - rows_at(d2, layer, 8, rows2) * here)
        rest2[j, pl.ds(8, rows2), :] = rest
        dst = pl.ds(8, rows3)
        b3[j + 1, dst, :] = pair_lanes(pair_rows(rest2.at[j], 8, rows3), 4)
        for field, scale, into in ((s2, 0.5, s3), (p2, 1.0, p3)):
            both = [pair_rows(field.at[1 + 2 * j + i], 8, rows3) for i in range(2)]
            into[j + 1, dst, :] = scale * pair_lanes(both[0] + both[1], 4)
        return carry

    each(0, n3, restrict2, 8)

    for layer in range(1, n3 + 1):
        setup(s3, p3, b3, q3, r3, None, g3, layer, 8, rows3, 8)
    source, target = g3, va
    for _ in range(COARSE_SWEEPS - 1):
        for layer in range(1, n3 + 1):
            here, total_ = packed_sum(source, q3, layer, 8, rows3, 8)
            target[layer, pl.ds(8, rows3), :] = (
                (1.0 - OMEGA) * here + rows_at(g3, layer, 8, rows3) + rows_at(r3, layer, 8, rows3) * total_
            )
        source, target = target, (vb if target is va else va)
    coarse = source

    wide2 = bx2 + 16

    def lift2(layer, carry):
        spread_rows(tmp.at[layer - 1], coarse[(layer + 1) // 2, pl.ds(12, wide2 // 2), :])
        v2[layer, pl.ds(16, wide2), :] += tmp[layer - 1, pl.ds(0, wide2), :]
        return carry

    each(1, n2 + 1, lift2, 8)

    def post2(layer, carry):
        here, total_ = packed_sum(v2, q2, layer, 16, wide2, 4)
        f2[layer, pl.ds(16, wide2), :] = (
            (1.0 - OMEGA) * here + rows_at(g2, layer, 16, wide2) + rows_at(r2, layer, 16, wide2) * total_
        )
        return carry

    each(1, n2 + 1, post2, 8)

    for copy in started[:5]:
        copy.wait()
    kind = lane_of(bx2 + 4) & 3

    def lift1(m, carry):
        x = f2[bz2 * h + m, pl.ds(22, bx2 + 4), :]
        moved = {shift: roll(x, shift) if shift else x for shift in range(-2, 4)}
        for c in range(3):
            part = jnp.where(
                kind == 0, moved[-c], jnp.where(kind == 1, moved[1 - c], jnp.where(kind == 2, moved[2 - c], moved[3 - c]))
            )
            spread_rows(tmp.at[3 * m + c], part)
            lifted = tmp[3 * m + c, pl.ds(0, rows1), :]
            for i in range(2):
                v1[c, 2 * m + i, mid, :] += lifted
        return carry

    each(0, n1 // 2, lift1, 8)

    def post(s_ref, y_ref, g_ref, r_ref, v_ref, into, layer, to, row, count, step):
        faces = all_faces(s_ref, y_ref, layer, row, count)
        for c in range(3):
            here, along = neighbours(v_ref.at[c], faces, layer, row, count, step)
            dst = pl.ds(row, count)
            into(c, (1.0 - OMEGA) * here + g_ref[c, layer, dst, :] + r_ref[c, layer, dst, :] * total(along, c))

    def post1(layer, carry):
        def into(c, value):
            f1[c, layer, mid, :] = value

        post(s1, y1, g1, r1, v1, into, layer, layer, 8, rows1, 2)
        return carry

    each(1, n1 - 1, post1, 8)

    for copy in started[5:]:
        copy.wait()

    for c in range(3):
        for k in range(1, n1 - 1):
            slot = 3 * (k - 1) + c
            spread_rows(tmp.at[slot], f1[c, k, mid, :])
            lifted = tmp[slot, pl.ds(0, bx + 16), :]
            for i in (2 * k - 3, 2 * k - 2):
                if 0 <= i < bz + 2:
                    v0[c, i, near, :] += lifted

    def post0(layer, carry):
        for row, count in chunks(16, 16 + bx, 16):

            def into(c, value):
                out_ref[c, layer - 1, pl.ds(row - 16, count), :] = value

            post(s0, y0, g0, r0, v0, into, layer, layer, row, count, 1)
        return carry

    each(1, bz + 1, post0, 8)


def swapped(x, axis, start):
    pairs = [(i, i + 1) for i in range(start, lax.axis_size(axis) - 1, 2)]
    return lax.ppermute(x, axis, pairs + [(j, i) for i, j in pairs])


def vmem(*shape):
    return pltpu.VMEM(shape, F32)


def local(heights, tiles, material, clamped, stiffness_table, eigenstrain):
    bz, bx, _ = material.shape

    held = pl.BlockSpec(memory_space=pltpu.VMEM)
    anywhere = pl.BlockSpec(memory_space=pl.ANY)
    outside = pl.BlockSpec(memory_space=pltpu.HBM)
    own = pl.pallas_call(
        functools.partial(pack_kernel, bz, bx),
        out_shape=pltpu.VMEM(((bz + 2) * bx + SPARE, LANES), F32),
        in_specs=[outside] * 4,
        out_specs=held,
        scratch_shapes=[
            pltpu.VMEM((bz, bx, LANES), jnp.int32), pltpu.VMEM((2, bx, LANES), jnp.int32),
            pltpu.SMEM((3,), F32), pltpu.SMEM((3, 3), F32), pltpu.SemaphoreType.DMA((4,)),
        ],
    )(material, clamped, stiffness_table, eigenstrain)
    bricks = lax.all_gather(own, "height")
    strip = pltpu.VMEM((-(-(strips(bz)[2] + 2 * HALO) // 8) * 8, LANES), F32)
    near, far = pl.pallas_call(
        functools.partial(strip_kernel, heights, bz, bx),
        out_shape=[strip, strip],
        in_specs=[held],
        out_specs=[held, held],
        compiler_params=pltpu.CompilerParams(vmem_limit_bytes=4 * 2**20),
    )(bricks)
    far = swapped(far, "tile", 1)
    near = swapped(near, "tile", 0)

    bx1, bx2 = bx // 2, bx // 4
    nz, n1 = bz + 2 * HALO, bz // 2 + 8
    r0, r1 = bx + 32, bx1 + 24
    rows1 = bx1 + 8
    kept = [
        (bz + 2, bx + 16), (2, bz, bx), (3, bz + 2, bx + 16), (3, bz, bx), (3, bz, bx),
        (n1 - 4, rows1), (2, n1 - 6, rows1), (3, n1 - 4, rows1), (3, n1 - 6, rows1), (3, n1 - 6, rows1),
    ]
    kept = [jax.ShapeDtypeStruct((*shape, LANES), F32) for shape in kept]
    field0, field1 = (nz, r0, LANES), (n1, r1, LANES)
    fields = [field0, field0, (3, *field0), (3, *field0), (3, *field0), (3, *field0), (3, *field0), (2, *field0), (3, *field0)]
    fields = [pltpu.VMEM(shape, F32) for shape in [*fields, (n1 - 2, 3, r0, LANES)]]
    work = 24 * 6 * 3 * 1024
    inner = pl.pallas_call(
        functools.partial(inner_kernel, heights, tiles, bz, bx),
        out_shape=fields,
        in_specs=[held] * 2,
        out_specs=[held] * len(fields),
        cost_estimate=pl.CostEstimate(flops=work * 60, bytes_accessed=work * 40, transcendentals=0),
        compiler_params=pltpu.CompilerParams(vmem_limit_bytes=4 * 2**20),
    )(bricks, near)
    send, *saved = pl.pallas_call(
        functools.partial(down_kernel, heights, tiles, bz, bx),
        out_shape=[
            jax.ShapeDtypeStruct((heights * tiles, (bz // 4 * bx2 + bx2 // 4) // 2, 2, LANES), F32), *kept, *fields
        ],
        in_specs=[held] * (2 + len(fields)),
        out_specs=[held] + [anywhere] * len(kept) + [held] * len(fields),
        input_output_aliases={2 + k: 1 + len(kept) + k for k in range(len(fields))},
        scratch_shapes=[
            vmem(n1 - 2, 3, r0, LANES),
            vmem(*field1), vmem(*field1), vmem(3, *field1), vmem(3, *field1), vmem(3, *field1), vmem(3, *field1),
            vmem(2, *field1), vmem(3, *field1), pltpu.SemaphoreType.DMA((10,)),
        ],
        compiler_params=pltpu.CompilerParams(vmem_limit_bytes=12 * 2**20),
    )(bricks, far, *inner)
    saved = saved[: len(kept)]

    received = lax.all_to_all(send, ("tile", "height"), 0, 0)

    rows2 = bx2 + 2 * REACH
    rows3 = -(-(rows2 // 2) // 8) * 8
    up0, up1 = (bz + 2, r0, LANES), (n1 - 4, r1, LANES)
    up2 = (heights * bz // 4 + 2, rows2 + 16, LANES)
    up3 = (heights * bz // 8 + 2, rows3 + 16, LANES)
    return pl.pallas_call(
        functools.partial(up_kernel, heights, tiles, bz, bx),
        out_shape=jax.ShapeDtypeStruct((3, bz, bx, LANES), F32),
        in_specs=[held] + [anywhere] * len(kept),
        out_specs=held,
        scratch_shapes=[
            vmem(*up0), vmem(2, *up0), vmem(3, *up0), vmem(3, *up0), vmem(3, *up0),
            vmem(*up1), vmem(2, *up1), vmem(3, *up1), vmem(3, *up1), vmem(3, *up1), vmem(3, *up1),
            vmem(*up2), vmem(*up2), vmem(*up2), vmem(6, *up2), vmem(*up2), vmem(*up2), vmem(*up2), vmem(*up2), vmem(*up2),
            vmem(*up3), vmem(*up3), vmem(*up3), vmem(6, *up3), vmem(*up3), vmem(*up3), vmem(*up3), vmem(*up3),
            vmem(heights * bz // 8, rows2 + 24, LANES), vmem(max(heights * bz // 4, 3 * (n1 - 6)), r0, LANES), pltpu.SemaphoreType.DMA((10,)),
        ],
        compiler_params=pltpu.CompilerParams(vmem_limit_bytes=16 * 2**20),
    )(received, *saved)


def solution(mesh):
    sides = mesh.shape["height"], mesh.shape["tile"]
    in_specs = (P("height", "tile", None), P("height", "tile", None), P(), P())
    out_specs = P(None, "height", "tile", None)
    return jax.shard_map(
        functools.partial(local, *sides), mesh=mesh, in_specs=in_specs, out_specs=out_specs, check_vma=False
    )
```

```python
import functools

import jax
import jax.numpy as jnp
from jax import lax
from jax.experimental import pallas as pl
from jax.experimental.pallas import tpu as pltpu
from jax.sharding import PartitionSpec as P

PENALTY = 50.0
OMEGA = 0.6
COARSE_SWEEPS = 6
LANES = 128
HALO = 9
REACH = 16
SPARE = 4
F32 = jnp.float32


def each(start, stop, body, step):
    groups = (stop - start) // step

    def group(i, carry):
        for k in range(step):
            body(start + i * step + k, 0)
        return carry

    if groups > 1:
        lax.fori_loop(0, groups, group, 0)
    elif groups == 1:
        group(0, 0)
    for layer in range(start + groups * step, stop):
        body(layer, 0)


def chunks(start, stop, size):
    return [(row, min(size, stop - row)) for row in range(start, stop, size)]


def lane_of(rows):
    return lax.broadcasted_iota(jnp.int32, (rows, LANES), 1)


def roll(x, shift):
    return pltpu.roll(x, shift % LANES, 1)


def rows_at(ref, layer, row, count):
    return ref[layer, pl.ds(row, count), :]


def cross_faces(s_ref, layer, row, count):
    here = rows_at(s_ref, layer, row, count)
    return here, [
        here + rows_at(s_ref, layer - 1, row, count),
        here + rows_at(s_ref, layer + 1, row, count),
        here + rows_at(s_ref, layer, row - 1, count),
        here + rows_at(s_ref, layer, row + 1, count),
    ]


def lane_faces(here, step):
    lane = lane_of(here.shape[0])
    first, last = lane < step, lane >= LANES - step
    low = here + jnp.where(first, 0.0, roll(here, step))
    high = here + jnp.where(last, 0.0, roll(here, -step))
    return low, high, jnp.where(first, 0.0, low), jnp.where(last, 0.0, high)


def neighbours(v_ref, faces, layer, row, count, step):
    here = rows_at(v_ref, layer, row, count)
    along = [
        faces[0] * rows_at(v_ref, layer - 1, row, count)
        + faces[1] * rows_at(v_ref, layer + 1, row, count),
        faces[2] * rows_at(v_ref, layer, row - 1, count)
        + faces[3] * rows_at(v_ref, layer, row + 1, count),
        faces[4] * roll(here, step) + faces[5] * roll(here, -step),
    ]
    return here, along


def total(along, component):
    return (along[0] + along[1] + along[2]) + along[component]


def safe_rate(here, doubled):
    return jnp.where(here > 0.0, OMEGA / doubled, 0.0)


def pair_lanes(x, step):
    upper = (lane_of(x.shape[0]) & step) != 0
    return x + jnp.where(upper, roll(x, step), roll(x, -step))


def pair_rows(ref, row, count):
    return ref[pl.ds(row, count, stride=2), :] + ref[pl.ds(row + 1, count, stride=2), :]


def spread_rows(ref, x):
    count = x.shape[0]
    ref[pl.ds(0, count, stride=2), :] = x
    ref[pl.ds(1, count, stride=2), :] = x


def level_setup(s_ref, p_ref, r_ref, d_ref, g_ref, y_ref, b_of, layer, row, count, step):
    here, cross = cross_faces(s_ref, layer, row, count)
    low, high, low_in, high_in = lane_faces(here, step)
    y_ref[0, layer, pl.ds(row, count), :] = low_in
    y_ref[1, layer, pl.ds(row, count), :] = high_in
    sums = [cross[0] + cross[1], cross[2] + cross[3], low + high]
    base = rows_at(p_ref, layer, row, count) + (sums[0] + sums[1] + sums[2])
    for c in range(3):
        doubled = base + sums[c]
        rate = safe_rate(here, doubled)
        d_ref[c, layer, pl.ds(row, count), :] = doubled
        r_ref[c, layer, pl.ds(row, count), :] = rate
        g_ref[c, layer, pl.ds(row, count), :] = (2.0 * rate) * b_of(c)


def all_faces(s_ref, y_ref, layer, row, count):
    _, cross = cross_faces(s_ref, layer, row, count)
    return cross + [
        y_ref[0, layer, pl.ds(row, count), :],
        y_ref[1, layer, pl.ds(row, count), :],
    ]


def first_sweep(s_ref, y_ref, r_ref, g_ref, v_ref, layer, row, count, step):
    faces = all_faces(s_ref, y_ref, layer, row, count)
    for c in range(3):
        here, along = neighbours(g_ref.at[c], faces, layer, row, count, step)
        rate = r_ref[c, layer, pl.ds(row, count), :]
        v_ref[c, layer, pl.ds(row, count), :] = (2.0 - OMEGA) * here + rate * total(along, c)


def remainder(s_ref, y_ref, b_ref, d_ref, v_ref, layer, row, count, step):
    faces = all_faces(s_ref, y_ref, layer, row, count)
    result = []
    for c in range(3):
        here, along = neighbours(v_ref.at[c], faces, layer, row, count, step)
        doubled = d_ref[c, layer, pl.ds(row, count), :]
        source = b_ref[c, layer, pl.ds(row, count), :]
        result.append(source + 0.5 * (total(along, c) - doubled * here))
    return result


def strips(bz):
    counts = [min(layer, HALO, bz + 2 * HALO - 1 - layer) for layer in range(bz + 2 * HALO)]
    starts = [sum(counts[:layer]) for layer in range(len(counts))]
    return counts, starts, sum(counts)


def pack_kernel(bz, bx, material_ref, clamped_ref, table_ref, strain_ref, own_ref, label, joined, table, strain, sem):
    copies = [
        pltpu.make_async_copy(material_ref, label, sem.at[0]),
        pltpu.make_async_copy(clamped_ref.at[pl.ds(0, 2)], joined, sem.at[1]),
        pltpu.make_async_copy(table_ref, table, sem.at[2]),
        pltpu.make_async_copy(strain_ref, strain, sem.at[3]),
    ]
    for copy in copies:
        copy.start()
    for copy in copies:
        copy.wait()
    for slot in range(bz + 2):
        src = label.at[slot] if slot < bz else joined.at[slot - bz]
        own_ref[pl.ds(slot * bx, bx), :] = src[...].astype(F32)
    lane = lane_of(SPARE)
    row = jnp.zeros((SPARE, LANES), F32)
    for k in range(3):
        row = jnp.where(lane == k, table[k], row)
        for c in range(3):
            row = jnp.where(lane == 3 + 3 * c + k, table[k] * strain[k, c], row)
    own_ref[pl.ds((bz + 2) * bx, SPARE), :] = row


def place(heights, bz, layer):
    z = bz * lax.axis_index("height") - HALO + layer
    z_in = jnp.clip(z, 0, heights * bz - 1)
    return z, z_in // bz, z_in % bz


def strip_kernel(heights, bz, bx, x_ref, near_ref, far_ref):
    odd = (lax.axis_index("tile") & 1) == 1
    counts, starts, end = strips(bz)
    wanted = [(place(heights, bz, layer)[1:], count, start) for layer, (count, start) in enumerate(zip(counts, starts))]
    wanted += [((0, bz + k), HALO, end + HALO * k) for k in range(2)]
    for (brick, slot), count, start in wanted:
        if count:
            first = x_ref[brick, pl.ds(slot * bx, count), :]
            last = x_ref[brick, pl.ds(slot * bx + bx - count, count), :]
            near_ref[pl.ds(start, count), :] = jnp.where(odd, first, last)
            far_ref[pl.ds(start, count), :] = jnp.where(odd, last, first)


def tables_of(x_ref, row):
    spare = x_ref[0, pl.ds(row, 1), :]
    table = [jnp.broadcast_to(spare[:, k : k + 1], (1, LANES)) for k in range(12)]
    return table[:3], [table[3 + 3 * c : 6 + 3 * c] for c in range(3)]


def store_layer(s, st, label, layer, to, weight, tables):
    is0, is1 = label == 0.0, label == 1.0
    dst = pl.ds(to, label.shape[0])
    for ref, values in zip((s, *(st.at[c] for c in range(3))), (tables[0], *tables[1])):
        a, b, c = (value * weight for value in values)
        ref[layer, dst, :] = jnp.where(is0, a, jnp.where(is1, b, c))


def store_strip(s, st, p, strip_ref, heights, bz, layer, far_side, valid, bx, tables):
    counts, starts, end = strips(bz)
    z, _, _ = place(heights, bz, layer)
    weight = jnp.where((z >= 0) & (z < heights * bz), valid, 0.0)
    count = counts[layer]
    if count:
        to = jnp.where(far_side, 16 + bx, 16 - count)
        store_layer(s, st, strip_ref[pl.ds(starts[layer], count), :], layer, to, weight, tables)
    joined = strip_ref[pl.ds(end + HALO * jnp.clip(z, 0, 1), HALO), :]
    to = jnp.where(far_side, 16 + bx, 16 - HALO)
    p[layer, pl.ds(to, HALO), :] = joined * jnp.where((z >= 0) & (z < 2), 2.0 * PENALTY * valid, 0.0)


def fine_setup(s, p, st, b, r, d, g, y, layer, row, count):
    lane = lane_of(count)
    here = st[2, layer, pl.ds(row, count), :]
    source = [
        0.5 * (rows_at(st.at[0], layer - 1, row, count) - rows_at(st.at[0], layer + 1, row, count)),
        0.5 * (rows_at(st.at[1], layer, row - 1, count) - rows_at(st.at[1], layer, row + 1, count)),
        0.5 * (jnp.where(lane < 1, 0.0, roll(here, 1)) - jnp.where(lane >= LANES - 1, 0.0, roll(here, -1))),
    ]
    for c in range(3):
        b[c, layer, pl.ds(row, count), :] = source[c]
    level_setup(s, p, r, d, g, y, lambda c: source[c], layer, row, count, 1)


def fine_down(bz, s, p, st, b, r, d, g, y, v, rest, rows, step):
    nz = bz + 2 * HALO

    def setup0(layer, carry):
        for row in rows[0]:
            fine_setup(s, p, st, b, r, d, g, y, layer, row, 16)
        return carry

    def sweep0(layer, carry):
        for row in rows[1]:
            first_sweep(s, y, r, g, v, layer, row, 16, 1)
        return carry

    def restrict0(j, carry):
        layer = 3 + 2 * j
        for row in rows[2]:
            one = remainder(s, y, b, d, v, layer, row, 16, 1)
            two = remainder(s, y, b, d, v, layer + 1, row, 16, 1)
            for c in range(3):
                rest[j, c, pl.ds(row, 16), :] = one[c] + two[c]
        return carry

    each(1, nz - 1, setup0, step)
    each(2, nz - 2, sweep0, step)
    each(0, bz // 2 + 6, restrict0, step)


def inner_kernel(heights, tiles, bz, bx, x_ref, near_ref, s, p, st, b, r, d, g, y, v, rest):
    t = lax.axis_index("tile")
    odd = (t & 1) == 1
    tables = tables_of(x_ref, (bz + 2) * bx)
    valid = jnp.where(odd | (t < tiles - 1), 1.0, 0.0)

    def read_layer(layer, carry):
        z, brick, slot = place(heights, bz, layer)
        inside = jnp.where((z >= 0) & (z < heights * bz), 1.0, 0.0)
        store_layer(s, st, x_ref[brick, pl.ds(slot * bx, bx), :], layer, 16, inside, tables)
        bottom = jnp.where((z >= 0) & (z < 2), 2.0 * PENALTY, 0.0)
        p[layer, pl.ds(16, bx), :] = x_ref[0, pl.ds((bz + jnp.clip(z, 0, 1)) * bx, bx), :] * bottom
        store_strip(s, st, p, near_ref, heights, bz, layer, jnp.logical_not(odd), valid, bx, tables)
        return carry

    each(0, bz + 2 * HALO, read_layer, bz + 2 * HALO + 1)
    rows = [[jnp.where(odd, 8 - k, 24 + k) + at for at in range(0, bx, 16)] for k in range(3)]
    fine_down(bz, s, p, st, b, r, d, g, y, v, rest, rows, 8)


def down_kernel(
    heights, tiles, bz, bx,
    x_ref, far_ref, *refs,
):
    send_ref, s1, y1, v1, g1, r1, s, p, st, b, r, d, g, y, v, rest, tmp, p1, b1, d1 = refs[10:]
    h, t = lax.axis_index("height"), lax.axis_index("tile")
    odd = (t & 1) == 1
    n1 = bz // 2 + 8
    bx1, bx2 = bx // 2, bx // 4
    low = 8
    tables = tables_of(x_ref, (bz + 2) * bx)
    valid = jnp.where(jnp.where(odd, t < tiles - 1, t > 0), 1.0, 0.0)

    def read_layer(layer, carry):
        store_strip(s, st, p, far_ref, heights, bz, layer, odd, valid, bx, tables)
        return carry

    each(0, bz + 2 * HALO, read_layer, bz + 2 * HALO + 1)
    rows = [[jnp.where(odd, bx + 8 - k, 8 + k)] for k in range(3)]
    fine_down(bz, s, p, st, b, r, d, g, y, v, rest, rows, 24)

    rows1 = bx1 + 8

    def restrict0(j, carry):
        for c in range(3):
            b1[c, j + 1, pl.ds(8, rows1), :] = pair_lanes(pair_rows(rest.at[j, c], low, rows1), 1)
        return carry

    each(0, n1 - 2, restrict0, 8)

    def coarse0(k, carry):
        for field, scale, into in ((s, 0.5, s1), (p, 1.0, p1)):
            both = [pair_rows(field.at[1 + 2 * k + i], low, rows1) for i in range(2)]
            into[k, pl.ds(8, rows1), :] = scale * pair_lanes(both[0] + both[1], 1)
        return carry

    each(0, n1, coarse0, 8)

    def setup1(layer, carry):
        level_setup(
            s1, p1, r1, d1, g1, y1,
            lambda c: b1[c, layer, pl.ds(8, rows1), :], layer, 8, rows1, 2,
        )
        return carry

    each(1, n1 - 1, setup1, 8)

    def sweep1(layer, carry):
        first_sweep(s1, y1, r1, g1, v1, layer, 8, rows1, 2)
        return carry

    each(2, n1 - 2, sweep1, 8)

    lane = lane_of(bx2) & 3
    packed = []
    for m in range(bz // 4):
        layer = 4 + 2 * m
        one = remainder(s1, y1, b1, d1, v1, layer, 8, rows1, 2)
        two = remainder(s1, y1, b1, d1, v1, layer + 1, 8, rows1, 2)
        fields = []
        for c in range(3):
            tmp[m, c, pl.ds(0, rows1), :] = one[c] + two[c]
            fields.append(pair_lanes(pair_rows(tmp.at[m, c], 4, bx2), 2))
        both = [pair_rows(s1.at[layer + i], 12, bx2) for i in range(2)]
        stiff = 0.5 * pair_lanes(both[0] + both[1], 2)
        packed.append(
            jnp.where(lane == 0, fields[0], jnp.where(lane == 1, fields[1], jnp.where(lane == 2, fields[2], stiff)))
        )
    bottom = jnp.maximum(bz // 2 * (1 - h), 0)
    both = [pair_rows(p1.at[bottom + i], 12, bx2) for i in range(2)]
    tmp[2, 0, pl.ds(0, bx2), :] = pair_lanes(both[0] + both[1], 2)
    quarter = bx2 // 8
    first = jnp.minimum(h, 1) * (bx2 // 2)
    part = [tmp[2, 0, pl.ds(first + j, quarter, stride=4), :] for j in range(4)]
    lane = lane_of(quarter) & 3
    packed.append(jnp.where(lane == 0, part[0], jnp.where(lane == 1, part[1], jnp.where(lane == 2, part[2], part[3]))))
    size = sum(value.shape[0] for value in packed)

    def fill(i, carry):
        at = i * size
        for value in packed:
            send_ref[pl.ds(at, value.shape[0]), :] = value
            at = at + value.shape[0]
        return carry

    each(0, heights * tiles, fill, 8)


def up_kernel(
    heights, tiles, bz, bx,
    recv_ref, s0, y0, v0, g0, r0, s1, y1, v1, g1, r1, out_ref,
    w0, w1, f1, s2, p2, b2, q2, r2, d2, g2, v2, f2, s3, p3, b3, q3, r3, g3, va, vb, rest2, tmp, done, sem,
):
    h, t = lax.axis_index("height"), lax.axis_index("tile")
    bx1, bx2, bz2 = bx // 2, bx // 4, bz // 4
    n1, n2, n3 = bz // 2 + 8, heights * bz // 4, heights * bz // 8
    rows1 = bx1 + 8
    near = pl.ds(8, bx + 16)
    mid = pl.ds(8, rows1)

    for ref in (s2, p2, g2, v2, f2, s3, p3, g3, va, vb):
        ref[...] = jnp.zeros(ref.shape, F32)
    rest2[...] = jnp.zeros(rest2.shape, F32)

    side = REACH // bx2
    size = bz2 * bx2 + bx2 // 8
    lane = lane_of(bx2) & 3
    for dt in range(-side, side + 1):
        other = t + dt
        valid = (other >= 0) & (other < tiles)
        other = jnp.clip(other, 0, tiles - 1)
        scale = jnp.where(valid, 1.0, 0.0)
        dst = pl.ds(8 + (dt + side) * bx2, bx2)
        for hh in range(heights):
            for m in range(bz2):
                x = recv_ref[pl.ds((other * heights + hh) * size + m * bx2, bx2), :] * scale
                layer = 1 + hh * bz2 + m
                b2[layer, dst, :] = jnp.where(lane == 3, 0.0, x)
                s2[layer, dst, :] = jnp.where(
                    lane == 3, x, jnp.where(lane == 2, roll(x, -1), jnp.where(lane == 1, roll(x, -2), roll(x, -3)))
                )
        quarter = bx2 // 8
        small = lane_of(quarter) & 3
        for hh in range(2):
            x = recv_ref[pl.ds((other * heights + hh) * size + bz2 * bx2, quarter), :] * scale
            moved = {shift: roll(x, shift) if shift else x for shift in range(-3, 4)}
            for j in range(4):
                row = 8 + (dt + side) * bx2 + hh * (bx2 // 2) + j
                p2[1, pl.ds(row, quarter, stride=4), :] = jnp.where(
                    small == 0, moved[-j], jnp.where(small == 1, moved[1 - j], jnp.where(small == 2, moved[2 - j], moved[3 - j]))
                )

    def weights(count):
        kind = lane_of(count) & 3
        return [jnp.where(kind == c, 2.0, 1.0) for c in range(3)]

    def setup(s_ref, p_ref, b_ref, q_ref, r_ref, d_ref, g_ref, layer, row, count, step):
        here, cross = cross_faces(s_ref, layer, row, count)
        low, high, low_in, high_in = lane_faces(here, step)
        w = weights(count)
        dst = pl.ds(row, count)
        for k in range(4):
            q_ref[k, layer, dst, :] = w[k // 2] * cross[k]
        q_ref[4, layer, dst, :] = w[2] * low_in
        q_ref[5, layer, dst, :] = w[2] * high_in
        doubled = rows_at(p_ref, layer, row, count) + (
            w[0] * (cross[0] + cross[1]) + w[1] * (cross[2] + cross[3]) + w[2] * (low + high)
        )
        rate = safe_rate(here, doubled)
        r_ref[layer, dst, :] = rate
        if d_ref is not None:
            d_ref[layer, dst, :] = doubled
        g_ref[layer, dst, :] = (2.0 * rate) * rows_at(b_ref, layer, row, count)

    def packed_sum(v_ref, q_ref, layer, row, count, step):
        faces = [q_ref[k, layer, pl.ds(row, count), :] for k in range(6)]
        here, along = neighbours(v_ref, faces, layer, row, count, step)
        return here, along[0] + along[1] + along[2]

    rows2 = bx2 + 2 * REACH

    def setup2(layer, carry):
        setup(s2, p2, b2, q2, r2, d2, g2, layer, 8, rows2, 4)
        return carry

    each(1, n2 + 1, setup2, 8)

    def sweep2(layer, carry):
        here, total_ = packed_sum(g2, q2, layer, 8, rows2, 4)
        v2[layer, pl.ds(8, rows2), :] = (2.0 - OMEGA) * here + rows_at(r2, layer, 8, rows2) * total_
        return carry

    each(1, n2 + 1, sweep2, 8)

    rows3 = -(-(rows2 // 2) // 8) * 8

    def restrict2(j, carry):
        rest = 0.0
        for i in range(2):
            layer = 1 + 2 * j + i
            here, total_ = packed_sum(v2, q2, layer, 8, rows2, 4)
            rest = rest + rows_at(b2, layer, 8, rows2) + 0.5 * (total_ - rows_at(d2, layer, 8, rows2) * here)
        rest2[j, pl.ds(8, rows2), :] = rest
        dst = pl.ds(8, rows3)
        b3[j + 1, dst, :] = pair_lanes(pair_rows(rest2.at[j], 8, rows3), 4)
        for field, scale, into in ((s2, 0.5, s3), (p2, 1.0, p3)):
            both = [pair_rows(field.at[1 + 2 * j + i], 8, rows3) for i in range(2)]
            into[j + 1, dst, :] = scale * pair_lanes(both[0] + both[1], 4)
        return carry

    each(0, n3, restrict2, 8)

    for layer in range(1, n3 + 1):
        setup(s3, p3, b3, q3, r3, None, g3, layer, 8, rows3, 8)
    source, target = g3, va
    for _ in range(COARSE_SWEEPS - 1):
        for layer in range(1, n3 + 1):
            here, total_ = packed_sum(source, q3, layer, 8, rows3, 8)
            target[layer, pl.ds(8, rows3), :] = (
                (1.0 - OMEGA) * here + rows_at(g3, layer, 8, rows3) + rows_at(r3, layer, 8, rows3) * total_
            )
        source, target = target, (vb if target is va else va)
    coarse = source

    wide2 = bx2 + 16

    def lift2(layer, carry):
        spread_rows(tmp.at[layer - 1], coarse[(layer + 1) // 2, pl.ds(12, wide2 // 2), :])
        v2[layer, pl.ds(16, wide2), :] += tmp[layer - 1, pl.ds(0, wide2), :]
        return carry

    each(1, n2 + 1, lift2, 8)

    def post2(layer, carry):
        here, total_ = packed_sum(v2, q2, layer, 16, wide2, 4)
        f2[layer, pl.ds(16, wide2), :] = (
            (1.0 - OMEGA) * here + rows_at(g2, layer, 16, wide2) + rows_at(r2, layer, 16, wide2) * total_
        )
        return carry

    each(1, n2 + 1, post2, 8)

    kind = lane_of(bx2 + 4) & 3

    def lift1(m, carry):
        x = f2[bz2 * h + m, pl.ds(22, bx2 + 4), :]
        moved = {shift: roll(x, shift) if shift else x for shift in range(-2, 4)}
        for c in range(3):
            part = jnp.where(
                kind == 0, moved[-c], jnp.where(kind == 1, moved[1 - c], jnp.where(kind == 2, moved[2 - c], moved[3 - c]))
            )
            spread_rows(tmp.at[3 * m + c], part)
            lifted = tmp[3 * m + c, pl.ds(0, rows1), :]
            for i in range(2):
                w1[c, 2 + 2 * m + i, mid, :] = v1[c, 2 + 2 * m + i, mid, :] + lifted
        return carry

    each(0, n1 // 2 - 2, lift1, 8)

    def post(s_ref, y_ref, g_ref, r_ref, v_ref, into, layer, row, count, step):
        faces = all_faces(s_ref, y_ref, layer, row, count)
        for c in range(3):
            here, along = neighbours(v_ref.at[c], faces, layer, row, count, step)
            dst = pl.ds(row, count)
            into(c, (1.0 - OMEGA) * here + g_ref[c, layer, dst, :] + r_ref[c, layer, dst, :] * total(along, c))

    def post1(layer, carry):
        def into(c, value):
            f1[c, layer, mid, :] = value

        post(s1, y1, g1, r1, w1, into, layer, 8, rows1, 2)
        return carry

    each(3, n1 - 3, post1, 8)

    for k in range(3, n1 - 3):
        for c in range(3):
            slot = 3 * (k - 3) + c
            spread_rows(tmp.at[slot], f1[c, k, mid, :])
            lifted = tmp[slot, pl.ds(0, bx + 16), :]
            for layer in (2 * k + 1, 2 * k + 2):
                if HALO - 1 <= layer <= HALO + bz:
                    w0[c, layer, near, :] = v0[c, layer, near, :] + lifted

    started = []
    for layer in range(HALO, HALO + bz):
        z = layer - HALO
        for row, count in chunks(16, 16 + bx, 16):

            def into(c, value):
                done[c, z, pl.ds(row - 16, count), :] = value

            post(s0, y0, g0, r0, w0, into, layer, row, count, 1)
        started.append(pltpu.make_async_copy(done.at[:, z], out_ref.at[:, z], sem.at[z]))
        started[-1].start()
    for copy in started:
        copy.wait()


def swapped(x, axis, start):
    pairs = [(i, i + 1) for i in range(start, lax.axis_size(axis) - 1, 2)]
    return lax.ppermute(x, axis, pairs + [(j, i) for i, j in pairs])


def vmem(*shape):
    return pltpu.VMEM(shape, F32)


def local(heights, tiles, material, clamped, stiffness_table, eigenstrain):
    bz, bx, _ = material.shape

    held = pl.BlockSpec(memory_space=pltpu.VMEM)
    outside = pl.BlockSpec(memory_space=pltpu.HBM)
    own = pl.pallas_call(
        functools.partial(pack_kernel, bz, bx),
        out_shape=pltpu.VMEM(((bz + 2) * bx + SPARE, LANES), F32),
        in_specs=[outside] * 4,
        out_specs=held,
        scratch_shapes=[
            pltpu.VMEM((bz, bx, LANES), jnp.int32), pltpu.VMEM((2, bx, LANES), jnp.int32),
            pltpu.SMEM((3,), F32), pltpu.SMEM((3, 3), F32), pltpu.SemaphoreType.DMA((4,)),
        ],
    )(material, clamped, stiffness_table, eigenstrain)
    bricks = lax.all_gather(own, "height")
    strip = pltpu.VMEM((-(-(strips(bz)[2] + 2 * HALO) // 8) * 8, LANES), F32)
    near, far = pl.pallas_call(
        functools.partial(strip_kernel, heights, bz, bx),
        out_shape=[strip, strip],
        in_specs=[held],
        out_specs=[held, held],
        compiler_params=pltpu.CompilerParams(vmem_limit_bytes=4 * 2**20),
    )(bricks)
    far = swapped(far, "tile", 1)
    near = swapped(near, "tile", 0)

    bx1, bx2 = bx // 2, bx // 4
    nz, n1 = bz + 2 * HALO, bz // 2 + 8
    r0, r1 = bx + 32, bx1 + 24
    rows1 = bx1 + 8
    field0, field1 = (nz, r0, LANES), (n1, r1, LANES)
    fields = [field0, field0, (3, *field0), (3, *field0), (3, *field0), (3, *field0), (3, *field0), (2, *field0), (3, *field0)]
    fields = [pltpu.VMEM(shape, F32) for shape in [*fields, (n1 - 2, 3, r0, LANES)]]
    work = 24 * 6 * 3 * 1024
    inner = pl.pallas_call(
        functools.partial(inner_kernel, heights, tiles, bz, bx),
        out_shape=fields,
        in_specs=[held] * 2,
        out_specs=[held] * len(fields),
        cost_estimate=pl.CostEstimate(flops=work * 60, bytes_accessed=work * 40, transcendentals=0),
        compiler_params=pltpu.CompilerParams(vmem_limit_bytes=4 * 2**20),
    )(bricks, near)
    kept = [field1, (2, *field1), (3, *field1), (3, *field1), (3, *field1)]
    kept = [pltpu.VMEM(shape, F32) for shape in kept]
    send, s1, y1, v1, g1, r1_, s, _, _, _, r, _, g, y, v, _ = pl.pallas_call(
        functools.partial(down_kernel, heights, tiles, bz, bx),
        out_shape=[
            pltpu.VMEM((heights * tiles * (bz // 4 * bx2 + bx2 // 8), LANES), F32), *kept, *fields
        ],
        in_specs=[held] * (2 + len(fields)),
        out_specs=[held] * (1 + len(kept) + len(fields)),
        input_output_aliases={2 + k: 1 + len(kept) + k for k in range(len(fields))},
        scratch_shapes=[vmem(n1 - 2, 3, r0, LANES), vmem(*field1), vmem(3, *field1), vmem(3, *field1)],
        compiler_params=pltpu.CompilerParams(vmem_limit_bytes=8 * 2**20),
    )(bricks, far, *inner)

    blocks = send.reshape(heights * tiles, -1, 1, LANES)
    received = lax.all_to_all(blocks, ("tile", "height"), 0, 0).reshape(send.shape)

    rows2 = bx2 + 2 * REACH
    rows3 = -(-(rows2 // 2) // 8) * 8
    up2 = (heights * bz // 4 + 2, rows2 + 16, LANES)
    up3 = (heights * bz // 8 + 2, rows3 + 16, LANES)
    return pl.pallas_call(
        functools.partial(up_kernel, heights, tiles, bz, bx),
        out_shape=jax.ShapeDtypeStruct((3, bz, bx, LANES), F32),
        in_specs=[held] * 11,
        out_specs=outside,
        scratch_shapes=[
            vmem(3, *field0), vmem(3, *field1), vmem(3, *field1),
            vmem(*up2), vmem(*up2), vmem(*up2), vmem(6, *up2), vmem(*up2), vmem(*up2), vmem(*up2), vmem(*up2), vmem(*up2),
            vmem(*up3), vmem(*up3), vmem(*up3), vmem(6, *up3), vmem(*up3), vmem(*up3), vmem(*up3), vmem(*up3),
            vmem(heights * bz // 8, rows2 + 24, LANES), vmem(max(heights * bz // 4, 3 * (n1 - 6)), r0, LANES),
            vmem(3, bz, bx, LANES), pltpu.SemaphoreType.DMA((bz,)),
        ],
        compiler_params=pltpu.CompilerParams(vmem_limit_bytes=16 * 2**20),
    )(received, s, y, v, g, r, s1, y1, v1, g1, r1_)


def solution(mesh):
    sides = mesh.shape["height"], mesh.shape["tile"]
    in_specs = (P("height", "tile", None), P("height", "tile", None), P(), P())
    out_specs = P(None, "height", "tile", None)
    return jax.shard_map(
        functools.partial(local, *sides), mesh=mesh, in_specs=in_specs, out_specs=out_specs, check_vma=False
    )
```

```python
import functools

import jax
import jax.numpy as jnp
from jax import lax
from jax.experimental import pallas as pl
from jax.experimental.pallas import tpu as pltpu
from jax.sharding import PartitionSpec as P

PENALTY = 50.0
OMEGA = 0.6
COARSE_SWEEPS = 6
LANES = 128
HALO = 9
REACH = 16
SPARE = 4
F32 = jnp.float32


def each(start, stop, body, step):
    groups = (stop - start) // step

    def group(i, carry):
        for k in range(step):
            body(start + i * step + k, 0)
        return carry

    if groups > 1:
        lax.fori_loop(0, groups, group, 0)
    elif groups == 1:
        group(0, 0)
    for layer in range(start + groups * step, stop):
        body(layer, 0)


def chunks(start, stop, size):
    return [(row, min(size, stop - row)) for row in range(start, stop, size)]


def lane_of(rows):
    return lax.broadcasted_iota(jnp.int32, (rows, LANES), 1)


def roll(x, shift):
    return pltpu.roll(x, shift % LANES, 1)


def rows_at(ref, layer, row, count):
    return ref[layer, pl.ds(row, count), :]


def cross_faces(s_ref, layer, row, count):
    here = rows_at(s_ref, layer, row, count)
    return here, [
        here + rows_at(s_ref, layer - 1, row, count),
        here + rows_at(s_ref, layer + 1, row, count),
        here + rows_at(s_ref, layer, row - 1, count),
        here + rows_at(s_ref, layer, row + 1, count),
    ]


def lane_faces(here, step):
    lane = lane_of(here.shape[0])
    first, last = lane < step, lane >= LANES - step
    low = here + jnp.where(first, 0.0, roll(here, step))
    high = here + jnp.where(last, 0.0, roll(here, -step))
    return low, high, jnp.where(first, 0.0, low), jnp.where(last, 0.0, high)


def neighbours(v_ref, faces, layer, row, count, step):
    here = rows_at(v_ref, layer, row, count)
    along = [
        faces[0] * rows_at(v_ref, layer - 1, row, count)
        + faces[1] * rows_at(v_ref, layer + 1, row, count),
        faces[2] * rows_at(v_ref, layer, row - 1, count)
        + faces[3] * rows_at(v_ref, layer, row + 1, count),
        faces[4] * roll(here, step) + faces[5] * roll(here, -step),
    ]
    return here, along


def total(along, component):
    return (along[0] + along[1] + along[2]) + along[component]


def safe_rate(here, doubled):
    return jnp.where(here > 0.0, OMEGA / doubled, 0.0)


def pair_lanes(x, step):
    upper = (lane_of(x.shape[0]) & step) != 0
    return x + jnp.where(upper, roll(x, step), roll(x, -step))


def pair_rows(ref, row, count):
    return ref[pl.ds(row, count, stride=2), :] + ref[pl.ds(row + 1, count, stride=2), :]


def spread_rows(ref, x):
    count = x.shape[0]
    ref[pl.ds(0, count, stride=2), :] = x
    ref[pl.ds(1, count, stride=2), :] = x


def level_setup(s_ref, p_ref, r_ref, d_ref, g_ref, y_ref, b_of, layer, row, count, step):
    here, cross = cross_faces(s_ref, layer, row, count)
    low, high, low_in, high_in = lane_faces(here, step)
    y_ref[0, layer, pl.ds(row, count), :] = low_in
    y_ref[1, layer, pl.ds(row, count), :] = high_in
    sums = [cross[0] + cross[1], cross[2] + cross[3], low + high]
    base = rows_at(p_ref, layer, row, count) + (sums[0] + sums[1] + sums[2])
    for c in range(3):
        doubled = base + sums[c]
        rate = safe_rate(here, doubled)
        d_ref[c, layer, pl.ds(row, count), :] = doubled
        r_ref[c, layer, pl.ds(row, count), :] = rate
        g_ref[c, layer, pl.ds(row, count), :] = rate * b_of(c)


def all_faces(s_ref, y_ref, layer, row, count):
    _, cross = cross_faces(s_ref, layer, row, count)
    return cross + [
        y_ref[0, layer, pl.ds(row, count), :],
        y_ref[1, layer, pl.ds(row, count), :],
    ]


def first_sweep(s_ref, y_ref, r_ref, g_ref, v_ref, layer, row, count, step):
    faces = all_faces(s_ref, y_ref, layer, row, count)
    for c in range(3):
        here, along = neighbours(g_ref.at[c], faces, layer, row, count, step)
        rate = r_ref[c, layer, pl.ds(row, count), :]
        v_ref[c, layer, pl.ds(row, count), :] = (2.0 - OMEGA) * here + rate * total(along, c)


def remainder(s_ref, y_ref, b_ref, d_ref, v_ref, layer, row, count, step):
    faces = all_faces(s_ref, y_ref, layer, row, count)
    result = []
    for c in range(3):
        here, along = neighbours(v_ref.at[c], faces, layer, row, count, step)
        doubled = d_ref[c, layer, pl.ds(row, count), :]
        source = b_ref[c, layer, pl.ds(row, count), :]
        result.append(source + (total(along, c) - doubled * here))
    return result


def strips(bz):
    counts = [min(layer, HALO, bz + 2 * HALO - 1 - layer) for layer in range(bz + 2 * HALO)]
    starts = [sum(counts[:layer]) for layer in range(len(counts))]
    return counts, starts, sum(counts)


def pack_kernel(
    heights, bz, bx, material_ref, clamped_ref, table_ref, strain_ref, own_ref, brick_ref, edge_ref, label, joined, table, strain, sem
):
    copies = [
        pltpu.make_async_copy(material_ref, label, sem.at[0]),
        pltpu.make_async_copy(clamped_ref.at[pl.ds(0, 2)], joined, sem.at[1]),
        pltpu.make_async_copy(table_ref, table, sem.at[2]),
        pltpu.make_async_copy(strain_ref, strain, sem.at[3]),
    ]
    for copy in copies:
        copy.start()
    for copy in copies:
        copy.wait()
    for slot in range(bz + 2):
        src = label.at[slot] if slot < bz else joined.at[slot - bz]
        value = src[...].astype(F32)
        own_ref[pl.ds(slot * bx, bx), :] = value
        if slot < bz:
            brick_ref[pl.ds(slot * bx, bx), :] = value
    lower = lax.axis_index("height") < heights // 2
    edge_ref[...] = jnp.where(lower, label[bz - 1], label[0]).astype(F32)
    lane = lane_of(SPARE)
    row = jnp.zeros((SPARE, LANES), F32)
    for k in range(3):
        row = jnp.where(lane == k, table[k], row)
        for c in range(3):
            row = jnp.where(lane == 3 + 3 * c + k, table[k] * strain[k, c], row)
    own_ref[pl.ds((bz + 2) * bx, SPARE), :] = row


def gathered_rows(bz, bx):
    whole, brick = (bz + 2) * bx + SPARE, bz * bx
    return [0, whole, 2 * whole, 2 * whole + brick]


def place(heights, bz, bx, layer):
    h = lax.axis_index("height")
    z = bz * h - HALO + layer
    z_in = jnp.clip(z, 0, heights * bz - 1)
    brick, slot = z_in // bz, z_in % bz
    starts = gathered_rows(bz, bx)
    apart = jnp.abs(brick - h)
    paired = (brick // 2) == (h // 2)
    inner = jnp.where(apart == 0, starts[0], jnp.where(paired, starts[1], starts[2])) + slot * bx
    return z, jnp.where(apart > 1, starts[3], inner)


def spring_row(bz, bx):
    return jnp.where(lax.axis_index("height") == 0, 0, gathered_rows(bz, bx)[1]) + bz * bx


def strip_kernel(heights, bz, bx, x_ref, near_ref, far_ref):
    odd = (lax.axis_index("tile") & 1) == 1
    counts, starts, end = strips(bz)
    wanted = [(place(heights, bz, bx, layer)[1], count, start) for layer, (count, start) in enumerate(zip(counts, starts))]
    wanted += [(spring_row(bz, bx) + bx * k, HALO, end + HALO * k) for k in range(2)]
    for row, count, start in wanted:
        if count:
            first = x_ref[pl.ds(row, count), :]
            last = x_ref[pl.ds(row + bx - count, count), :]
            near_ref[pl.ds(start, count), :] = jnp.where(odd, first, last)
            far_ref[pl.ds(start, count), :] = jnp.where(odd, last, first)


def tables_of(x_ref, row):
    spare = x_ref[pl.ds(row, 1), :]
    table = [jnp.broadcast_to(spare[:, k : k + 1], (1, LANES)) for k in range(12)]
    return table[:3], [table[3 + 3 * c : 6 + 3 * c] for c in range(3)]


def store_layer(s, st, label, layer, to, weight, tables):
    is0, is1 = label == 0.0, label == 1.0
    dst = pl.ds(to, label.shape[0])
    for ref, values in zip((s, *(st.at[c] for c in range(3))), (tables[0], *tables[1])):
        a, b, c = (value * weight for value in values)
        ref[layer, dst, :] = jnp.where(is0, a, jnp.where(is1, b, c))


def store_strip(s, st, p, strip_ref, heights, bz, layer, far_side, valid, bx, tables):
    counts, starts, end = strips(bz)
    z, _ = place(heights, bz, bx, layer)
    weight = jnp.where((z >= 0) & (z < heights * bz), valid, 0.0)
    count = counts[layer]
    if count:
        to = jnp.where(far_side, 16 + bx, 16 - count)
        store_layer(s, st, strip_ref[pl.ds(starts[layer], count), :], layer, to, weight, tables)
    joined = strip_ref[pl.ds(end + HALO * jnp.clip(z, 0, 1), HALO), :]
    to = jnp.where(far_side, 16 + bx, 16 - HALO)
    p[layer, pl.ds(to, HALO), :] = joined * jnp.where((z >= 0) & (z < 2), 2.0 * PENALTY * valid, 0.0)


def fine_setup(s, p, st, b, r, d, g, y, layer, row, count):
    lane = lane_of(count)
    here = st[2, layer, pl.ds(row, count), :]
    source = [
        (rows_at(st.at[0], layer - 1, row, count) - rows_at(st.at[0], layer + 1, row, count)),
        (rows_at(st.at[1], layer, row - 1, count) - rows_at(st.at[1], layer, row + 1, count)),
        (jnp.where(lane < 1, 0.0, roll(here, 1)) - jnp.where(lane >= LANES - 1, 0.0, roll(here, -1))),
    ]
    for c in range(3):
        b[c, layer, pl.ds(row, count), :] = source[c]
    level_setup(s, p, r, d, g, y, lambda c: source[c], layer, row, count, 1)


def fine_down(bz, s, p, st, b, r, d, g, y, v, rest, rows, step):
    nz = bz + 2 * HALO

    def setup0(layer, carry):
        for row in rows[0]:
            fine_setup(s, p, st, b, r, d, g, y, layer, row, 16)
        return carry

    def sweep0(layer, carry):
        for row in rows[1]:
            first_sweep(s, y, r, g, v, layer, row, 16, 1)
        return carry

    def restrict0(j, carry):
        layer = 3 + 2 * j
        for row in rows[2]:
            one = remainder(s, y, b, d, v, layer, row, 16, 1)
            two = remainder(s, y, b, d, v, layer + 1, row, 16, 1)
            for c in range(3):
                rest[j, c, pl.ds(row, 16), :] = one[c] + two[c]
        return carry

    each(1, nz - 1, setup0, step)
    each(2, nz - 2, sweep0, step)
    each(0, bz // 2 + 6, restrict0, step)


def inner_kernel(heights, tiles, bz, bx, x_ref, near_ref, s, p, st, b, r, d, g, y, v, rest):
    t = lax.axis_index("tile")
    odd = (t & 1) == 1
    tables = tables_of(x_ref, (bz + 2) * bx)
    valid = jnp.where(odd | (t < tiles - 1), 1.0, 0.0)

    def read_layer(layer, carry):
        z, row = place(heights, bz, bx, layer)
        inside = jnp.where((z >= 0) & (z < heights * bz), 1.0, 0.0)
        store_layer(s, st, x_ref[pl.ds(row, bx), :], layer, 16, inside, tables)
        bottom = jnp.where((z >= 0) & (z < 2), 2.0 * PENALTY, 0.0)
        p[layer, pl.ds(16, bx), :] = x_ref[pl.ds(spring_row(bz, bx) + jnp.clip(z, 0, 1) * bx, bx), :] * bottom
        store_strip(s, st, p, near_ref, heights, bz, layer, jnp.logical_not(odd), valid, bx, tables)
        return carry

    each(0, bz + 2 * HALO, read_layer, bz + 2 * HALO + 1)
    rows = [[jnp.where(odd, 8 - k, 24 + k) + at for at in range(0, bx, 16)] for k in range(3)]
    fine_down(bz, s, p, st, b, r, d, g, y, v, rest, rows, 8)


def down_kernel(
    heights, tiles, bz, bx,
    x_ref, far_ref, *refs,
):
    send_ref, s1, y1, v1, g1, r1, s, p, st, b, r, d, g, y, v, rest, tmp, p1, b1, d1 = refs[10:]
    h, t = lax.axis_index("height"), lax.axis_index("tile")
    odd = (t & 1) == 1
    n1 = bz // 2 + 8
    bx1, bx2 = bx // 2, bx // 4
    low = 8
    tables = tables_of(x_ref, (bz + 2) * bx)
    valid = jnp.where(jnp.where(odd, t < tiles - 1, t > 0), 1.0, 0.0)

    def read_layer(layer, carry):
        store_strip(s, st, p, far_ref, heights, bz, layer, odd, valid, bx, tables)
        return carry

    each(0, bz + 2 * HALO, read_layer, bz + 2 * HALO + 1)
    rows = [[jnp.where(odd, bx + 8 - k, 8 + k)] for k in range(3)]
    fine_down(bz, s, p, st, b, r, d, g, y, v, rest, rows, 24)

    rows1 = bx1 + 8

    def restrict0(j, carry):
        for c in range(3):
            b1[c, j + 1, pl.ds(8, rows1), :] = pair_lanes(pair_rows(rest.at[j, c], low, rows1), 1)
        return carry

    each(0, n1 - 2, restrict0, 8)

    def coarse0(k, carry):
        for field, scale, into in ((s, 0.5, s1), (p, 1.0, p1)):
            both = [pair_rows(field.at[1 + 2 * k + i], low, rows1) for i in range(2)]
            into[k, pl.ds(8, rows1), :] = scale * pair_lanes(both[0] + both[1], 1)
        return carry

    each(0, n1, coarse0, 8)

    def setup1(layer, carry):
        level_setup(
            s1, p1, r1, d1, g1, y1,
            lambda c: b1[c, layer, pl.ds(8, rows1), :], layer, 8, rows1, 2,
        )
        return carry

    each(1, n1 - 1, setup1, 8)

    def sweep1(layer, carry):
        first_sweep(s1, y1, r1, g1, v1, layer, 8, rows1, 2)
        return carry

    each(2, n1 - 2, sweep1, 8)

    lane = lane_of(bx2) & 3
    packed = []
    for m in range(bz // 4):
        layer = 4 + 2 * m
        one = remainder(s1, y1, b1, d1, v1, layer, 8, rows1, 2)
        two = remainder(s1, y1, b1, d1, v1, layer + 1, 8, rows1, 2)
        fields = []
        for c in range(3):
            tmp[m, c, pl.ds(0, rows1), :] = one[c] + two[c]
            fields.append(pair_lanes(pair_rows(tmp.at[m, c], 4, bx2), 2))
        both = [pair_rows(s1.at[layer + i], 12, bx2) for i in range(2)]
        stiff = 0.5 * pair_lanes(both[0] + both[1], 2)
        packed.append(
            jnp.where(lane == 0, fields[0], jnp.where(lane == 1, fields[1], jnp.where(lane == 2, fields[2], stiff)))
        )
    bottom = jnp.maximum(bz // 2 * (1 - h), 0)
    both = [pair_rows(p1.at[bottom + i], 12, bx2) for i in range(2)]
    tmp[2, 0, pl.ds(0, bx2), :] = pair_lanes(both[0] + both[1], 2)
    quarter = bx2 // 8
    first = jnp.minimum(h, 1) * (bx2 // 2)
    part = [tmp[2, 0, pl.ds(first + j, quarter, stride=4), :] for j in range(4)]
    lane = lane_of(quarter) & 3
    packed.append(jnp.where(lane == 0, part[0], jnp.where(lane == 1, part[1], jnp.where(lane == 2, part[2], part[3]))))
    size = sum(value.shape[0] for value in packed)

    def fill(i, carry):
        at = i * size
        for value in packed:
            send_ref[pl.ds(at, value.shape[0]), :] = value
            at = at + value.shape[0]
        return carry

    each(0, heights * tiles, fill, 8)


def up_kernel(
    heights, tiles, bz, bx,
    recv_ref, s0, y0, v0, g0, r0, s1, y1, v1, g1, r1, out_ref,
    w0, w1, f1, s2, p2, b2, q2, r2, d2, g2, v2, f2, s3, p3, b3, q3, r3, g3, va, vb, rest2, tmp, done, sem,
):
    h, t = lax.axis_index("height"), lax.axis_index("tile")
    bx1, bx2, bz2 = bx // 2, bx // 4, bz // 4
    n1, n2, n3 = bz // 2 + 8, heights * bz // 4, heights * bz // 8
    rows1 = bx1 + 8
    near = pl.ds(8, bx + 16)
    mid = pl.ds(8, rows1)

    for ref in (s2, p2, g2, v2, f2, s3, p3, g3, va, vb):
        ref[...] = jnp.zeros(ref.shape, F32)
    rest2[...] = jnp.zeros(rest2.shape, F32)

    side = REACH // bx2
    size = bz2 * bx2 + bx2 // 8
    lane = lane_of(bx2) & 3
    for dt in range(-side, side + 1):
        other = t + dt
        valid = (other >= 0) & (other < tiles)
        other = jnp.clip(other, 0, tiles - 1)
        scale = jnp.where(valid, 1.0, 0.0)
        dst = pl.ds(8 + (dt + side) * bx2, bx2)
        for hh in range(heights):
            for m in range(bz2):
                x = recv_ref[pl.ds((other * heights + hh) * size + m * bx2, bx2), :] * scale
                layer = 1 + hh * bz2 + m
                b2[layer, dst, :] = jnp.where(lane == 3, 0.0, x)
                s2[layer, dst, :] = jnp.where(
                    lane == 3, x, jnp.where(lane == 2, roll(x, -1), jnp.where(lane == 1, roll(x, -2), roll(x, -3)))
                )
        quarter = bx2 // 8
        small = lane_of(quarter) & 3
        for hh in range(2):
            x = recv_ref[pl.ds((other * heights + hh) * size + bz2 * bx2, quarter), :] * scale
            moved = {shift: roll(x, shift) if shift else x for shift in range(-3, 4)}
            for j in range(4):
                row = 8 + (dt + side) * bx2 + hh * (bx2 // 2) + j
                p2[1, pl.ds(row, quarter, stride=4), :] = jnp.where(
                    small == 0, moved[-j], jnp.where(small == 1, moved[1 - j], jnp.where(small == 2, moved[2 - j], moved[3 - j]))
                )

    def weights(count):
        kind = lane_of(count) & 3
        return [jnp.where(kind == c, 2.0, 1.0) for c in range(3)]

    def setup(s_ref, p_ref, b_ref, q_ref, r_ref, d_ref, g_ref, layer, row, count, step):
        here, cross = cross_faces(s_ref, layer, row, count)
        low, high, low_in, high_in = lane_faces(here, step)
        w = weights(count)
        dst = pl.ds(row, count)
        for k in range(4):
            q_ref[k, layer, dst, :] = w[k // 2] * cross[k]
        q_ref[4, layer, dst, :] = w[2] * low_in
        q_ref[5, layer, dst, :] = w[2] * high_in
        doubled = rows_at(p_ref, layer, row, count) + (
            w[0] * (cross[0] + cross[1]) + w[1] * (cross[2] + cross[3]) + w[2] * (low + high)
        )
        rate = safe_rate(here, doubled)
        r_ref[layer, dst, :] = rate
        if d_ref is not None:
            d_ref[layer, dst, :] = doubled
        g_ref[layer, dst, :] = rate * rows_at(b_ref, layer, row, count)

    def packed_sum(v_ref, q_ref, layer, row, count, step):
        faces = [q_ref[k, layer, pl.ds(row, count), :] for k in range(6)]
        here, along = neighbours(v_ref, faces, layer, row, count, step)
        return here, along[0] + along[1] + along[2]

    rows2 = bx2 + 2 * REACH

    def setup2(layer, carry):
        setup(s2, p2, b2, q2, r2, d2, g2, layer, 8, rows2, 4)
        return carry

    each(1, n2 + 1, setup2, 8)

    def sweep2(layer, carry):
        here, total_ = packed_sum(g2, q2, layer, 8, rows2, 4)
        v2[layer, pl.ds(8, rows2), :] = (2.0 - OMEGA) * here + rows_at(r2, layer, 8, rows2) * total_
        return carry

    each(1, n2 + 1, sweep2, 8)

    rows3 = -(-(rows2 // 2) // 8) * 8

    def restrict2(j, carry):
        rest = 0.0
        for i in range(2):
            layer = 1 + 2 * j + i
            here, total_ = packed_sum(v2, q2, layer, 8, rows2, 4)
            rest = rest + rows_at(b2, layer, 8, rows2) + (total_ - rows_at(d2, layer, 8, rows2) * here)
        rest2[j, pl.ds(8, rows2), :] = rest
        dst = pl.ds(8, rows3)
        b3[j + 1, dst, :] = pair_lanes(pair_rows(rest2.at[j], 8, rows3), 4)
        for field, scale, into in ((s2, 0.5, s3), (p2, 1.0, p3)):
            both = [pair_rows(field.at[1 + 2 * j + i], 8, rows3) for i in range(2)]
            into[j + 1, dst, :] = scale * pair_lanes(both[0] + both[1], 4)
        return carry

    each(0, n3, restrict2, 8)

    for layer in range(1, n3 + 1):
        setup(s3, p3, b3, q3, r3, None, g3, layer, 8, rows3, 8)
    source, target = g3, va
    for _ in range(COARSE_SWEEPS - 1):
        for layer in range(1, n3 + 1):
            here, total_ = packed_sum(source, q3, layer, 8, rows3, 8)
            target[layer, pl.ds(8, rows3), :] = (
                (1.0 - OMEGA) * here + rows_at(g3, layer, 8, rows3) + rows_at(r3, layer, 8, rows3) * total_
            )
        source, target = target, (vb if target is va else va)
    coarse = source

    wide2 = bx2 + 16

    def lift2(layer, carry):
        spread_rows(tmp.at[layer - 1], coarse[(layer + 1) // 2, pl.ds(12, wide2 // 2), :])
        v2[layer, pl.ds(16, wide2), :] += tmp[layer - 1, pl.ds(0, wide2), :]
        return carry

    each(1, n2 + 1, lift2, 8)

    def post2(layer, carry):
        here, total_ = packed_sum(v2, q2, layer, 16, wide2, 4)
        f2[layer, pl.ds(16, wide2), :] = (
            (1.0 - OMEGA) * here + rows_at(g2, layer, 16, wide2) + rows_at(r2, layer, 16, wide2) * total_
        )
        return carry

    each(1, n2 + 1, post2, 8)

    kind = lane_of(bx2 + 4) & 3

    def lift1(m, carry):
        x = f2[bz2 * h + m, pl.ds(22, bx2 + 4), :]
        moved = {shift: roll(x, shift) if shift else x for shift in range(-2, 4)}
        for c in range(3):
            part = jnp.where(
                kind == 0, moved[-c], jnp.where(kind == 1, moved[1 - c], jnp.where(kind == 2, moved[2 - c], moved[3 - c]))
            )
            spread_rows(tmp.at[3 * m + c], part)
            lifted = tmp[3 * m + c, pl.ds(0, rows1), :]
            for i in range(2):
                w1[c, 2 + 2 * m + i, mid, :] = v1[c, 2 + 2 * m + i, mid, :] + lifted
        return carry

    each(0, n1 // 2 - 2, lift1, 8)

    def post(s_ref, y_ref, g_ref, r_ref, v_ref, into, layer, row, count, step):
        faces = all_faces(s_ref, y_ref, layer, row, count)
        for c in range(3):
            here, along = neighbours(v_ref.at[c], faces, layer, row, count, step)
            dst = pl.ds(row, count)
            into(c, (1.0 - OMEGA) * here + g_ref[c, layer, dst, :] + r_ref[c, layer, dst, :] * total(along, c))

    def post1(layer, carry):
        def into(c, value):
            f1[c, layer, mid, :] = value

        post(s1, y1, g1, r1, w1, into, layer, 8, rows1, 2)
        return carry

    each(3, n1 - 3, post1, 8)

    for k in range(3, n1 - 3):
        for c in range(3):
            slot = 3 * (k - 3) + c
            spread_rows(tmp.at[slot], f1[c, k, mid, :])
            lifted = tmp[slot, pl.ds(0, bx + 16), :]
            for layer in (2 * k + 1, 2 * k + 2):
                if HALO - 1 <= layer <= HALO + bz:
                    w0[c, layer, near, :] = v0[c, layer, near, :] + lifted

    started = []
    for layer in range(HALO, HALO + bz):
        z = layer - HALO
        for row, count in chunks(16, 16 + bx, 16):

            def into(c, value):
                done[c, z, pl.ds(row - 16, count), :] = value

            post(s0, y0, g0, r0, w0, into, layer, row, count, 1)
        started.append(pltpu.make_async_copy(done.at[:, z], out_ref.at[:, z], sem.at[z]))
        started[-1].start()
    for copy in started:
        copy.wait()


def swapped(x, axis, start):
    pairs = [(i, i + 1) for i in range(start, lax.axis_size(axis) - 1, 2)]
    return lax.ppermute(x, axis, pairs + [(j, i) for i, j in pairs])


def vmem(*shape):
    return pltpu.VMEM(shape, F32)


def local(heights, tiles, material, clamped, stiffness_table, eigenstrain):
    bz, bx, _ = material.shape

    held = pl.BlockSpec(memory_space=pltpu.VMEM)
    outside = pl.BlockSpec(memory_space=pltpu.HBM)
    own, brick, edge = pl.pallas_call(
        functools.partial(pack_kernel, heights, bz, bx),
        out_shape=[pltpu.VMEM((rows, LANES), F32) for rows in ((bz + 2) * bx + SPARE, bz * bx, bx)],
        in_specs=[outside] * 4,
        out_specs=[held] * 3,
        scratch_shapes=[
            pltpu.VMEM((bz, bx, LANES), jnp.int32), pltpu.VMEM((2, bx, LANES), jnp.int32),
            pltpu.SMEM((3,), F32), pltpu.SMEM((3, 3), F32), pltpu.SemaphoreType.DMA((4,)),
        ],
    )(material, clamped, stiffness_table, eigenstrain)
    beside = swapped(brick, "height", 1)
    beyond = lax.ppermute(edge, "height", [(i, (i + 2) % heights) for i in range(heights)])
    paired = swapped(own, "height", 0)
    bricks = jnp.concatenate([own, paired, beside, beyond], 0)
    strip = pltpu.VMEM((-(-(strips(bz)[2] + 2 * HALO) // 8) * 8, LANES), F32)
    near, far = pl.pallas_call(
        functools.partial(strip_kernel, heights, bz, bx),
        out_shape=[strip, strip],
        in_specs=[held],
        out_specs=[held, held],
        compiler_params=pltpu.CompilerParams(vmem_limit_bytes=4 * 2**20),
    )(bricks)
    far = swapped(far, "tile", 1)
    near = swapped(near, "tile", 0)

    bx1, bx2 = bx // 2, bx // 4
    nz, n1 = bz + 2 * HALO, bz // 2 + 8
    r0, r1 = bx + 32, bx1 + 24
    rows1 = bx1 + 8
    field0, field1 = (nz, r0, LANES), (n1, r1, LANES)
    fields = [field0, field0, (3, *field0), (3, *field0), (3, *field0), (3, *field0), (3, *field0), (2, *field0), (3, *field0)]
    fields = [pltpu.VMEM(shape, F32) for shape in [*fields, (n1 - 2, 3, r0, LANES)]]
    work = 24 * 6 * 3 * 1024
    inner = pl.pallas_call(
        functools.partial(inner_kernel, heights, tiles, bz, bx),
        out_shape=fields,
        in_specs=[held] * 2,
        out_specs=[held] * len(fields),
        cost_estimate=pl.CostEstimate(flops=work * 60, bytes_accessed=work * 40, transcendentals=0),
        compiler_params=pltpu.CompilerParams(vmem_limit_bytes=4 * 2**20),
    )(bricks, near)
    kept = [field1, (2, *field1), (3, *field1), (3, *field1), (3, *field1)]
    kept = [pltpu.VMEM(shape, F32) for shape in kept]
    send, s1, y1, v1, g1, r1_, s, _, _, _, r, _, g, y, v, _ = pl.pallas_call(
        functools.partial(down_kernel, heights, tiles, bz, bx),
        out_shape=[
            pltpu.VMEM((heights * tiles * (bz // 4 * bx2 + bx2 // 8), LANES), F32), *kept, *fields
        ],
        in_specs=[held] * (2 + len(fields)),
        out_specs=[held] * (1 + len(kept) + len(fields)),
        input_output_aliases={2 + k: 1 + len(kept) + k for k in range(len(fields))},
        scratch_shapes=[vmem(n1 - 2, 3, r0, LANES), vmem(*field1), vmem(3, *field1), vmem(3, *field1)],
        compiler_params=pltpu.CompilerParams(vmem_limit_bytes=8 * 2**20),
    )(bricks, far, *inner)

    blocks = send.reshape(heights * tiles, -1, 1, LANES)
    received = lax.all_to_all(blocks, ("tile", "height"), 0, 0).reshape(send.shape)

    rows2 = bx2 + 2 * REACH
    rows3 = -(-(rows2 // 2) // 8) * 8
    up2 = (heights * bz // 4 + 2, rows2 + 16, LANES)
    up3 = (heights * bz // 8 + 2, rows3 + 16, LANES)
    return pl.pallas_call(
        functools.partial(up_kernel, heights, tiles, bz, bx),
        out_shape=jax.ShapeDtypeStruct((3, bz, bx, LANES), F32),
        in_specs=[held] * 11,
        out_specs=outside,
        scratch_shapes=[
            vmem(3, *field0), vmem(3, *field1), vmem(3, *field1),
            vmem(*up2), vmem(*up2), vmem(*up2), vmem(6, *up2), vmem(*up2), vmem(*up2), vmem(*up2), vmem(*up2), vmem(*up2),
            vmem(*up3), vmem(*up3), vmem(*up3), vmem(6, *up3), vmem(*up3), vmem(*up3), vmem(*up3), vmem(*up3),
            vmem(heights * bz // 8, rows2 + 24, LANES), vmem(max(heights * bz // 4, 3 * (n1 - 6)), r0, LANES),
            vmem(3, bz, bx, LANES), pltpu.SemaphoreType.DMA((bz,)),
        ],
        compiler_params=pltpu.CompilerParams(vmem_limit_bytes=16 * 2**20),
    )(received, s, y, v, g, r, s1, y1, v1, g1, r1_)


def solution(mesh):
    sides = mesh.shape["height"], mesh.shape["tile"]
    in_specs = (P("height", "tile", None), P("height", "tile", None), P(), P())
    out_specs = P(None, "height", "tile", None)
    return jax.shard_map(
        functools.partial(local, *sides), mesh=mesh, in_specs=in_specs, out_specs=out_specs, check_vma=False
    )
```

```python
import functools

import jax
import jax.numpy as jnp
from jax import lax
from jax.experimental import pallas as pl
from jax.experimental.pallas import tpu as pltpu
from jax.sharding import PartitionSpec as P

PENALTY = 50.0
OMEGA = 0.6
COARSE_SWEEPS = 6
LANES = 128
HALO = 9
REACH = 16
SPARE = 4
F32 = jnp.float32


def each(start, stop, body, step):
    groups = (stop - start) // step

    def group(i, carry):
        for k in range(step):
            body(start + i * step + k, 0)
        return carry

    if groups > 1:
        lax.fori_loop(0, groups, group, 0)
    elif groups == 1:
        group(0, 0)
    for layer in range(start + groups * step, stop):
        body(layer, 0)


def chunks(start, stop, size):
    return [(row, min(size, stop - row)) for row in range(start, stop, size)]


def lane_of(rows):
    return lax.broadcasted_iota(jnp.int32, (rows, LANES), 1)


def roll(x, shift):
    return pltpu.roll(x, shift % LANES, 1)


def rows_at(ref, layer, row, count):
    return ref[layer, pl.ds(row, count), :]


def cross_faces(s_ref, layer, row, count):
    here = rows_at(s_ref, layer, row, count)
    return here, [
        here + rows_at(s_ref, layer - 1, row, count),
        here + rows_at(s_ref, layer + 1, row, count),
        here + rows_at(s_ref, layer, row - 1, count),
        here + rows_at(s_ref, layer, row + 1, count),
    ]


def lane_faces(here, step):
    lane = lane_of(here.shape[0])
    first, last = lane < step, lane >= LANES - step
    low = here + jnp.where(first, 0.0, roll(here, step))
    high = here + jnp.where(last, 0.0, roll(here, -step))
    return low, high, jnp.where(first, 0.0, low), jnp.where(last, 0.0, high)


def neighbours(v_ref, faces, layer, row, count, step):
    here = rows_at(v_ref, layer, row, count)
    along = [
        faces[0] * rows_at(v_ref, layer - 1, row, count)
        + faces[1] * rows_at(v_ref, layer + 1, row, count),
        faces[2] * rows_at(v_ref, layer, row - 1, count)
        + faces[3] * rows_at(v_ref, layer, row + 1, count),
        faces[4] * roll(here, step) + faces[5] * roll(here, -step),
    ]
    return here, along


def total(along, component):
    return (along[0] + along[1] + along[2]) + along[component]


def safe_rate(here, doubled):
    return jnp.where(here > 0.0, OMEGA / doubled, 0.0)


def pair_lanes(x, step):
    upper = (lane_of(x.shape[0]) & step) != 0
    return x + jnp.where(upper, roll(x, step), roll(x, -step))


def pair_rows(ref, row, count):
    return ref[pl.ds(row, count, stride=2), :] + ref[pl.ds(row + 1, count, stride=2), :]


def spread_rows(ref, x):
    count = x.shape[0]
    ref[pl.ds(0, count, stride=2), :] = x
    ref[pl.ds(1, count, stride=2), :] = x


def level_setup(s_ref, p_ref, r_ref, d_ref, g_ref, y_ref, b_of, layer, row, count, step):
    here, cross = cross_faces(s_ref, layer, row, count)
    low, high, low_in, high_in = lane_faces(here, step)
    y_ref[0, layer, pl.ds(row, count), :] = low_in
    y_ref[1, layer, pl.ds(row, count), :] = high_in
    sums = [cross[0] + cross[1], cross[2] + cross[3], low + high]
    base = rows_at(p_ref, layer, row, count) + (sums[0] + sums[1] + sums[2])
    for c in range(3):
        doubled = base + sums[c]
        rate = safe_rate(here, doubled)
        d_ref[c, layer, pl.ds(row, count), :] = doubled
        r_ref[c, layer, pl.ds(row, count), :] = rate
        g_ref[c, layer, pl.ds(row, count), :] = rate * b_of(c)


def all_faces(s_ref, y_ref, layer, row, count):
    _, cross = cross_faces(s_ref, layer, row, count)
    return cross + [
        y_ref[0, layer, pl.ds(row, count), :],
        y_ref[1, layer, pl.ds(row, count), :],
    ]


def first_sweep(s_ref, y_ref, r_ref, g_ref, v_ref, layer, row, count, step):
    faces = all_faces(s_ref, y_ref, layer, row, count)
    for c in range(3):
        here, along = neighbours(g_ref.at[c], faces, layer, row, count, step)
        rate = r_ref[c, layer, pl.ds(row, count), :]
        v_ref[c, layer, pl.ds(row, count), :] = (2.0 - OMEGA) * here + rate * total(along, c)


def remainder(s_ref, y_ref, b_ref, d_ref, v_ref, layer, row, count, step):
    faces = all_faces(s_ref, y_ref, layer, row, count)
    result = []
    for c in range(3):
        here, along = neighbours(v_ref.at[c], faces, layer, row, count, step)
        doubled = d_ref[c, layer, pl.ds(row, count), :]
        source = b_ref[c, layer, pl.ds(row, count), :]
        result.append(source + (total(along, c) - doubled * here))
    return result


def strips(bz):
    counts = [min(layer, HALO, bz + 2 * HALO - 1 - layer) for layer in range(bz + 2 * HALO)]
    starts = [sum(counts[:layer]) for layer in range(len(counts))]
    return counts, starts, sum(counts)


def pack_kernel(
    heights, bz, bx, material_ref, clamped_ref, table_ref, strain_ref, own_ref, brick_ref, edge_ref, label, joined, table, strain, sem
):
    copies = [
        pltpu.make_async_copy(material_ref, label, sem.at[0]),
        pltpu.make_async_copy(clamped_ref.at[pl.ds(0, 2)], joined, sem.at[1]),
        pltpu.make_async_copy(table_ref, table, sem.at[2]),
        pltpu.make_async_copy(strain_ref, strain, sem.at[3]),
    ]
    for copy in copies:
        copy.start()
    for copy in copies:
        copy.wait()
    for slot in range(bz + 2):
        src = label.at[slot] if slot < bz else joined.at[slot - bz]
        value = src[...].astype(F32)
        own_ref[pl.ds(slot * bx, bx), :] = value
        if slot < bz:
            brick_ref[pl.ds(slot * bx, bx), :] = value
    lower = lax.axis_index("height") < heights // 2
    edge_ref[...] = jnp.where(lower, label[bz - 1], label[0]).astype(F32)
    lane = lane_of(SPARE)
    row = jnp.zeros((SPARE, LANES), F32)
    for k in range(3):
        row = jnp.where(lane == k, table[k], row)
        for c in range(3):
            row = jnp.where(lane == 3 + 3 * c + k, table[k] * strain[k, c], row)
    own_ref[pl.ds((bz + 2) * bx, SPARE), :] = row


def gathered_rows(bz, bx):
    whole, brick = (bz + 2) * bx + SPARE, bz * bx
    return [0, whole, 2 * whole, 2 * whole + brick]


def place(bz, bx, layer):
    h = lax.axis_index("height")
    own, paired, beside, beyond = gathered_rows(bz, bx)
    even = (h & 1) == 0
    if layer in (0, bz + 2 * HALO - 1):
        row = beyond
    elif layer < HALO:
        row = jnp.where(even, beside, paired) + (bz - HALO + layer) * bx
    elif layer < HALO + bz:
        row = own + (layer - HALO) * bx
    else:
        row = jnp.where(even, paired, beside) + (layer - HALO - bz) * bx
    return bz * h - HALO + layer, row


def spring_row(bz, bx):
    return jnp.where(lax.axis_index("height") == 0, 0, gathered_rows(bz, bx)[1]) + bz * bx


def strip_kernel(heights, bz, bx, x_ref, near_ref, far_ref):
    odd = (lax.axis_index("tile") & 1) == 1
    counts, starts, end = strips(bz)
    wanted = [(place(bz, bx, layer)[1], count, start) for layer, (count, start) in enumerate(zip(counts, starts))]
    wanted += [(spring_row(bz, bx) + bx * k, HALO, end + HALO * k) for k in range(2)]
    for row, count, start in wanted:
        if count:
            first = x_ref[pl.ds(row, count), :]
            last = x_ref[pl.ds(row + bx - count, count), :]
            near_ref[pl.ds(start, count), :] = jnp.where(odd, first, last)
            far_ref[pl.ds(start, count), :] = jnp.where(odd, last, first)


def tables_of(x_ref, row):
    spare = x_ref[pl.ds(row, 1), :]
    table = [jnp.broadcast_to(spare[:, k : k + 1], (1, LANES)) for k in range(12)]
    return table[:3], [table[3 + 3 * c : 6 + 3 * c] for c in range(3)]


def store_layer(s, st, label, layer, to, weight, tables):
    is0, is1 = label == 0.0, label == 1.0
    dst = pl.ds(to, label.shape[0])
    for ref, values in zip((s, *(st.at[c] for c in range(3))), (tables[0], *tables[1])):
        a, b, c = (value * weight for value in values)
        ref[layer, dst, :] = jnp.where(is0, a, jnp.where(is1, b, c))


def store_strip(s, st, p, strip_ref, heights, bz, layer, far_side, valid, bx, tables):
    counts, starts, end = strips(bz)
    z, _ = place(bz, bx, layer)
    weight = jnp.where((z >= 0) & (z < heights * bz), valid, 0.0)
    count = counts[layer]
    if count:
        to = jnp.where(far_side, 16 + bx, 16 - count)
        store_layer(s, st, strip_ref[pl.ds(starts[layer], count), :], layer, to, weight, tables)
    joined = strip_ref[pl.ds(end + HALO * jnp.clip(z, 0, 1), HALO), :]
    to = jnp.where(far_side, 16 + bx, 16 - HALO)
    p[layer, pl.ds(to, HALO), :] = joined * jnp.where((z >= 0) & (z < 2), 2.0 * PENALTY * valid, 0.0)


def fine_setup(s, p, st, b, r, d, g, y, layer, row, count):
    lane = lane_of(count)
    here = st[2, layer, pl.ds(row, count), :]
    source = [
        (rows_at(st.at[0], layer - 1, row, count) - rows_at(st.at[0], layer + 1, row, count)),
        (rows_at(st.at[1], layer, row - 1, count) - rows_at(st.at[1], layer, row + 1, count)),
        (jnp.where(lane < 1, 0.0, roll(here, 1)) - jnp.where(lane >= LANES - 1, 0.0, roll(here, -1))),
    ]
    for c in range(3):
        b[c, layer, pl.ds(row, count), :] = source[c]
    level_setup(s, p, r, d, g, y, lambda c: source[c], layer, row, count, 1)


def fine_down(bz, s, p, st, b, r, d, g, y, v, rest, rows, step):
    nz = bz + 2 * HALO

    def setup0(layer, carry):
        for row in rows[0]:
            fine_setup(s, p, st, b, r, d, g, y, layer, row, 16)
        return carry

    def sweep0(layer, carry):
        for row in rows[1]:
            first_sweep(s, y, r, g, v, layer, row, 16, 1)
        return carry

    def restrict0(j, carry):
        layer = 3 + 2 * j
        for row in rows[2]:
            one = remainder(s, y, b, d, v, layer, row, 16, 1)
            two = remainder(s, y, b, d, v, layer + 1, row, 16, 1)
            for c in range(3):
                rest[j, c, pl.ds(row, 16), :] = one[c] + two[c]
        return carry

    each(1, nz - 1, setup0, step or 12)
    each(2, nz - 2, sweep0, step or 11)
    each(0, bz // 2 + 6, restrict0, step or 5)


def inner_kernel(heights, tiles, bz, bx, x_ref, near_ref, s, p, st, b, r, d, g, y, v, rest):
    t = lax.axis_index("tile")
    odd = (t & 1) == 1
    tables = tables_of(x_ref, (bz + 2) * bx)
    valid = jnp.where(odd | (t < tiles - 1), 1.0, 0.0)

    def read_layer(layer, carry):
        z, row = place(bz, bx, layer)
        inside = jnp.where((z >= 0) & (z < heights * bz), 1.0, 0.0)
        store_layer(s, st, x_ref[pl.ds(row, bx), :], layer, 16, inside, tables)
        bottom = jnp.where((z >= 0) & (z < 2), 2.0 * PENALTY, 0.0)
        p[layer, pl.ds(16, bx), :] = x_ref[pl.ds(spring_row(bz, bx) + jnp.clip(z, 0, 1) * bx, bx), :] * bottom
        store_strip(s, st, p, near_ref, heights, bz, layer, jnp.logical_not(odd), valid, bx, tables)
        return carry

    each(0, bz + 2 * HALO, read_layer, bz + 2 * HALO + 1)
    rows = [[jnp.where(odd, 8 - k, 24 + k) + at for at in range(0, bx, 16)] for k in range(3)]
    fine_down(bz, s, p, st, b, r, d, g, y, v, rest, rows, 0)


def down_kernel(
    heights, tiles, bz, bx,
    x_ref, far_ref, *refs,
):
    send_ref, s1, y1, v1, g1, r1, s, p, st, b, r, d, g, y, v, rest, tmp, p1, b1, d1 = refs[10:]
    h, t = lax.axis_index("height"), lax.axis_index("tile")
    odd = (t & 1) == 1
    n1 = bz // 2 + 8
    bx1, bx2 = bx // 2, bx // 4
    low = 8
    tables = tables_of(x_ref, (bz + 2) * bx)
    valid = jnp.where(jnp.where(odd, t < tiles - 1, t > 0), 1.0, 0.0)

    def read_layer(layer, carry):
        store_strip(s, st, p, far_ref, heights, bz, layer, odd, valid, bx, tables)
        return carry

    each(0, bz + 2 * HALO, read_layer, bz + 2 * HALO + 1)
    rows = [[jnp.where(odd, bx + 8 - k, 8 + k)] for k in range(3)]
    fine_down(bz, s, p, st, b, r, d, g, y, v, rest, rows, 12)

    rows1 = bx1 + 8

    def restrict0(j, carry):
        for c in range(3):
            b1[c, j + 1, pl.ds(8, rows1), :] = pair_lanes(pair_rows(rest.at[j, c], low, rows1), 1)
        return carry

    each(0, n1 - 2, restrict0, 8)

    def coarse0(k, carry):
        for field, scale, into in ((s, 0.5, s1), (p, 1.0, p1)):
            both = [pair_rows(field.at[1 + 2 * k + i], low, rows1) for i in range(2)]
            into[k, pl.ds(8, rows1), :] = scale * pair_lanes(both[0] + both[1], 1)
        return carry

    each(0, n1, coarse0, 8)

    def setup1(layer, carry):
        level_setup(
            s1, p1, r1, d1, g1, y1,
            lambda c: b1[c, layer, pl.ds(8, rows1), :], layer, 8, rows1, 2,
        )
        return carry

    each(1, n1 - 1, setup1, 8)

    def sweep1(layer, carry):
        first_sweep(s1, y1, r1, g1, v1, layer, 8, rows1, 2)
        return carry

    each(2, n1 - 2, sweep1, 8)

    lane = lane_of(bx2) & 3
    packed = []
    for m in range(bz // 4):
        layer = 4 + 2 * m
        one = remainder(s1, y1, b1, d1, v1, layer, 8, rows1, 2)
        two = remainder(s1, y1, b1, d1, v1, layer + 1, 8, rows1, 2)
        fields = []
        for c in range(3):
            tmp[m, c, pl.ds(0, rows1), :] = one[c] + two[c]
            fields.append(pair_lanes(pair_rows(tmp.at[m, c], 4, bx2), 2))
        both = [pair_rows(s1.at[layer + i], 12, bx2) for i in range(2)]
        stiff = 0.5 * pair_lanes(both[0] + both[1], 2)
        packed.append(
            jnp.where(lane == 0, fields[0], jnp.where(lane == 1, fields[1], jnp.where(lane == 2, fields[2], stiff)))
        )
    bottom = jnp.maximum(bz // 2 * (1 - h), 0)
    both = [pair_rows(p1.at[bottom + i], 12, bx2) for i in range(2)]
    tmp[2, 0, pl.ds(0, bx2), :] = pair_lanes(both[0] + both[1], 2)
    quarter = bx2 // 8
    first = jnp.minimum(h, 1) * (bx2 // 2)
    part = [tmp[2, 0, pl.ds(first + j, quarter, stride=4), :] for j in range(4)]
    lane = lane_of(quarter) & 3
    packed.append(jnp.where(lane == 0, part[0], jnp.where(lane == 1, part[1], jnp.where(lane == 2, part[2], part[3]))))
    size = sum(value.shape[0] for value in packed)

    def fill(i, carry):
        at = i * size
        for value in packed:
            send_ref[pl.ds(at, value.shape[0]), :] = value
            at = at + value.shape[0]
        return carry

    each(0, heights * tiles, fill, 8)


def up_kernel(
    heights, tiles, bz, bx,
    recv_ref, s0, y0, v0, g0, r0, s1, y1, v1, g1, r1, out_ref,
    w0, w1, f1, s2, p2, b2, q2, r2, d2, g2, v2, f2, s3, p3, b3, q3, r3, g3, va, vb, rest2, tmp, done, sem,
):
    h, t = lax.axis_index("height"), lax.axis_index("tile")
    bx1, bx2, bz2 = bx // 2, bx // 4, bz // 4
    n1, n2, n3 = bz // 2 + 8, heights * bz // 4, heights * bz // 8
    rows1 = bx1 + 8
    near = pl.ds(8, bx + 16)
    mid = pl.ds(8, rows1)

    for ref in (s2, p2, g2, v2, f2, s3, p3, g3, va, vb):
        ref[...] = jnp.zeros(ref.shape, F32)
    rest2[...] = jnp.zeros(rest2.shape, F32)

    side = REACH // bx2
    size = bz2 * bx2 + bx2 // 8
    lane = lane_of(bx2) & 3
    for dt in range(-side, side + 1):
        other = t + dt
        valid = (other >= 0) & (other < tiles)
        other = jnp.clip(other, 0, tiles - 1)
        scale = jnp.where(valid, 1.0, 0.0)
        dst = pl.ds(8 + (dt + side) * bx2, bx2)
        for hh in range(heights):
            for m in range(bz2):
                x = recv_ref[pl.ds((other * heights + hh) * size + m * bx2, bx2), :] * scale
                layer = 1 + hh * bz2 + m
                b2[layer, dst, :] = jnp.where(lane == 3, 0.0, x)
                s2[layer, dst, :] = jnp.where(
                    lane == 3, x, jnp.where(lane == 2, roll(x, -1), jnp.where(lane == 1, roll(x, -2), roll(x, -3)))
                )
        quarter = bx2 // 8
        small = lane_of(quarter) & 3
        for hh in range(2):
            x = recv_ref[pl.ds((other * heights + hh) * size + bz2 * bx2, quarter), :] * scale
            moved = {shift: roll(x, shift) if shift else x for shift in range(-3, 4)}
            for j in range(4):
                row = 8 + (dt + side) * bx2 + hh * (bx2 // 2) + j
                p2[1, pl.ds(row, quarter, stride=4), :] = jnp.where(
                    small == 0, moved[-j], jnp.where(small == 1, moved[1 - j], jnp.where(small == 2, moved[2 - j], moved[3 - j]))
                )

    def weights(count):
        kind = lane_of(count) & 3
        return [jnp.where(kind == c, 2.0, 1.0) for c in range(3)]

    def setup(s_ref, p_ref, b_ref, q_ref, r_ref, d_ref, g_ref, layer, row, count, step):
        here, cross = cross_faces(s_ref, layer, row, count)
        low, high, low_in, high_in = lane_faces(here, step)
        w = weights(count)
        dst = pl.ds(row, count)
        for k in range(4):
            q_ref[k, layer, dst, :] = w[k // 2] * cross[k]
        q_ref[4, layer, dst, :] = w[2] * low_in
        q_ref[5, layer, dst, :] = w[2] * high_in
        doubled = rows_at(p_ref, layer, row, count) + (
            w[0] * (cross[0] + cross[1]) + w[1] * (cross[2] + cross[3]) + w[2] * (low + high)
        )
        rate = safe_rate(here, doubled)
        r_ref[layer, dst, :] = rate
        if d_ref is not None:
            d_ref[layer, dst, :] = doubled
        g_ref[layer, dst, :] = rate * rows_at(b_ref, layer, row, count)

    def packed_sum(v_ref, q_ref, layer, row, count, step):
        faces = [q_ref[k, layer, pl.ds(row, count), :] for k in range(6)]
        here, along = neighbours(v_ref, faces, layer, row, count, step)
        return here, along[0] + along[1] + along[2]

    rows2 = bx2 + 2 * REACH

    def setup2(layer, carry):
        setup(s2, p2, b2, q2, r2, d2, g2, layer, 8, rows2, 4)
        return carry

    each(1, n2 + 1, setup2, 8)

    def sweep2(layer, carry):
        here, total_ = packed_sum(g2, q2, layer, 8, rows2, 4)
        v2[layer, pl.ds(8, rows2), :] = (2.0 - OMEGA) * here + rows_at(r2, layer, 8, rows2) * total_
        return carry

    each(1, n2 + 1, sweep2, 8)

    rows3 = -(-(rows2 // 2) // 8) * 8

    def restrict2(j, carry):
        rest = 0.0
        for i in range(2):
            layer = 1 + 2 * j + i
            here, total_ = packed_sum(v2, q2, layer, 8, rows2, 4)
            rest = rest + rows_at(b2, layer, 8, rows2) + (total_ - rows_at(d2, layer, 8, rows2) * here)
        rest2[j, pl.ds(8, rows2), :] = rest
        dst = pl.ds(8, rows3)
        b3[j + 1, dst, :] = pair_lanes(pair_rows(rest2.at[j], 8, rows3), 4)
        for field, scale, into in ((s2, 0.5, s3), (p2, 1.0, p3)):
            both = [pair_rows(field.at[1 + 2 * j + i], 8, rows3) for i in range(2)]
            into[j + 1, dst, :] = scale * pair_lanes(both[0] + both[1], 4)
        return carry

    each(0, n3, restrict2, 8)

    for layer in range(1, n3 + 1):
        setup(s3, p3, b3, q3, r3, None, g3, layer, 8, rows3, 8)
    source, target = g3, va
    for _ in range(COARSE_SWEEPS - 1):
        for layer in range(1, n3 + 1):
            here, total_ = packed_sum(source, q3, layer, 8, rows3, 8)
            target[layer, pl.ds(8, rows3), :] = (
                (1.0 - OMEGA) * here + rows_at(g3, layer, 8, rows3) + rows_at(r3, layer, 8, rows3) * total_
            )
        source, target = target, (vb if target is va else va)
    coarse = source

    wide2 = bx2 + 16

    def lift2(layer, carry):
        spread_rows(tmp.at[layer - 1], coarse[(layer + 1) // 2, pl.ds(12, wide2 // 2), :])
        v2[layer, pl.ds(16, wide2), :] += tmp[layer - 1, pl.ds(0, wide2), :]
        return carry

    each(1, n2 + 1, lift2, 8)

    def post2(layer, carry):
        here, total_ = packed_sum(v2, q2, layer, 16, wide2, 4)
        f2[layer, pl.ds(16, wide2), :] = (
            (1.0 - OMEGA) * here + rows_at(g2, layer, 16, wide2) + rows_at(r2, layer, 16, wide2) * total_
        )
        return carry

    each(1, n2 + 1, post2, 8)

    kind = lane_of(bx2 + 4) & 3

    def lift1(m, carry):
        x = f2[bz2 * h + m, pl.ds(22, bx2 + 4), :]
        moved = {shift: roll(x, shift) if shift else x for shift in range(-2, 4)}
        for c in range(3):
            part = jnp.where(
                kind == 0, moved[-c], jnp.where(kind == 1, moved[1 - c], jnp.where(kind == 2, moved[2 - c], moved[3 - c]))
            )
            spread_rows(tmp.at[3 * m + c], part)
            lifted = tmp[3 * m + c, pl.ds(0, rows1), :]
            for i in range(2):
                w1[c, 2 + 2 * m + i, mid, :] = v1[c, 2 + 2 * m + i, mid, :] + lifted
        return carry

    each(0, n1 // 2 - 2, lift1, 8)

    def post(s_ref, y_ref, g_ref, r_ref, v_ref, into, layer, row, count, step):
        faces = all_faces(s_ref, y_ref, layer, row, count)
        for c in range(3):
            here, along = neighbours(v_ref.at[c], faces, layer, row, count, step)
            dst = pl.ds(row, count)
            into(c, (1.0 - OMEGA) * here + g_ref[c, layer, dst, :] + r_ref[c, layer, dst, :] * total(along, c))

    def post1(layer, carry):
        def into(c, value):
            f1[c, layer, mid, :] = value

        post(s1, y1, g1, r1, w1, into, layer, 8, rows1, 2)
        return carry

    each(3, n1 - 3, post1, 8)

    for k in range(3, n1 - 3):
        for c in range(3):
            slot = 3 * (k - 3) + c
            spread_rows(tmp.at[slot], f1[c, k, mid, :])
            lifted = tmp[slot, pl.ds(0, bx + 16), :]
            for layer in (2 * k + 1, 2 * k + 2):
                if HALO - 1 <= layer <= HALO + bz:
                    w0[c, layer, near, :] = v0[c, layer, near, :] + lifted

    started = []
    for layer in range(HALO, HALO + bz):
        z = layer - HALO
        for row, count in chunks(16, 16 + bx, 16):

            def into(c, value):
                done[c, z, pl.ds(row - 16, count), :] = value

            post(s0, y0, g0, r0, w0, into, layer, row, count, 1)
        started.append(pltpu.make_async_copy(done.at[:, z], out_ref.at[:, z], sem.at[z]))
        started[-1].start()
    for copy in started:
        copy.wait()


def swapped(x, axis, start):
    pairs = [(i, i + 1) for i in range(start, lax.axis_size(axis) - 1, 2)]
    return lax.ppermute(x, axis, pairs + [(j, i) for i, j in pairs])


def vmem(*shape):
    return pltpu.VMEM(shape, F32)


def local(heights, tiles, material, clamped, stiffness_table, eigenstrain):
    bz, bx, _ = material.shape

    held = pl.BlockSpec(memory_space=pltpu.VMEM)
    outside = pl.BlockSpec(memory_space=pltpu.HBM)
    own, brick, edge = pl.pallas_call(
        functools.partial(pack_kernel, heights, bz, bx),
        out_shape=[pltpu.VMEM((rows, LANES), F32) for rows in ((bz + 2) * bx + SPARE, bz * bx, bx)],
        in_specs=[outside] * 4,
        out_specs=[held] * 3,
        scratch_shapes=[
            pltpu.VMEM((bz, bx, LANES), jnp.int32), pltpu.VMEM((2, bx, LANES), jnp.int32),
            pltpu.SMEM((3,), F32), pltpu.SMEM((3, 3), F32), pltpu.SemaphoreType.DMA((4,)),
        ],
    )(material, clamped, stiffness_table, eigenstrain)
    beside = swapped(brick, "height", 1)
    beyond = lax.ppermute(edge, "height", [(i, (i + 2) % heights) for i in range(heights)])
    paired = swapped(own, "height", 0)
    bricks = jnp.concatenate([own, paired, beside, beyond], 0)
    strip = pltpu.VMEM((-(-(strips(bz)[2] + 2 * HALO) // 8) * 8, LANES), F32)
    near, far = pl.pallas_call(
        functools.partial(strip_kernel, heights, bz, bx),
        out_shape=[strip, strip],
        in_specs=[held],
        out_specs=[held, held],
        compiler_params=pltpu.CompilerParams(vmem_limit_bytes=4 * 2**20),
    )(bricks)
    far = swapped(far, "tile", 1)
    near = swapped(near, "tile", 0)

    bx1, bx2 = bx // 2, bx // 4
    nz, n1 = bz + 2 * HALO, bz // 2 + 8
    r0, r1 = bx + 32, bx1 + 24
    rows1 = bx1 + 8
    field0, field1 = (nz, r0, LANES), (n1, r1, LANES)
    fields = [field0, field0, (3, *field0), (3, *field0), (3, *field0), (3, *field0), (3, *field0), (2, *field0), (3, *field0)]
    fields = [pltpu.VMEM(shape, F32) for shape in [*fields, (n1 - 2, 3, r0, LANES)]]
    work = 24 * 6 * 3 * 1024
    inner = pl.pallas_call(
        functools.partial(inner_kernel, heights, tiles, bz, bx),
        out_shape=fields,
        in_specs=[held] * 2,
        out_specs=[held] * len(fields),
        cost_estimate=pl.CostEstimate(flops=work * 60, bytes_accessed=work * 40, transcendentals=0),
        compiler_params=pltpu.CompilerParams(vmem_limit_bytes=4 * 2**20),
    )(bricks, near)
    kept = [field1, (2, *field1), (3, *field1), (3, *field1), (3, *field1)]
    kept = [pltpu.VMEM(shape, F32) for shape in kept]
    send, s1, y1, v1, g1, r1_, s, _, _, _, r, _, g, y, v, _ = pl.pallas_call(
        functools.partial(down_kernel, heights, tiles, bz, bx),
        out_shape=[
            pltpu.VMEM((heights * tiles * (bz // 4 * bx2 + bx2 // 8), LANES), F32), *kept, *fields
        ],
        in_specs=[held] * (2 + len(fields)),
        out_specs=[held] * (1 + len(kept) + len(fields)),
        input_output_aliases={2 + k: 1 + len(kept) + k for k in range(len(fields))},
        scratch_shapes=[vmem(n1 - 2, 3, r0, LANES), vmem(*field1), vmem(3, *field1), vmem(3, *field1)],
        compiler_params=pltpu.CompilerParams(vmem_limit_bytes=8 * 2**20),
    )(bricks, far, *inner)

    blocks = send.reshape(heights * tiles, -1, 1, LANES)
    received = lax.all_to_all(blocks, ("tile", "height"), 0, 0).reshape(send.shape)

    rows2 = bx2 + 2 * REACH
    rows3 = -(-(rows2 // 2) // 8) * 8
    up2 = (heights * bz // 4 + 2, rows2 + 16, LANES)
    up3 = (heights * bz // 8 + 2, rows3 + 16, LANES)
    return pl.pallas_call(
        functools.partial(up_kernel, heights, tiles, bz, bx),
        out_shape=jax.ShapeDtypeStruct((3, bz, bx, LANES), F32),
        in_specs=[held] * 11,
        out_specs=outside,
        scratch_shapes=[
            vmem(3, *field0), vmem(3, *field1), vmem(3, *field1),
            vmem(*up2), vmem(*up2), vmem(*up2), vmem(6, *up2), vmem(*up2), vmem(*up2), vmem(*up2), vmem(*up2), vmem(*up2),
            vmem(*up3), vmem(*up3), vmem(*up3), vmem(6, *up3), vmem(*up3), vmem(*up3), vmem(*up3), vmem(*up3),
            vmem(heights * bz // 8, rows2 + 24, LANES), vmem(max(heights * bz // 4, 3 * (n1 - 6)), r0, LANES),
            vmem(3, bz, bx, LANES), pltpu.SemaphoreType.DMA((bz,)),
        ],
        compiler_params=pltpu.CompilerParams(vmem_limit_bytes=16 * 2**20),
    )(received, s, y, v, g, r, s1, y1, v1, g1, r1_)


def solution(mesh):
    sides = mesh.shape["height"], mesh.shape["tile"]
    in_specs = (P("height", "tile", None), P("height", "tile", None), P(), P())
    out_specs = P(None, "height", "tile", None)
    return jax.shard_map(
        functools.partial(local, *sides), mesh=mesh, in_specs=in_specs, out_specs=out_specs, check_vma=False
    )
```

```python
import functools

import jax
import jax.numpy as jnp
from jax import lax
from jax.experimental import pallas as pl
from jax.experimental.pallas import tpu as pltpu
from jax.sharding import PartitionSpec as P

PENALTY = 50.0
OMEGA = 0.6
COARSE_SWEEPS = 6
LANES = 128
HALO = 9
REACH = 16
SPARE = 4
F32 = jnp.float32


def each(start, stop, body, step):
    groups = (stop - start) // step

    def group(i, carry):
        for k in range(step):
            body(start + i * step + k, 0)
        return carry

    if groups > 1:
        lax.fori_loop(0, groups, group, 0)
    elif groups == 1:
        group(0, 0)
    for layer in range(start + groups * step, stop):
        body(layer, 0)


def chunks(start, stop, size):
    return [(row, min(size, stop - row)) for row in range(start, stop, size)]


def lane_of(rows):
    return lax.broadcasted_iota(jnp.int32, (rows, LANES), 1)


def roll(x, shift):
    return pltpu.roll(x, shift % LANES, 1)


def rows_at(ref, layer, row, count):
    return ref[layer, pl.ds(row, count), :]


def cross_faces(s_ref, layer, row, count):
    here = rows_at(s_ref, layer, row, count)
    return here, [
        here + rows_at(s_ref, layer - 1, row, count),
        here + rows_at(s_ref, layer + 1, row, count),
        here + rows_at(s_ref, layer, row - 1, count),
        here + rows_at(s_ref, layer, row + 1, count),
    ]


def lane_faces(here, step):
    lane = lane_of(here.shape[0])
    first, last = lane < step, lane >= LANES - step
    low = here + jnp.where(first, 0.0, roll(here, step))
    high = here + jnp.where(last, 0.0, roll(here, -step))
    return low, high, jnp.where(first, 0.0, low), jnp.where(last, 0.0, high)


def neighbours(v_ref, faces, layer, row, count, step):
    here = rows_at(v_ref, layer, row, count)
    along = [
        faces[0] * rows_at(v_ref, layer - 1, row, count)
        + faces[1] * rows_at(v_ref, layer + 1, row, count),
        faces[2] * rows_at(v_ref, layer, row - 1, count)
        + faces[3] * rows_at(v_ref, layer, row + 1, count),
        faces[4] * roll(here, step) + faces[5] * roll(here, -step),
    ]
    return here, along


def total(along, component):
    return (along[0] + along[1] + along[2]) + along[component]


def safe_rate(here, doubled):
    return jnp.where(here > 0.0, OMEGA / doubled, 0.0)


def pair_lanes(x, step):
    upper = (lane_of(x.shape[0]) & step) != 0
    return x + jnp.where(upper, roll(x, step), roll(x, -step))


def pair_rows(ref, row, count):
    return ref[pl.ds(row, count, stride=2), :] + ref[pl.ds(row + 1, count, stride=2), :]


def spread_rows(ref, x):
    count = x.shape[0]
    ref[pl.ds(0, count, stride=2), :] = x
    ref[pl.ds(1, count, stride=2), :] = x


def level_setup(s_ref, p_ref, r_ref, d_ref, g_ref, y_ref, b_of, layer, row, count, step):
    here, cross = cross_faces(s_ref, layer, row, count)
    low, high, low_in, high_in = lane_faces(here, step)
    y_ref[0, layer, pl.ds(row, count), :] = low_in
    y_ref[1, layer, pl.ds(row, count), :] = high_in
    sums = [cross[0] + cross[1], cross[2] + cross[3], low + high]
    base = rows_at(p_ref, layer, row, count) + (sums[0] + sums[1] + sums[2])
    for c in range(3):
        doubled = base + sums[c]
        rate = safe_rate(here, doubled)
        d_ref[c, layer, pl.ds(row, count), :] = doubled
        r_ref[c, layer, pl.ds(row, count), :] = rate
        g_ref[c, layer, pl.ds(row, count), :] = rate * b_of(c)


def all_faces(s_ref, y_ref, layer, row, count):
    _, cross = cross_faces(s_ref, layer, row, count)
    return cross + [
        y_ref[0, layer, pl.ds(row, count), :],
        y_ref[1, layer, pl.ds(row, count), :],
    ]


def first_sweep(s_ref, y_ref, r_ref, g_ref, v_ref, layer, row, count, step):
    faces = all_faces(s_ref, y_ref, layer, row, count)
    for c in range(3):
        here, along = neighbours(g_ref.at[c], faces, layer, row, count, step)
        rate = r_ref[c, layer, pl.ds(row, count), :]
        v_ref[c, layer, pl.ds(row, count), :] = (2.0 - OMEGA) * here + rate * total(along, c)


def remainder(s_ref, y_ref, b_ref, d_ref, v_ref, layer, row, count, step):
    faces = all_faces(s_ref, y_ref, layer, row, count)
    result = []
    for c in range(3):
        here, along = neighbours(v_ref.at[c], faces, layer, row, count, step)
        doubled = d_ref[c, layer, pl.ds(row, count), :]
        source = b_ref[c, layer, pl.ds(row, count), :]
        result.append(source + (total(along, c) - doubled * here))
    return result


def strips(bz):
    counts = [min(layer, HALO, bz + 2 * HALO - 1 - layer) for layer in range(bz + 2 * HALO)]
    starts = [sum(counts[:layer]) for layer in range(len(counts))]
    return counts, starts, sum(counts)


def pack_kernel(
    heights, bz, bx, material_ref, clamped_ref, table_ref, strain_ref, own_ref, brick_ref, edge_ref, label, joined, table, strain, sem
):
    copies = [
        pltpu.make_async_copy(material_ref, label, sem.at[0]),
        pltpu.make_async_copy(clamped_ref.at[pl.ds(0, 2)], joined, sem.at[1]),
        pltpu.make_async_copy(table_ref, table, sem.at[2]),
        pltpu.make_async_copy(strain_ref, strain, sem.at[3]),
    ]
    for copy in copies:
        copy.start()
    for copy in copies:
        copy.wait()
    for slot in range(bz + 2):
        src = label.at[slot] if slot < bz else joined.at[slot - bz]
        value = src[...].astype(F32)
        own_ref[pl.ds(slot * bx, bx), :] = value
        if slot < bz:
            brick_ref[pl.ds(slot * bx, bx), :] = value
    lower = lax.axis_index("height") < heights // 2
    edge_ref[...] = jnp.where(lower, label[bz - 1], label[0]).astype(F32)
    lane = lane_of(SPARE)
    row = jnp.zeros((SPARE, LANES), F32)
    for k in range(3):
        row = jnp.where(lane == k, table[k], row)
        for c in range(3):
            row = jnp.where(lane == 3 + 3 * c + k, table[k] * strain[k, c], row)
    own_ref[pl.ds((bz + 2) * bx, SPARE), :] = row


def spring_layers(heights, bz):
    layers = {HALO - bz * h + k for h in range(heights) for k in range(2)}
    return {layer for layer in layers if 0 <= layer < bz + 2 * HALO}


def gathered_rows(bz, bx):
    whole, brick = (bz + 2) * bx + SPARE, bz * bx
    return [0, whole, 2 * whole, 2 * whole + brick]


def place(bz, bx, layer):
    h = lax.axis_index("height")
    own, paired, beside, beyond = gathered_rows(bz, bx)
    even = (h & 1) == 0
    if layer in (0, bz + 2 * HALO - 1):
        row = beyond
    elif layer < HALO:
        row = jnp.where(even, beside, paired) + (bz - HALO + layer) * bx
    elif layer < HALO + bz:
        row = own + (layer - HALO) * bx
    else:
        row = jnp.where(even, paired, beside) + (layer - HALO - bz) * bx
    return bz * h - HALO + layer, row


def spring_row(bz, bx):
    return jnp.where(lax.axis_index("height") == 0, 0, gathered_rows(bz, bx)[1]) + bz * bx


def strip_kernel(heights, bz, bx, x_ref, near_ref, far_ref):
    odd = (lax.axis_index("tile") & 1) == 1
    counts, starts, end = strips(bz)
    wanted = [(place(bz, bx, layer)[1], count, start) for layer, (count, start) in enumerate(zip(counts, starts))]
    wanted += [(spring_row(bz, bx) + bx * k, HALO - 1, end + (HALO - 1) * k) for k in range(2)]
    for row, count, start in wanted:
        if count:
            first = x_ref[pl.ds(row, count), :]
            last = x_ref[pl.ds(row + bx - count, count), :]
            near_ref[pl.ds(start, count), :] = jnp.where(odd, first, last)
            far_ref[pl.ds(start, count), :] = jnp.where(odd, last, first)


def tables_of(x_ref, row):
    spare = x_ref[pl.ds(row, 1), :]
    table = [jnp.broadcast_to(spare[:, k : k + 1], (1, LANES)) for k in range(12)]
    return table[:3], [table[3 + 3 * c : 6 + 3 * c] for c in range(3)]


def store_layer(s, st, label, layer, to, weight, tables):
    is0, is1 = label == 0.0, label == 1.0
    dst = pl.ds(to, label.shape[0])
    for ref, values in zip((s, *(st.at[c] for c in range(3))), (tables[0], *tables[1])):
        a, b, c = (value * weight for value in values)
        ref[layer, dst, :] = jnp.where(is0, a, jnp.where(is1, b, c))


def store_strip(s, st, p, strip_ref, heights, bz, layer, far_side, valid, bx, tables):
    counts, starts, end = strips(bz)
    z, _ = place(bz, bx, layer)
    weight = jnp.where((z >= 0) & (z < heights * bz), valid, 0.0)
    count = counts[layer]
    if count:
        to = jnp.where(far_side, 16 + bx, 16 - count)
        store_layer(s, st, strip_ref[pl.ds(starts[layer], count), :], layer, to, weight, tables)
    if layer not in spring_layers(heights, bz):
        return
    reach = HALO - 1
    joined = strip_ref[pl.ds(end + reach * jnp.clip(z, 0, 1), reach), :]
    to = jnp.where(far_side, 16 + bx, 16 - reach)
    p[layer, pl.ds(to, reach), :] = joined * jnp.where((z >= 0) & (z < 2), 2.0 * PENALTY * valid, 0.0)


def fine_setup(s, p, st, b, r, d, g, y, layer, row, count):
    lane = lane_of(count)
    here = st[2, layer, pl.ds(row, count), :]
    source = [
        (rows_at(st.at[0], layer - 1, row, count) - rows_at(st.at[0], layer + 1, row, count)),
        (rows_at(st.at[1], layer, row - 1, count) - rows_at(st.at[1], layer, row + 1, count)),
        (jnp.where(lane < 1, 0.0, roll(here, 1)) - jnp.where(lane >= LANES - 1, 0.0, roll(here, -1))),
    ]
    for c in range(3):
        b[c, layer, pl.ds(row, count), :] = source[c]
    level_setup(s, p, r, d, g, y, lambda c: source[c], layer, row, count, 1)


def fine_down(bz, s, p, st, b, r, d, g, y, v, rest, rows, step):
    nz = bz + 2 * HALO

    def setup0(layer, carry):
        for row in rows[0]:
            fine_setup(s, p, st, b, r, d, g, y, layer, row, 16)
        return carry

    def sweep0(layer, carry):
        for row in rows[1]:
            first_sweep(s, y, r, g, v, layer, row, 16, 1)
        return carry

    def restrict0(j, carry):
        layer = 3 + 2 * j
        for row in rows[2]:
            one = remainder(s, y, b, d, v, layer, row, 16, 1)
            two = remainder(s, y, b, d, v, layer + 1, row, 16, 1)
            for c in range(3):
                rest[j, c, pl.ds(row, 16), :] = one[c] + two[c]
        return carry

    each(1, nz - 1, setup0, step or 12)
    each(2, nz - 2, sweep0, step or 11)
    each(0, bz // 2 + 6, restrict0, step or 5)


def inner_kernel(heights, tiles, bz, bx, x_ref, near_ref, s, p, st, b, r, d, g, y, v, rest):
    t = lax.axis_index("tile")
    odd = (t & 1) == 1
    tables = tables_of(x_ref, (bz + 2) * bx)
    valid = jnp.where(odd | (t < tiles - 1), 1.0, 0.0)

    def read_layer(layer, carry):
        z, row = place(bz, bx, layer)
        inside = jnp.where((z >= 0) & (z < heights * bz), 1.0, 0.0)
        store_layer(s, st, x_ref[pl.ds(row, bx), :], layer, 16, inside, tables)
        if layer in spring_layers(heights, bz):
            bottom = jnp.where((z >= 0) & (z < 2), 2.0 * PENALTY, 0.0)
            p[layer, pl.ds(16, bx), :] = x_ref[pl.ds(spring_row(bz, bx) + jnp.clip(z, 0, 1) * bx, bx), :] * bottom
        else:
            p[layer, :, :] = jnp.zeros(p.shape[1:], F32)
        store_strip(s, st, p, near_ref, heights, bz, layer, jnp.logical_not(odd), valid, bx, tables)
        return carry

    each(0, bz + 2 * HALO, read_layer, bz + 2 * HALO + 1)
    rows = [[jnp.where(odd, 8 - k, 24 + k) + at for at in range(0, bx, 16)] for k in range(3)]
    fine_down(bz, s, p, st, b, r, d, g, y, v, rest, rows, 0)


def down_kernel(
    heights, tiles, bz, bx,
    x_ref, far_ref, *refs,
):
    send_ref, s1, y1, v1, g1, r1, s, p, st, b, r, d, g, y, v, rest, tmp, p1, b1, d1 = refs[10:]
    h, t = lax.axis_index("height"), lax.axis_index("tile")
    odd = (t & 1) == 1
    n1 = bz // 2 + 8
    bx1, bx2 = bx // 2, bx // 4
    low = 8
    tables = tables_of(x_ref, (bz + 2) * bx)
    valid = jnp.where(jnp.where(odd, t < tiles - 1, t > 0), 1.0, 0.0)

    def read_layer(layer, carry):
        store_strip(s, st, p, far_ref, heights, bz, layer, odd, valid, bx, tables)
        return carry

    each(0, bz + 2 * HALO, read_layer, bz + 2 * HALO + 1)
    rows = [[jnp.where(odd, bx + 8 - k, 8 + k)] for k in range(3)]
    fine_down(bz, s, p, st, b, r, d, g, y, v, rest, rows, 12)

    rows1 = bx1 + 8

    def restrict0(j, carry):
        for c in range(3):
            b1[c, j + 1, pl.ds(8, rows1), :] = pair_lanes(pair_rows(rest.at[j, c], low, rows1), 1)
        return carry

    each(0, n1 - 2, restrict0, 8)

    def coarse0(k, carry):
        pair = (1 + 2 * k, 2 + 2 * k)
        both = [pair_rows(s.at[layer], low, rows1) for layer in pair]
        s1[k, pl.ds(8, rows1), :] = 0.5 * pair_lanes(both[0] + both[1], 1)
        if spring_layers(heights, bz).isdisjoint(pair):
            p1[k, pl.ds(8, rows1), :] = jnp.zeros((rows1, LANES), F32)
        else:
            both = [pair_rows(p.at[layer], low, rows1) for layer in pair]
            p1[k, pl.ds(8, rows1), :] = pair_lanes(both[0] + both[1], 1)
        return carry

    each(0, n1, coarse0, n1 + 1)

    def setup1(layer, carry):
        level_setup(
            s1, p1, r1, d1, g1, y1,
            lambda c: b1[c, layer, pl.ds(8, rows1), :], layer, 8, rows1, 2,
        )
        return carry

    each(1, n1 - 1, setup1, 8)

    def sweep1(layer, carry):
        first_sweep(s1, y1, r1, g1, v1, layer, 8, rows1, 2)
        return carry

    each(2, n1 - 2, sweep1, 8)

    lane = lane_of(bx2) & 3
    packed = []
    for m in range(bz // 4):
        layer = 4 + 2 * m
        one = remainder(s1, y1, b1, d1, v1, layer, 8, rows1, 2)
        two = remainder(s1, y1, b1, d1, v1, layer + 1, 8, rows1, 2)
        fields = []
        for c in range(3):
            tmp[m, c, pl.ds(0, rows1), :] = one[c] + two[c]
            fields.append(pair_lanes(pair_rows(tmp.at[m, c], 4, bx2), 2))
        both = [pair_rows(s1.at[layer + i], 12, bx2) for i in range(2)]
        stiff = 0.5 * pair_lanes(both[0] + both[1], 2)
        packed.append(
            jnp.where(lane == 0, fields[0], jnp.where(lane == 1, fields[1], jnp.where(lane == 2, fields[2], stiff)))
        )
    bottom = jnp.maximum(bz // 2 * (1 - h), 0)
    both = [pair_rows(p1.at[bottom + i], 12, bx2) for i in range(2)]
    tmp[2, 0, pl.ds(0, bx2), :] = pair_lanes(both[0] + both[1], 2)
    quarter = bx2 // 8
    first = jnp.minimum(h, 1) * (bx2 // 2)
    part = [tmp[2, 0, pl.ds(first + j, quarter, stride=4), :] for j in range(4)]
    lane = lane_of(quarter) & 3
    packed.append(jnp.where(lane == 0, part[0], jnp.where(lane == 1, part[1], jnp.where(lane == 2, part[2], part[3]))))
    size = sum(value.shape[0] for value in packed)

    def fill(i, carry):
        at = i * size
        for value in packed:
            send_ref[pl.ds(at, value.shape[0]), :] = value
            at = at + value.shape[0]
        return carry

    each(0, heights * tiles, fill, 8)


def up_kernel(
    heights, tiles, bz, bx,
    recv_ref, s0, y0, v0, g0, r0, s1, y1, v1, g1, r1, out_ref,
    w0, w1, f1, s2, p2, b2, q2, r2, d2, g2, v2, f2, s3, p3, b3, q3, r3, g3, va, vb, rest2, tmp, done, sem,
):
    h, t = lax.axis_index("height"), lax.axis_index("tile")
    bx1, bx2, bz2 = bx // 2, bx // 4, bz // 4
    n1, n2, n3 = bz // 2 + 8, heights * bz // 4, heights * bz // 8
    rows1 = bx1 + 8
    near = pl.ds(8, bx + 16)
    mid = pl.ds(8, rows1)

    for ref in (s2, p2, g2, v2, f2, s3, p3, g3, va, vb):
        ref[...] = jnp.zeros(ref.shape, F32)
    rest2[...] = jnp.zeros(rest2.shape, F32)

    side = REACH // bx2
    size = bz2 * bx2 + bx2 // 8
    lane = lane_of(bx2) & 3
    for dt in range(-side, side + 1):
        other = t + dt
        valid = (other >= 0) & (other < tiles)
        other = jnp.clip(other, 0, tiles - 1)
        scale = jnp.where(valid, 1.0, 0.0)
        dst = pl.ds(8 + (dt + side) * bx2, bx2)
        for hh in range(heights):
            for m in range(bz2):
                x = recv_ref[pl.ds((other * heights + hh) * size + m * bx2, bx2), :] * scale
                layer = 1 + hh * bz2 + m
                b2[layer, dst, :] = jnp.where(lane == 3, 0.0, x)
                s2[layer, dst, :] = jnp.where(
                    lane == 3, x, jnp.where(lane == 2, roll(x, -1), jnp.where(lane == 1, roll(x, -2), roll(x, -3)))
                )
        quarter = bx2 // 8
        small = lane_of(quarter) & 3
        for hh in range(2):
            x = recv_ref[pl.ds((other * heights + hh) * size + bz2 * bx2, quarter), :] * scale
            moved = {shift: roll(x, shift) if shift else x for shift in range(-3, 4)}
            for j in range(4):
                row = 8 + (dt + side) * bx2 + hh * (bx2 // 2) + j
                p2[1, pl.ds(row, quarter, stride=4), :] = jnp.where(
                    small == 0, moved[-j], jnp.where(small == 1, moved[1 - j], jnp.where(small == 2, moved[2 - j], moved[3 - j]))
                )

    def weights(count):
        kind = lane_of(count) & 3
        return [jnp.where(kind == c, 2.0, 1.0) for c in range(3)]

    def setup(s_ref, p_ref, b_ref, q_ref, r_ref, d_ref, g_ref, layer, row, count, step):
        here, cross = cross_faces(s_ref, layer, row, count)
        low, high, low_in, high_in = lane_faces(here, step)
        w = weights(count)
        dst = pl.ds(row, count)
        for k in range(4):
            q_ref[k, layer, dst, :] = w[k // 2] * cross[k]
        q_ref[4, layer, dst, :] = w[2] * low_in
        q_ref[5, layer, dst, :] = w[2] * high_in
        doubled = rows_at(p_ref, layer, row, count) + (
            w[0] * (cross[0] + cross[1]) + w[1] * (cross[2] + cross[3]) + w[2] * (low + high)
        )
        rate = safe_rate(here, doubled)
        r_ref[layer, dst, :] = rate
        if d_ref is not None:
            d_ref[layer, dst, :] = doubled
        g_ref[layer, dst, :] = rate * rows_at(b_ref, layer, row, count)

    def packed_sum(v_ref, q_ref, layer, row, count, step):
        faces = [q_ref[k, layer, pl.ds(row, count), :] for k in range(6)]
        here, along = neighbours(v_ref, faces, layer, row, count, step)
        return here, along[0] + along[1] + along[2]

    rows2 = bx2 + 2 * REACH

    def setup2(layer, carry):
        setup(s2, p2, b2, q2, r2, d2, g2, layer, 8, rows2, 4)
        return carry

    each(1, n2 + 1, setup2, 8)

    def sweep2(layer, carry):
        here, total_ = packed_sum(g2, q2, layer, 8, rows2, 4)
        v2[layer, pl.ds(8, rows2), :] = (2.0 - OMEGA) * here + rows_at(r2, layer, 8, rows2) * total_
        return carry

    each(1, n2 + 1, sweep2, 8)

    rows3 = -(-(rows2 // 2) // 8) * 8

    def restrict2(j, carry):
        rest = 0.0
        for i in range(2):
            layer = 1 + 2 * j + i
            here, total_ = packed_sum(v2, q2, layer, 8, rows2, 4)
            rest = rest + rows_at(b2, layer, 8, rows2) + (total_ - rows_at(d2, layer, 8, rows2) * here)
        rest2[j, pl.ds(8, rows2), :] = rest
        dst = pl.ds(8, rows3)
        b3[j + 1, dst, :] = pair_lanes(pair_rows(rest2.at[j], 8, rows3), 4)
        for field, scale, into in ((s2, 0.5, s3), (p2, 1.0, p3)):
            both = [pair_rows(field.at[1 + 2 * j + i], 8, rows3) for i in range(2)]
            into[j + 1, dst, :] = scale * pair_lanes(both[0] + both[1], 4)
        return carry

    each(0, n3, restrict2, 8)

    for layer in range(1, n3 + 1):
        setup(s3, p3, b3, q3, r3, None, g3, layer, 8, rows3, 8)
    source, target = g3, va
    for _ in range(COARSE_SWEEPS - 1):
        for layer in range(1, n3 + 1):
            here, total_ = packed_sum(source, q3, layer, 8, rows3, 8)
            target[layer, pl.ds(8, rows3), :] = (
                (1.0 - OMEGA) * here + rows_at(g3, layer, 8, rows3) + rows_at(r3, layer, 8, rows3) * total_
            )
        source, target = target, (vb if target is va else va)
    coarse = source

    wide2 = bx2 + 16

    def lift2(layer, carry):
        spread_rows(tmp.at[layer - 1], coarse[(layer + 1) // 2, pl.ds(12, wide2 // 2), :])
        v2[layer, pl.ds(16, wide2), :] += tmp[layer - 1, pl.ds(0, wide2), :]
        return carry

    each(1, n2 + 1, lift2, 8)

    def post2(layer, carry):
        here, total_ = packed_sum(v2, q2, layer, 16, wide2, 4)
        f2[layer, pl.ds(16, wide2), :] = (
            (1.0 - OMEGA) * here + rows_at(g2, layer, 16, wide2) + rows_at(r2, layer, 16, wide2) * total_
        )
        return carry

    each(1, n2 + 1, post2, 8)

    kind = lane_of(bx2 + 4) & 3

    def lift1(m, carry):
        x = f2[bz2 * h + m, pl.ds(22, bx2 + 4), :]
        moved = {shift: roll(x, shift) if shift else x for shift in range(-2, 4)}
        for c in range(3):
            part = jnp.where(
                kind == 0, moved[-c], jnp.where(kind == 1, moved[1 - c], jnp.where(kind == 2, moved[2 - c], moved[3 - c]))
            )
            spread_rows(tmp.at[3 * m + c], part)
            lifted = tmp[3 * m + c, pl.ds(0, rows1), :]
            for i in range(2):
                w1[c, 2 + 2 * m + i, mid, :] = v1[c, 2 + 2 * m + i, mid, :] + lifted
        return carry

    each(0, n1 // 2 - 2, lift1, 8)

    def post(s_ref, y_ref, g_ref, r_ref, v_ref, into, layer, row, count, step):
        faces = all_faces(s_ref, y_ref, layer, row, count)
        for c in range(3):
            here, along = neighbours(v_ref.at[c], faces, layer, row, count, step)
            dst = pl.ds(row, count)
            into(c, (1.0 - OMEGA) * here + g_ref[c, layer, dst, :] + r_ref[c, layer, dst, :] * total(along, c))

    def post1(layer, carry):
        def into(c, value):
            f1[c, layer, mid, :] = value

        post(s1, y1, g1, r1, w1, into, layer, 8, rows1, 2)
        return carry

    each(3, n1 - 3, post1, 8)

    for k in range(3, n1 - 3):
        for c in range(3):
            slot = 3 * (k - 3) + c
            spread_rows(tmp.at[slot], f1[c, k, mid, :])
            lifted = tmp[slot, pl.ds(0, bx + 16), :]
            for layer in (2 * k + 1, 2 * k + 2):
                if HALO - 1 <= layer <= HALO + bz:
                    w0[c, layer, near, :] = v0[c, layer, near, :] + lifted

    started = []
    for layer in range(HALO, HALO + bz):
        z = layer - HALO
        for row, count in chunks(16, 16 + bx, 16):

            def into(c, value):
                done[c, z, pl.ds(row - 16, count), :] = value

            post(s0, y0, g0, r0, w0, into, layer, row, count, 1)
        started.append(pltpu.make_async_copy(done.at[:, z], out_ref.at[:, z], sem.at[z]))
        started[-1].start()
    for copy in started:
        copy.wait()


def swapped(x, axis, start):
    pairs = [(i, i + 1) for i in range(start, lax.axis_size(axis) - 1, 2)]
    return lax.ppermute(x, axis, pairs + [(j, i) for i, j in pairs])


def vmem(*shape):
    return pltpu.VMEM(shape, F32)


def local(heights, tiles, material, clamped, stiffness_table, eigenstrain):
    bz, bx, _ = material.shape

    held = pl.BlockSpec(memory_space=pltpu.VMEM)
    outside = pl.BlockSpec(memory_space=pltpu.HBM)
    own, brick, edge = pl.pallas_call(
        functools.partial(pack_kernel, heights, bz, bx),
        out_shape=[pltpu.VMEM((rows, LANES), F32) for rows in ((bz + 2) * bx + SPARE, bz * bx, bx)],
        in_specs=[outside] * 4,
        out_specs=[held] * 3,
        scratch_shapes=[
            pltpu.VMEM((bz, bx, LANES), jnp.int32), pltpu.VMEM((2, bx, LANES), jnp.int32),
            pltpu.SMEM((3,), F32), pltpu.SMEM((3, 3), F32), pltpu.SemaphoreType.DMA((4,)),
        ],
    )(material, clamped, stiffness_table, eigenstrain)
    beside = swapped(brick, "height", 1)
    beyond = lax.ppermute(edge, "height", [(i, (i + 2) % heights) for i in range(heights)])
    paired = swapped(own, "height", 0)
    bricks = jnp.concatenate([own, paired, beside, beyond], 0)
    strip = pltpu.VMEM((-(-(strips(bz)[2] + 2 * (HALO - 1)) // 8) * 8, LANES), F32)
    near, far = pl.pallas_call(
        functools.partial(strip_kernel, heights, bz, bx),
        out_shape=[strip, strip],
        in_specs=[held],
        out_specs=[held, held],
        compiler_params=pltpu.CompilerParams(vmem_limit_bytes=4 * 2**20),
    )(bricks)
    far = swapped(far, "tile", 1)
    near = swapped(near, "tile", 0)

    bx1, bx2 = bx // 2, bx // 4
    nz, n1 = bz + 2 * HALO, bz // 2 + 8
    r0, r1 = bx + 32, bx1 + 24
    rows1 = bx1 + 8
    field0, field1 = (nz, r0, LANES), (n1, r1, LANES)
    fields = [field0, field0, (3, *field0), (3, *field0), (3, *field0), (3, *field0), (3, *field0), (2, *field0), (3, *field0)]
    fields = [pltpu.VMEM(shape, F32) for shape in [*fields, (n1 - 2, 3, r0, LANES)]]
    work = 24 * 6 * 3 * 1024
    inner = pl.pallas_call(
        functools.partial(inner_kernel, heights, tiles, bz, bx),
        out_shape=fields,
        in_specs=[held] * 2,
        out_specs=[held] * len(fields),
        cost_estimate=pl.CostEstimate(flops=work * 60, bytes_accessed=work * 40, transcendentals=0),
        compiler_params=pltpu.CompilerParams(vmem_limit_bytes=4 * 2**20),
    )(bricks, near)
    kept = [field1, (2, *field1), (3, *field1), (3, *field1), (3, *field1)]
    kept = [pltpu.VMEM(shape, F32) for shape in kept]
    send, s1, y1, v1, g1, r1_, s, _, _, _, r, _, g, y, v, _ = pl.pallas_call(
        functools.partial(down_kernel, heights, tiles, bz, bx),
        out_shape=[
            pltpu.VMEM((heights * tiles * (bz // 4 * bx2 + bx2 // 8), LANES), F32), *kept, *fields
        ],
        in_specs=[held] * (2 + len(fields)),
        out_specs=[held] * (1 + len(kept) + len(fields)),
        input_output_aliases={2 + k: 1 + len(kept) + k for k in range(len(fields))},
        scratch_shapes=[vmem(n1 - 2, 3, r0, LANES), vmem(*field1), vmem(3, *field1), vmem(3, *field1)],
        compiler_params=pltpu.CompilerParams(vmem_limit_bytes=8 * 2**20),
    )(bricks, far, *inner)

    blocks = send.reshape(heights * tiles, -1, 1, LANES)
    received = lax.all_to_all(blocks, ("tile", "height"), 0, 0).reshape(send.shape)

    rows2 = bx2 + 2 * REACH
    rows3 = -(-(rows2 // 2) // 8) * 8
    up2 = (heights * bz // 4 + 2, rows2 + 16, LANES)
    up3 = (heights * bz // 8 + 2, rows3 + 16, LANES)
    return pl.pallas_call(
        functools.partial(up_kernel, heights, tiles, bz, bx),
        out_shape=jax.ShapeDtypeStruct((3, bz, bx, LANES), F32),
        in_specs=[held] * 11,
        out_specs=outside,
        scratch_shapes=[
            vmem(3, *field0), vmem(3, *field1), vmem(3, *field1),
            vmem(*up2), vmem(*up2), vmem(*up2), vmem(6, *up2), vmem(*up2), vmem(*up2), vmem(*up2), vmem(*up2), vmem(*up2),
            vmem(*up3), vmem(*up3), vmem(*up3), vmem(6, *up3), vmem(*up3), vmem(*up3), vmem(*up3), vmem(*up3),
            vmem(heights * bz // 8, rows2 + 24, LANES), vmem(max(heights * bz // 4, 3 * (n1 - 6)), r0, LANES),
            vmem(3, bz, bx, LANES), pltpu.SemaphoreType.DMA((bz,)),
        ],
        compiler_params=pltpu.CompilerParams(vmem_limit_bytes=16 * 2**20),
    )(received, s, y, v, g, r, s1, y1, v1, g1, r1_)


def solution(mesh):
    sides = mesh.shape["height"], mesh.shape["tile"]
    in_specs = (P("height", "tile", None), P("height", "tile", None), P(), P())
    out_specs = P(None, "height", "tile", None)
    return jax.shard_map(
        functools.partial(local, *sides), mesh=mesh, in_specs=in_specs, out_specs=out_specs, check_vma=False
    )
```
